32 devices in a mesh: dp: 8 (over z, y), shard: 4 (over x, core).
Axes of the slice: x: 2, y: 2, z: 4, core: 2. Of those that a mesh axis runs over, the one named last changes fastest.
Arguments:
- tokens: bfloat16 [16384, 768], P(('dp', 'shard')), may hold values from -6 to 6
- cotangent: bfloat16 [16384, 768], P(('dp', 'shard')), may hold values from -6 to 6
- lengths: int32 [8, 2], P('dp'), may hold values from 1 to 2047, as said below
- counts: int32 [8, 4], P('dp'), may hold values from 384 to 512, as said below
- attn_w: float32 [768, 3072], P('shard')
- attn_m: float32 [768, 3072], P('shard'), may hold values from -0.00061035156 to 0.00061035156
- attn_v: float32 [768, 3072], P('shard'), may hold values from 1.4110135e-10 to 5.644054e-10
- mlp_w: float32 [2, 768, 3072], P(None, 'shard')
- mlp_m: float32 [2, 768, 3072], P(None, 'shard'), may hold values from -0.00061035156 to 0.00061035156
- mlp_v: float32 [2, 768, 3072], P(None, 'shard'), may hold values from 1.4110135e-10 to 5.644054e-10
- vec_w: float32 [12, 768], P(None, 'shard')
- vec_m: float32 [12, 768], P(None, 'shard'), may hold values from -0.0024414062 to 0.0024414062
- vec_v: float32 [12, 768], P(None, 'shard'), may hold values from 2.2576216e-09 to 9.030487e-09
Outputs:
- block_out: bfloat16 [16384, 768], P(('dp', 'shard'))
- grad_in: bfloat16 [16384, 768], P(('dp', 'shard'))
- attn_grad: float32 [768, 3072], P('shard')
- mlp_grad: float32 [2, 768, 3072], P(None, 'shard')
- vec_grad: float32 [12, 768], P(None, 'shard')
- attn_w_new: float32 [768, 3072], P('shard')
- attn_m_new: float32 [768, 3072], P('shard')
- attn_v_new: float32 [768, 3072], P('shard')
- mlp_w_new: float32 [2, 768, 3072], P(None, 'shard')
- mlp_m_new: float32 [2, 768, 3072], P(None, 'shard')
- mlp_v_new: float32 [2, 768, 3072], P(None, 'shard')
- vec_w_new: float32 [12, 768], P(None, 'shard')
- vec_m_new: float32 [12, 768], P(None, 'shard')
- vec_v_new: float32 [12, 768], P(None, 'shard')
- clip_norm: float32 [1], replicated
The draws below stay inside these ranges and needn't reach their ends.
Inputs may be any that keep to these rules, and one draw needn't show every extreme that they name: `counts`: in every group one device holds exactly 512 tokens. A group's lengths sum to the sum of its counts; one of its sequences holds tokens of the group's first device and of its last. In some group every device is full and its first sequence is a single token.
All inputs are finite; a program needn't handle non-finite values.
Results may differ from the reference program's by a relative error of at most 0.015.
The reference program's roundings to bfloat16 on the way count: a program that leaves them out, or rounds other values in their place, can miss the bound.
Values may be sent and summed in bfloat16 or wider, within the bound.
No kernel may reach another device: no remote copies, remote signals or barrier semaphores. Data moves between devices by JAX's collectives and lax.ppermute only.
A program may use at most 320 MiB of HBM per device.

```python
import jax
import jax.numpy as jnp
from jax import lax

D = 768
HEADS = 12
HEAD = 64
FF = 3072
NVEC = 12
STEP = 10
TOK_CAP = 512
MIN_COUNT = 384
GROUPS = 8
SHARDS = 4
ROWS = 16384
PARAMS = 7087104
N_DP = 8
N_SHARD = 4


def deal_tokens(key):
    key_count, key_full, key_side, key_cut, key_pick = jax.random.split(jax.random.fold_in(key, 7), 5)
    counts = jax.random.randint(key_count, (GROUPS, SHARDS), MIN_COUNT, TOK_CAP + 1)
    fullest = jax.random.randint(key_full, (GROUPS, 1), 0, SHARDS)
    counts = jnp.where(jnp.arange(SHARDS)[None, :] == fullest, TOK_CAP, counts)
    picked = jax.random.randint(key_pick, (), 0, GROUPS)
    chosen = jnp.arange(GROUPS) == picked
    counts = jnp.where(chosen[:, None], TOK_CAP, counts)
    total = jnp.sum(counts, axis=1)
    first_count = counts[:, 0]
    last_count = counts[:, SHARDS - 1]
    side = jax.random.randint(key_side, (GROUPS,), 0, 2)
    side = jnp.where(chosen, 0, side)
    offset = jax.random.randint(key_cut, (GROUPS,), 0, 1 << 20)
    offset = jnp.where(chosen, 0, offset)
    left_cut = 1 + offset % (first_count - 1)
    right_cut = total - last_count + 1 + offset % (last_count - 1)
    cut_point = jnp.where(side == 0, left_cut, right_cut)
    lengths = jnp.stack([cut_point, total - cut_point], axis=1)
    return (counts.astype(jnp.int32), lengths.astype(jnp.int32))


def draw_counts(key, part):
    counts, lengths = deal_tokens(key)
    return counts


def draw_lengths(key, part):
    counts, lengths = deal_tokens(key)
    return lengths


def draw_attn_w(key, part):
    key = jax.random.fold_in(key, 21)
    column = jnp.arange(4 * D)[None, :]
    boost = jnp.where(column >= 3 * D, 8.0, 1.0)
    return jax.random.normal(key, (D, 4 * D), jnp.float32) * D ** (-0.5) * boost


def draw_mlp_w(key, part):
    key = jax.random.fold_in(key, 22)
    which = jnp.arange(2)[:, None, None]
    factor = jnp.where(which == 0, D ** (-0.5), FF ** (-0.5))
    return jax.random.normal(key, (2, D, FF), jnp.float32) * factor


def draw_vec_w(key, part):
    key = jax.random.fold_in(key, 23)
    key_base, key_gain = jax.random.split(key)
    base = jax.random.normal(key_base, (NVEC, D), jnp.float32) * 0.2
    rise = 3.0
    start = 0.6
    ramp = start * rise ** (jnp.arange(D, dtype=jnp.float32) / (D - 1))
    gains = ramp[None, :] * jax.random.uniform(key_gain, (NVEC, D), jnp.float32, 0.7, 1.3)
    row = jnp.arange(NVEC)[:, None]
    return jnp.where((row == 0) | (row == 5), gains, base)


def level_of(stream_key, extent, cuts, smallest, largest):
    factor_of = 1.0
    for dim, blocks in cuts:
        draws = jax.random.uniform(jax.random.fold_in(jax.random.fold_in(stream_key, 6), dim), (blocks,), jnp.float32, smallest / len(cuts), largest / len(cuts))
        factor_of = factor_of * jnp.repeat(jnp.exp(draws), extent[dim] // blocks).reshape((-1,) + (1,) * (len(extent) - 1 - dim))
    return factor_of


def bell_draw(rng, shape, scale, most, cuts=(), held_as=jnp.bfloat16):
    entries = jax.random.normal(rng, shape, jnp.float32) * scale
    if len(cuts) > 0:
        entries = level_of(rng, shape, cuts, -0.22, 0.18) * entries
    return jnp.clip(entries, min=-most, max=most).astype(held_as)


def setup_inputs(seed: int = 0) -> dict:
    arg_keys = jax.random.split(jax.random.key(seed), 14)
    return {
        "tokens": bell_draw(arg_keys[0], (ROWS, D), 1.0, 6.0, ((0, 32),)),
        "cotangent": bell_draw(arg_keys[1], (ROWS, D), 1.0, 6.0, ((0, 32),)),
        "lengths": draw_lengths(jax.random.fold_in(arg_keys[13], 71), 0),
        "counts": draw_counts(jax.random.fold_in(arg_keys[13], 71), 0),
        "attn_w": draw_attn_w(jax.random.fold_in(arg_keys[13], 71), 0),
        "attn_m": bell_draw(arg_keys[5], (D, 4 * D), (0.111 * PARAMS ** -0.5), 0.00061035156, ((0, 4),), jnp.float32),
        "attn_v": jnp.clip(1.411013528240801e-10 + 4.233040584722403e-10 * jax.random.uniform(arg_keys[6], (D, 4 * D), jnp.float32) ** level_of(arg_keys[6], (D, 4 * D), ((0, 4),), -0.2, 0.2), 1.411013528240801e-10, 5.644054112963204e-10),
        "mlp_w": draw_mlp_w(jax.random.fold_in(arg_keys[13], 71), 0),
        "mlp_m": bell_draw(arg_keys[8], (2, D, FF), (0.111 * PARAMS ** -0.5), 0.00061035156, ((1, 4),), jnp.float32),
        "mlp_v": jnp.clip(1.411013528240801e-10 + 4.233040584722403e-10 * jax.random.uniform(arg_keys[9], (2, D, FF), jnp.float32) ** level_of(arg_keys[9], (2, D, FF), ((1, 4),), -0.2, 0.2), 1.411013528240801e-10, 5.644054112963204e-10),
        "vec_w": draw_vec_w(jax.random.fold_in(arg_keys[13], 71), 0),
        "vec_m": bell_draw(arg_keys[11], (NVEC, D), (0.44 * PARAMS ** -0.5), 0.0024414062, ((1, 4),), jnp.float32),
        "vec_v": jnp.clip(2.2576216451852815e-09 + 6.7728649355558446e-09 * jax.random.uniform(arg_keys[12], (NVEC, D), jnp.float32) ** level_of(arg_keys[12], (NVEC, D), ((1, 4),), -0.2, 0.2), 2.2576216451852815e-09, 9.030486580741126e-09),
    }


@jax.custom_vjp
def low(v):
    return lax.optimization_barrier(v.astype(jnp.bfloat16)).astype(jnp.float32)

@jax.custom_vjp
def low_back(v):
    return v

def low_keep(v):
    return (low(v), None)

def low_pass(kept, grad):
    return (grad,)

def back_keep(v):
    return (v, None)

def back_low(kept, grad):
    return (low(grad),)
low.defvjp(low_keep, low_pass)
low_back.defvjp(back_keep, back_low)
PRECISE = lax.Precision.HIGHEST
NORM_EPSILON = 1e-05
BETA_FIRST = 0.9
BETA_SECOND = 0.999
ADAM_EPSILON = 1e-08
RATE_MATRIX = 0.1
RATE_VECTOR = 0.2
DECAY_MATRIX = 0.1
CLIP_LIMIT = 1.0
MASKED_SCORE = -1e+30

def layer_norm(features, norm_gain, norm_bias):
    centered = features - lax.optimization_barrier(jnp.mean(features, axis=-1, keepdims=True))
    variance = lax.optimization_barrier(jnp.mean(centered * centered, axis=-1, keepdims=True))
    return centered * lax.rsqrt(variance + NORM_EPSILON) * norm_gain + norm_bias

def gelu_tanh(features):
    return jax.nn.gelu(features, approximate=True)

def group_layout(length_row, count_row, slots):
    count_row = count_row.astype(jnp.int32)
    starts = (jnp.cumsum(count_row) - count_row).astype(jnp.int32)
    within = jnp.arange(slots, dtype=jnp.int32)
    position = (starts[:, None] + within[None, :]).reshape(-1).astype(jnp.int32)
    live_rows = (within[None, :] < count_row[:, None]).reshape(-1)
    boundary = jnp.cumsum(length_row.astype(jnp.int32)).astype(jnp.int32)
    segment = lax.optimization_barrier(jnp.sum((position[:, None] >= boundary[None, :]).astype(jnp.int32), axis=1)).astype(jnp.int32)
    buffer_slot = jnp.arange(position.shape[0], dtype=jnp.int32)
    segment = jnp.where(live_rows, segment, -1 - buffer_slot).astype(jnp.int32)
    return (segment, position, live_rows)

def forward(inputs, attn_master, mlp_master, vec_master, segment, position):
    attn_round = low(attn_master)
    mlp_round = low(mlp_master)
    vec_round = low(vec_master)
    total_rows = inputs.shape[0]
    scale = HEAD ** (-0.5)
    fc_rows = FF // D
    normed_first = low(layer_norm(inputs, vec_round[0], vec_round[1]))
    qkv_bias = jnp.concatenate([vec_round[2], jnp.zeros((D,), jnp.float32), vec_round[3]])
    projected = jnp.dot(normed_first, attn_round[:, :3 * D], precision=PRECISE) + qkv_bias
    projected = low(low_back(projected))
    queries = projected[:, :D].reshape(N_SHARD, TOK_CAP, HEADS, HEAD)
    keys_all = projected[:, D:2 * D].reshape(total_rows, HEADS, HEAD)
    values_all = projected[:, 2 * D:].reshape(total_rows, HEADS, HEAD)
    seg_blocks = segment.reshape(N_SHARD, TOK_CAP)
    pos_blocks = position.reshape(N_SHARD, TOK_CAP)

    def attend_rows(piece):
        query_rows, seg_rows, pos_rows = piece
        scores = jnp.einsum('qhd,khd->hqk', query_rows, keys_all, precision=PRECISE) * scale
        scores = low_back(scores)
        allowed = (seg_rows[:, None] == segment[None, :]) & (position[None, :] <= pos_rows[:, None])
        scores = jnp.where(allowed[None], scores, MASKED_SCORE)
        highest = lax.optimization_barrier(jnp.max(scores, axis=-1, keepdims=True))
        weights = jnp.exp(scores - highest)
        weights = low(weights / lax.optimization_barrier(jnp.sum(weights, axis=-1, keepdims=True)))
        return jnp.einsum('hqk,khd->qhd', weights, values_all, precision=PRECISE)
    mixed = lax.map(jax.checkpoint(attend_rows), (queries, seg_blocks, pos_blocks))
    mixed = low(low_back(mixed.reshape(total_rows, D)))
    attn_out = low_back(jnp.dot(mixed, attn_round[:, 3 * D:], precision=PRECISE) + vec_round[4])
    resid = inputs + attn_out
    normed_second = low(layer_norm(resid, vec_round[5], vec_round[6]))
    fc_bias = vec_round[7:7 + fc_rows].reshape(FF)
    preact = low_back(jnp.dot(normed_second, mlp_round[0], precision=PRECISE) + fc_bias)
    activated = low(gelu_tanh(preact))
    mlp_out = low_back(jnp.einsum('tf,df->td', activated, mlp_round[1], precision=PRECISE) + vec_round[7 + fc_rows])
    return resid + mlp_out

def adam_update(master, first, second, gradient, factor, rate, decay):
    clipped = gradient * factor
    first_new = BETA_FIRST * first + (1.0 - BETA_FIRST) * clipped
    second_new = BETA_SECOND * second + (1.0 - BETA_SECOND) * clipped * clipped
    first_hat = first_new / (1.0 - BETA_FIRST ** STEP)
    second_hat = second_new / (1.0 - BETA_SECOND ** STEP)
    master_new = master - rate * (first_hat / (jnp.sqrt(second_hat) + ADAM_EPSILON) + decay * master)
    return (clipped, master_new, first_new, second_new)

def reference(tokens, cotangent, lengths, counts, attn_w, attn_m, attn_v, mlp_w, mlp_m, mlp_v, vec_w, vec_m, vec_v):
    group_rows = N_SHARD * TOK_CAP
    tok_groups = tokens.reshape(N_DP, group_rows, D)
    cot_groups = cotangent.reshape(N_DP, group_rows, D)

    def one_group(totals, piece):
        tok_rows, cot_rows, length_row, count_row = piece
        segment, position, live_rows = group_layout(length_row, count_row, TOK_CAP)

        def run_block(inputs, attn_master, mlp_master, vec_master):
            return forward(inputs, attn_master, mlp_master, vec_master, segment, position)
        output, pull_back = jax.vjp(run_block, tok_rows.astype(jnp.float32), attn_w, mlp_w, vec_w)
        upstream = jnp.where(live_rows[:, None], cot_rows.astype(jnp.float32), 0.0)
        grad_input, grad_attn, grad_mlp, grad_vec = pull_back(upstream)
        totals = (totals[0] + grad_attn, totals[1] + grad_mlp, totals[2] + grad_vec)
        out_rows = jnp.where(live_rows[:, None], output, 0.0).astype(jnp.bfloat16)
        back_rows = jnp.where(live_rows[:, None], grad_input, 0.0).astype(jnp.bfloat16)
        return (totals, (out_rows, back_rows))
    start = (jnp.zeros_like(attn_w), jnp.zeros_like(mlp_w), jnp.zeros_like(vec_w))
    totals, (out_groups, back_groups) = lax.scan(one_group, start, (tok_groups, cot_groups, lengths, counts))
    block_out = out_groups.reshape(-1, D)
    grad_in = back_groups.reshape(-1, D)
    squares = jnp.sum(totals[0] * totals[0]) + jnp.sum(totals[1] * totals[1]) + jnp.sum(totals[2] * totals[2])
    norm_total = jnp.sqrt(squares)
    factor = jnp.minimum(1.0, CLIP_LIMIT / (norm_total + 1e-06))
    attn_grad, attn_w_new, attn_m_new, attn_v_new = adam_update(attn_w, attn_m, attn_v, totals[0], factor, RATE_MATRIX, DECAY_MATRIX)
    mlp_grad, mlp_w_new, mlp_m_new, mlp_v_new = adam_update(mlp_w, mlp_m, mlp_v, totals[1], factor, RATE_MATRIX, DECAY_MATRIX)
    vec_grad, vec_w_new, vec_m_new, vec_v_new = adam_update(vec_w, vec_m, vec_v, totals[2], factor, RATE_VECTOR, 0.0)
    return (block_out, grad_in, attn_grad, mlp_grad, vec_grad, attn_w_new, attn_m_new, attn_v_new, mlp_w_new, mlp_m_new, mlp_v_new, vec_w_new, vec_m_new, vec_v_new, norm_total.reshape(1))
```

```python
import functools

import jax
import jax.numpy as jnp
from jax import lax
from jax.experimental import pallas as pl
from jax.experimental.pallas import tpu as pltpu
from jax.sharding import PartitionSpec as P

HEADS = 12
STEP = 10
NORM_EPSILON = 1e-05
BETA_FIRST = 0.9
BETA_SECOND = 0.999
ADAM_EPSILON = 1e-08
RATE_MATRIX = 0.1
RATE_VECTOR = 0.2
DECAY_MATRIX = 0.1
CLIP_LIMIT = 1.0
MASKED_SCORE = -1e30
QUERY_BLOCK = 256
VMEM_LIMIT = 50 * 1024 * 1024
LOW = jnp.bfloat16
HIGH = jnp.float32


def dot_nn(a, b):
    return lax.dot_general(a, b, (((1,), (0,)), ((), ())), preferred_element_type=HIGH)


def dot_nt(a, b):
    return lax.dot_general(a, b, (((1,), (1,)), ((), ())), preferred_element_type=HIGH)


def low_t(a):
    return a.astype(HIGH).T.astype(LOW)


def normalize(features):
    centered = features - jnp.mean(features, axis=-1, keepdims=True)
    variance = jnp.mean(centered * centered, axis=-1, keepdims=True)
    inverse = lax.rsqrt(variance + NORM_EPSILON)
    return centered * inverse, inverse


def normalize_back(unit, inverse, grad_unit):
    first = jnp.mean(grad_unit, axis=-1, keepdims=True)
    second = jnp.mean(grad_unit * unit, axis=-1, keepdims=True)
    return inverse * (grad_unit - first - unit * second)


def cut_kernel(place, w_ref, vec_ref, *out_refs):
    parts = len(out_refs)
    rows, columns = w_ref.shape
    width = columns // 3
    cols = width // parts
    vec = vec_ref[...]
    tail = [
        jnp.concatenate([vec[3 * k + m : 3 * k + m + 1, :] for m in range(3)], axis=1)
        for k in range(vec.shape[0] // 3)
    ]
    tail.append(jnp.zeros((16 - len(tail), 3 * cols), HIGH))
    tail = jnp.concatenate(tail, axis=0).astype(LOW)
    for r in range(parts):
        starts = [k * width + r * cols for k in range(3)]
        piece = jnp.concatenate([w_ref[:, c : c + cols] for c in starts], axis=1).astype(LOW)
        for j in range(parts):

            @pl.when((place[0] ^ j) == r)
            def _():
                out_refs[j][:rows, :] = piece
                out_refs[j][rows:, :] = tail


def widen_kernel(half, out_ref, mlp_ref, wide_ref, *half_refs):
    rows, width = out_ref.shape
    start = pl.multiple_of(half[0] * (rows // 2), 16)
    near = pl.ds(start, rows // 2)
    sources = [(out_ref[...], out_ref[near, :])]
    for f in range(mlp_ref.shape[2] // width):
        span = slice(f * width, (f + 1) * width)
        sources += [(mlp_ref[n, :, span], mlp_ref[n, near, span]) for n in range(2)]
    split = half_refs[0].shape[1] // width
    for n, (block, part) in enumerate(sources):
        wide_ref[:, n * width : (n + 1) * width] = block.astype(LOW)
        k = int(n >= split)
        at = (n - k * split) * width
        half_refs[k][:, at : at + width] = part.astype(LOW)


def project_kernel(parts, place, *refs):
    x_refs, w_refs, refs = refs[:parts], refs[parts : 2 * parts], refs[2 * parts :]
    bias_ref, a1_ref, qkv_ref, wt_ref, vec_ref, w_scr, x_scr, sems = refs
    step = pl.program_id(0)
    rows = vec_ref.shape[1] // parts

    def copy(j):
        return pltpu.make_async_copy(x_refs[j], x_scr.at[j], sems.at[j])

    @pl.when(step == 0)
    def _():
        for j in range(parts):
            copy(j).start()
        vec_ref[...] = jnp.zeros_like(vec_ref)
        for j in range(parts):
            start = pl.multiple_of((place[0] ^ j) * rows, 16)
            w_scr[pl.ds(start, rows), :] = w_refs[j][:rows, :].astype(HIGH)
            tail = w_refs[j][rows:, :].astype(HIGH)
            for r in range(parts):

                @pl.when((place[0] ^ j) == r)
                def _():
                    for n in range(12):
                        piece = tail[n // 3 : n // 3 + 1, n % 3 * rows : (n % 3 + 1) * rows]
                        vec_ref[n : n + 1, r * rows : (r + 1) * rows] = piece

        wt_ref[...] = w_scr[...].T.astype(LOW)

    for j in range(parts):

        @pl.when(step == j)
        def _():
            copy(j).wait()

    unit, _ = normalize(x_scr[step].astype(HIGH))
    a1 = (unit * vec_ref[0:1, :] + vec_ref[1:2, :]).astype(LOW)
    a1_ref[...] = a1
    qkv_ref[...] = (dot_nt(wt_ref[...], a1) + bias_ref[...]).astype(LOW)


def masked_scores(q, kt, seg_q, seg_k, start):
    block = q.shape[0]
    out = []
    if start:
        s = dot_nn(q, kt[:, :start])
        out.append(jnp.where(seg_q == seg_k[:, :start], s, MASKED_SCORE))
    s = dot_nn(q, kt[:, start : start + block])
    row = lax.broadcasted_iota(jnp.int32, (block, block), 0)
    col = lax.broadcasted_iota(jnp.int32, (block, block), 1)
    allowed = (seg_q == seg_k[:, start : start + block]) & (col <= row)
    out.append(jnp.where(allowed, s, MASKED_SCORE))
    return out


def attend_kernel(scale, place, qt_ref, kt_ref, vt_ref, segc_ref, segr_ref, o_ref, lse_ref, v_scr):
    total = qt_ref.shape[1]
    per_part = o_ref.shape[2]
    block = min(QUERY_BLOCK, per_part)
    v_scr[...] = low_t(vt_ref[...])
    for start in range(0, total, block):
        span = slice(start, start + block)
        q = (qt_ref[:, span].astype(HIGH) * scale).T.astype(LOW)
        pieces = masked_scores(q, kt_ref, segc_ref[span, :], segr_ref, start)
        top = functools.reduce(jnp.maximum, [jnp.max(s, axis=1, keepdims=True) for s in pieces])
        weights = [jnp.exp(s - top) for s in pieces]
        mass = sum(jnp.sum(w, axis=1, keepdims=True) for w in weights)
        lse_ref[0, span, :] = top + jnp.log(mass)
        inverse = 1.0 / mass
        mixed = dot_nn((weights[-1] * inverse).astype(LOW), v_scr[span, :])
        if start:
            mixed += dot_nn((weights[0] * inverse).astype(LOW), v_scr[:start, :])
        inner = start % per_part
        o_ref[place[0] ^ (start // per_part), :, inner : inner + block] = mixed.T.astype(LOW)


def attend_back_kernel(
    scale, place, qt_ref, kt_ref, vt_ref, segc_ref, segr_ref, lse_ref, *refs
):
    *do_refs, out_ref, k_scr, do_scr, dk_scr, dv_scr = refs
    total = qt_ref.shape[1]
    parts, per_part = len(do_refs), do_refs[0].shape[1]
    block = min(QUERY_BLOCK, per_part)
    k_scr[...] = low_t(kt_ref[...])
    for j in range(parts):
        do_scr[place[0] ^ j] = do_refs[j][...]
    dk_scr[...] = jnp.zeros_like(dk_scr)
    dv_scr[...] = jnp.zeros_like(dv_scr)
    for start in range(0, total, block):
        span = slice(start, start + block)
        inner = start % per_part
        qt = qt_ref[:, span].astype(HIGH) * scale
        dot_ = do_scr[start // per_part, :, inner : inner + block]
        q = qt.T.astype(LOW)
        qt = qt.astype(LOW)
        do = low_t(dot_)
        pieces = masked_scores(q, kt_ref, segc_ref[span, :], segr_ref, start)
        spans = [slice(0, start), span] if start else [span]
        lse = lse_ref[0, span, :]
        weights = [jnp.exp(s - lse) for s in pieces]
        grads = [dot_nn(do, vt_ref[:, at]) for at in spans]
        delta = sum(jnp.sum(g * w, axis=1, keepdims=True) for g, w in zip(grads, weights))
        dq = None
        for at, w, g in zip(spans, weights, grads):
            ds = (w * (g - delta)).astype(LOW)
            term = dot_nn(ds, k_scr[at, :])
            dq = term if dq is None else dq + term
            dk_scr[:, at] += dot_nn(qt, ds)
            dv_scr[:, at] += dot_nn(dot_, w.astype(LOW))
        out_ref[0, :, span] = (dq * scale).T.astype(LOW)
    out_ref[1] = dk_scr[...].astype(LOW)
    out_ref[2] = dv_scr[...].astype(LOW)


def projection_back_kernel(heads, parts, place, half, *refs):
    x_refs, (a1_ref, *refs) = refs[:parts], refs[parts:]
    head_refs, refs = refs[:heads], refs[heads:]
    wt_ref, vec_ref, grads_ref, keep_ref, send_ref, qkeep_ref, qsend_ref, *scratch = refs
    g_scr, vec_scr, sums_scr, ext_scr, all_scr, x_scr, sems = scratch
    step = pl.program_id(0)
    cols = g_scr.shape[0] // 3
    extra = grads_ref.shape[0]
    count = qkeep_ref.shape[2] - 3 * cols

    def copy(j):
        return pltpu.make_async_copy(x_refs[j], x_scr.at[j], sems.at[j])

    @pl.when(step == 0)
    def _():
        for j in range(parts):
            copy(j).start()
        g_scr[...] = jnp.zeros_like(g_scr)
        vec_scr[...] = grads_ref[...]
        sums_scr[...] = jnp.zeros_like(sums_scr)

    for j in range(parts):

        @pl.when(step == j)
        def _():
            copy(j).wait()

    dqkv = jnp.concatenate([ref[k] for k in range(3) for ref in head_refs], axis=0)
    da1 = dot_nn(low_t(dqkv), wt_ref[...])

    @pl.when(step % 2 == 0)
    def _():
        keep_ref[0] = da1.astype(LOW)

    @pl.when(step % 2 == 1)
    def _():
        send_ref[0] = da1.astype(LOW)

    g_scr[...] += dot_nn(dqkv, a1_ref[...])
    unit, _ = normalize(x_scr[step].astype(HIGH))
    vec_scr[0:1, :] += jnp.sum(da1 * unit, axis=0, keepdims=True)
    vec_scr[1:2, :] += jnp.sum(da1, axis=0, keepdims=True)
    sums_scr[...] += jnp.sum(dqkv.astype(HIGH), axis=1, keepdims=True)

    @pl.when(step == pl.num_programs(0) - 1)
    def _():
        ext_scr[...] = vec_scr[...].T
        own = pl.ds(pl.multiple_of(place[0] * cols, 16), cols)
        ext_scr[own, 2:3] = sums_scr[:cols, :]
        ext_scr[own, 3:4] = sums_scr[2 * cols :, :]
        all_scr[:, : 3 * cols] = g_scr[...].T
        all_scr[:, 3 * cols : 3 * cols + extra] = ext_scr[...]
        rows = all_scr.shape[0] // parts
        for r in range(parts):
            for ref, side in ((qkeep_ref, half[0]), (qsend_ref, 1 - half[0])):
                start = pl.multiple_of(r * rows + side * (rows // 2), 16)
                ref[r] = all_scr[pl.ds(start, rows // 2), : 3 * cols + count].astype(LOW)


GELU_C = 0.7978845608028654
GELU_A = 0.044715


def mlp_kernel(
    parts, first_blocks, place, half, live_ref, x_ref, cot_ref, vec_ref, *refs
):
    o_refs, refs = refs[:parts], refs[parts:]
    own_ref, core_ref, *wide_refs = refs[:10]
    out_ref, *grad_refs = refs[10:15]
    dr1_ref, vecg_ref, *refs = refs[15:]
    do_refs, scratch = refs[:parts], refs[parts:]
    wide, ot_scr, r1_scr, a2_scr, a2t_scr, dy_scr, dyt_scr, y_scr, da2_scr, act_scr, sems = scratch
    step = pl.program_id(0)
    rows = o_refs[0].shape[0]
    slots, width = x_ref.shape
    bo, gain, shift, bp = (vec_ref[r : r + 1, :] for r in (4, 5, 6, 11))
    split = wide_refs[0].shape[1]
    live = lax.broadcasted_iota(jnp.int32, (slots, 1), 0) < live_ref[0]

    def copies(k):
        half_rows = rows // 2
        near, far = half[0] * half_rows, (1 - half[0]) * half_rows
        span = slice(0, split) if k == 0 else slice(split, wide.shape[1])
        sources = [(own_ref.at[:, span], 0, 0), (core_ref.at[:, span], 1, 0)]
        spots = [(2, near), (2, far), (3, near), (3, far)]
        sources += [(wide_refs[4 * k + n], *spot) for n, spot in enumerate(spots)]
        for n, (source, j, offset) in enumerate(sources):
            start = pl.multiple_of((place[0] ^ j) * rows + offset, 16)
            target = wide.at[pl.ds(start, source.shape[0]), span]
            yield pltpu.make_async_copy(source, target, sems.at[k, n])

    def block(n):
        return wide[:, pl.ds(pl.multiple_of(n * width, 128), width)]

    def permuted(scratch, value):
        for j in range(parts):
            scratch[j * rows : (j + 1) * rows, :] = value(pl.multiple_of((place[0] ^ j) * rows, 16))

    def put(value):
        value = value.astype(LOW)
        for k in range(2):

            @pl.when((step >= first_blocks) == bool(k))
            def _():
                keep, send = grad_refs[2 * k : 2 * k + 2]
                for j in range(parts):
                    (send if j % 2 else keep)[j // 2] = value[j * rows : (j + 1) * rows, :]

    @pl.when(step == 0)
    def _():
        for k in range(2):
            for copy in copies(k):
                copy.start()
        for j in range(parts):
            start = pl.multiple_of((place[0] ^ j) * rows, 16)
            ot_scr[pl.ds(start, rows), :] = o_refs[j][...]
        mixed = low_t(ot_scr[...])
        dy = jnp.where(live, cot_ref[...].astype(HIGH), 0.0)
        dy_scr[...] = dy.astype(LOW)
        ot_scr[...] = dy.T.astype(LOW)
        permuted(dyt_scr, lambda start: ot_scr[pl.ds(start, rows), :])
        for copy in copies(0):
            copy.wait()
        r1 = x_ref[...].astype(HIGH) + dot_nn(mixed, wide[:, :width]) + bo
        r1_scr[...] = r1
        unit, _ = normalize(r1)
        a2 = unit * gain + shift
        a2_scr[...] = a2.astype(LOW)
        ot_scr[...] = a2.T.astype(LOW)
        permuted(a2t_scr, lambda start: ot_scr[pl.ds(start, rows), :])
        vecg_ref[...] = jnp.zeros_like(vecg_ref)
        vecg_ref[11:12, :] = jnp.sum(dy, axis=0, keepdims=True)
        y_scr[...] = r1 + bp
        da2_scr[...] = jnp.zeros_like(da2_scr)

    @pl.when(step == first_blocks)
    def _():
        for copy in copies(1):
            copy.wait()

    last = pl.num_programs(0) - 1

    @pl.when((step < last) & (step % 2 == 0))
    def _():
        w_fc, w_pt = block(1 + step), block(2 + step)
        u = dot_nn(a2_scr[...], w_fc) + vec_ref[pl.ds(7 + step // 2, 1), :]
        square = u * u
        t = jnp.tanh(GELU_C * (u + GELU_A * (square * u)))
        grown = 0.5 * (1.0 + t)
        act = (u * grown).astype(LOW)
        act_scr[...] = act
        y_scr[...] += dot_nt(act, w_pt)
        slope = grown + 0.5 * u * (1.0 - t * t) * (GELU_C + (3.0 * GELU_C * GELU_A) * square)
        du = (dot_nn(dy_scr[...], w_pt) * slope).astype(LOW)
        vecg_ref[pl.ds(7 + step // 2, 1), :] = jnp.sum(du.astype(HIGH), axis=0, keepdims=True)
        da2_scr[...] += dot_nt(du, w_fc)
        put(dot_nn(a2t_scr[...], du))

    @pl.when((step < last) & (step % 2 == 1))
    def _():
        put(dot_nn(dyt_scr[...], act_scr[...]))

    @pl.when(step == last)
    def _():
        out_ref[...] = jnp.where(live, y_scr[...], 0.0).astype(LOW)
        unit, inverse = normalize(r1_scr[...])
        da2 = da2_scr[...]
        vecg_ref[5:6, :] = jnp.sum(da2 * unit, axis=0, keepdims=True)
        vecg_ref[6:7, :] = jnp.sum(da2, axis=0, keepdims=True)
        dr1 = dy_scr[...].astype(HIGH) + normalize_back(unit, inverse, da2 * gain)
        dr1_ref[...] = dr1
        low = dr1.astype(LOW)
        vecg_ref[4:5, :] = jnp.sum(low.astype(HIGH), axis=0, keepdims=True)
        put(dot_nn(jnp.concatenate([ref[...] for ref in o_refs], axis=0), low))
        for j in range(parts):
            start = pl.multiple_of((place[0] ^ j) * rows, 16)
            do_refs[j][...] = dot_nt(wide[pl.ds(start, rows), :width], low).astype(LOW)


def group_layout(length_row, count_row, slots):
    starts = jnp.cumsum(count_row) - count_row
    within = jnp.arange(slots, dtype=jnp.int32)
    position = (starts[:, None] + within[None, :]).reshape(-1)
    live_rows = (within[None, :] < count_row[:, None]).reshape(-1)
    boundary = jnp.cumsum(length_row)
    segment = jnp.sum((position[:, None] >= boundary[None, :]).astype(jnp.int32), axis=1)
    buffer_slot = jnp.arange(position.shape[0], dtype=jnp.int32)
    return jnp.where(live_rows, segment, -1 - buffer_slot)


def adam_update(master, first, second, gradient, factor, rate, decay):
    clipped = gradient * factor
    first_new = BETA_FIRST * first + (1.0 - BETA_FIRST) * clipped
    second_new = BETA_SECOND * second + (1.0 - BETA_SECOND) * clipped * clipped
    first_hat = first_new / (1.0 - BETA_FIRST**STEP)
    second_hat = second_new / (1.0 - BETA_SECOND**STEP)
    master_new = master - rate * (
        first_hat / (jnp.sqrt(second_hat) + ADAM_EPSILON) + decay * master
    )
    return (clipped, master_new, first_new, second_new)


def adam_kernel(fc_rows, factor_ref, _, *refs):
    grads, states, outs = refs[:4], refs[4:10], refs[10:]
    near = pl.program_id(0) < pl.num_programs(0) // 2
    first, second = grads[0][0], grads[1][0]
    factor = factor_ref[0]
    width = outs[0].shape[-1] // fc_rows
    qkv = jnp.where(near, grads[2][0], grads[3][0])[:, : 3 * width]

    def update(gradient, at, base):
        results = adam_update(
            *[states[base + n][at] for n in range(3)],
            gradient.astype(HIGH), factor, RATE_MATRIX, DECAY_MATRIX,
        )
        for n, result in enumerate(results):
            outs[base // 3 * 4 + n][at] = result

    blocks = [first[:, n : n + width] for n in range(0, first.shape[1], width)]
    blocks += [second[:, n : n + width] for n in range(0, second.shape[1], width)]
    for f in range(fc_rows):
        span = slice(f * width, (f + 1) * width)
        for n in range(2):
            update(blocks[2 * f + n], (n, 0, slice(None), span), 3)
    update(qkv, (0, slice(None), slice(0, 3 * width)), 0)
    update(blocks[-1], (0, slice(None), slice(3 * width, 4 * width)), 0)


def swap(array, axis, bit, count):
    return lax.ppermute(array, axis, [(i, i ^ bit) for i in range(count)])


def pick(array, index):
    return lax.dynamic_index_in_dim(array, index, 0, keepdims=False)


def deal(pieces, parts):
    return list(pieces[:1]) + [swap(pieces[j], "shard", j, parts) for j in range(1, parts)]


def in_order(relative, place, parts):
    relative = jnp.stack(relative)
    return jnp.stack([pick(relative, place ^ r) for r in range(parts)])


def collect(own, parts):
    have = [own]
    bit = parts // 2
    slots = [0]
    while bit:
        have = have + [swap(piece, "shard", bit, parts) for piece in have]
        slots = slots + [s ^ bit for s in slots]
        bit //= 2
    return [have[slots.index(j)] for j in range(parts)]


def after(value, *others):
    return lax.optimization_barrier((value, *others))[0]


def add_low(a, b):
    return (a.astype(HIGH) + b.astype(HIGH)).astype(LOW)


def bits_of(count):
    return [1 << n for n in range(count.bit_length() - 1)]


def halve(array, upper, dim):
    length = array.shape[dim] // 2
    keep = lax.dynamic_slice_in_dim(array, upper * length, length, dim)
    return keep, lax.dynamic_slice_in_dim(array, (1 - upper) * length, length, dim)


def scatter_half(array, dim, bit, replica, replicas):
    keep, send = halve(array, (replica // bit) % 2, dim)
    return keep, swap(send, "dp", bit, replicas)


def params(*semantics):
    return pltpu.CompilerParams(dimension_semantics=semantics, vmem_limit_bytes=VMEM_LIMIT)


def cost(flops, moved, special=0):
    return pl.CostEstimate(flops=int(flops), bytes_accessed=int(moved), transcendentals=int(special))


def whole(*shape):
    zeros = (0,) * len(shape)
    return pl.BlockSpec(shape, lambda *_: zeros)


def make_on_device(parts, replicas):
    def on_device(
        tokens, cotangent, lengths, counts,
        attn_w, attn_m, attn_v, mlp_w, mlp_m, mlp_v, vec_w, vec_m, vec_v,
    ):
        slots, width = tokens.shape
        rows = attn_w.shape[0]
        hidden = mlp_w.shape[2]
        fc_rows = hidden // width
        total = parts * slots
        head_size = width // HEADS
        own_heads = HEADS // parts
        own_cols = own_heads * head_size
        scale = head_size ** (-0.5)
        place = lax.axis_index("shard")
        replica = lax.axis_index("dp")
        prefetch = place.reshape(1).astype(jnp.int32)

        half = replica % 2
        side = half.reshape(1).astype(jnp.int32)

        x_all = collect(tokens, parts)
        w_pieces = pl.pallas_call(
            cut_kernel,
            grid_spec=pltpu.PrefetchScalarGridSpec(
                num_scalar_prefetch=1,
                grid=(1,),
                in_specs=[whole(rows, 3 * width), whole(vec_w.shape[0], rows)],
                out_specs=[whole(rows + 16, 3 * own_cols)] * parts,
            ),
            out_shape=[jax.ShapeDtypeStruct((rows + 16, 3 * own_cols), LOW)] * parts,
            compiler_params=params("arbitrary"),
            cost_estimate=cost(0, 4e6),
            name="cut",
        )(prefetch, attn_w, vec_w)
        w_local = deal(w_pieces, parts)

        blocks = 2 * fc_rows + 1
        split = (fc_rows // 2 * 2 + 1) * width
        wide_own, *wide_half = pl.pallas_call(
            widen_kernel,
            grid_spec=pltpu.PrefetchScalarGridSpec(
                num_scalar_prefetch=1,
                grid=(1,),
                in_specs=[
                    pl.BlockSpec((rows, width), lambda *_: (0, 3)),
                    whole(2, rows, hidden),
                ],
                out_specs=[
                    whole(rows, blocks * width),
                    whole(rows // 2, split),
                    whole(rows // 2, blocks * width - split),
                ],
            ),
            out_shape=[
                jax.ShapeDtypeStruct((rows, blocks * width), LOW),
                jax.ShapeDtypeStruct((rows // 2, split), LOW),
                jax.ShapeDtypeStruct((rows // 2, blocks * width - split), LOW),
            ],
            compiler_params=params("arbitrary"),
            cost_estimate=cost(0, 12e6),
            name="widen",
        )(side, attn_w, mlp_w)
        wide_own, *wide_half = lax.optimization_barrier((wide_own, *wide_half, *w_local, *x_all))[:3]
        near = [swap(mine, "shard", parts // 2, parts) for mine in wide_half]
        wide_core = swap(wide_own, "shard", 1, parts)

        segment = group_layout(lengths[0], counts[0], slots)
        seg_col = segment[:, None]
        seg_row = segment[None, :]
        own_vec = vec_w.astype(LOW).astype(HIGH)
        bias_local = jnp.concatenate(
            [own_vec[2], jnp.zeros((own_cols,), HIGH), own_vec[3]]
        )[:, None]

        a1, qkv, w_t, vectors = pl.pallas_call(
            functools.partial(project_kernel, parts),
            grid_spec=pltpu.PrefetchScalarGridSpec(
                num_scalar_prefetch=1,
                grid=(parts,),
                in_specs=[
                    *[pl.BlockSpec(memory_space=pl.ANY)] * parts,
                    *[whole(rows + 16, 3 * own_cols)] * parts,
                    whole(3 * own_cols, 1),
                ],
                out_specs=[
                    pl.BlockSpec((slots, width), lambda i, p: (p[0] ^ i, 0)),
                    pl.BlockSpec((3 * own_cols, slots), lambda i, p: (0, p[0] ^ i)),
                    whole(3 * own_cols, width),
                    whole(16, width),
                ],
                scratch_shapes=[
                    pltpu.VMEM((width, 3 * own_cols), HIGH),
                    pltpu.VMEM((parts, slots, width), LOW),
                    pltpu.SemaphoreType.DMA((parts,)),
                ],
            ),
            out_shape=[
                jax.ShapeDtypeStruct((total, width), LOW),
                jax.ShapeDtypeStruct((3 * own_cols, total), LOW),
                jax.ShapeDtypeStruct((3 * own_cols, width), LOW),
                jax.ShapeDtypeStruct((16, width), HIGH),
            ],
            compiler_params=params("arbitrary"),
            cost_estimate=cost(2 * total * width * 3 * own_cols * 3, 12e6),
            name="project",
        )(prefetch, *x_all, *w_local, bias_local)

        pair_flops = 2 * total * total * head_size * 4 // 2

        def head_specs(h):
            return [
                pl.BlockSpec((head_size, total), functools.partial(lambda k, *_: (k * own_heads + h, 0), k))
                for k in range(3)
            ]

        def attend(h, qkv):
            return pl.pallas_call(
                functools.partial(attend_kernel, scale),
                grid_spec=pltpu.PrefetchScalarGridSpec(
                    num_scalar_prefetch=1,
                    grid=(1,),
                    in_specs=head_specs(h) + [whole(total, 1), whole(1, total)],
                    out_specs=[whole(parts, head_size, slots), whole(1, total, 1)],
                    scratch_shapes=[pltpu.VMEM((total, head_size), LOW)],
                ),
                out_shape=[
                    jax.ShapeDtypeStruct((parts, head_size, slots), LOW),
                    jax.ShapeDtypeStruct((1, total, 1), HIGH),
                ],
                compiler_params=params("arbitrary"),
                cost_estimate=cost(2 * pair_flops, 4e6, total * total // 2),
                name="attend",
            )(prefetch, qkv, qkv, qkv, seg_col, seg_row)

        mixed, lse = [], []
        for h in range(own_heads):
            if h == 1:
                qkv, near[0] = lax.optimization_barrier((qkv, near[0]))
                far = [swap(near[0], "dp", 1, replicas)]
                turned = [swap(near[0], "shard", 1, parts)]
            head_mixed, head_lse = attend(h, qkv)
            mixed.append(head_mixed)
            lse.append(head_lse)
        near[1] = after(near[1], mixed[-1])
        far.append(swap(near[1], "dp", 1, replicas))
        mixed_own = deal(
            [jnp.concatenate([head[j] for head in mixed], axis=0) for j in range(parts)], parts
        )
        turned.append(swap(near[1], "shard", 1, parts))
        wide = [wide_own, wide_core]
        for k in range(2):
            wide += [near[k], far[k], turned[k], swap(far[k], "shard", 1, parts)]

        steps = blocks
        live_own = lax.dynamic_index_in_dim(counts[0], place, 0, keepdims=True)
        first_blocks = fc_rows // 2 * 2

        def grad_spec(k):
            first, last = ((0, first_blocks - 1), (first_blocks, steps - 1))[k]
            return pl.BlockSpec(
                (parts // 2, rows, width), lambda i, *_: (0, 0, jnp.clip(i, first, last) - first)
            )

        grad_columns = [first_blocks * width, (steps - first_blocks) * width]

        in_hbm = pl.BlockSpec(memory_space=pltpu.HBM)
        out = pl.pallas_call(
            functools.partial(mlp_kernel, parts, first_blocks),
            grid_spec=pltpu.PrefetchScalarGridSpec(
                num_scalar_prefetch=3,
                grid=(steps,),
                in_specs=[whole(slots, width), whole(slots, width), whole(16, width)]
                + [whole(own_cols, slots)] * parts
                + [in_hbm] * len(wide),
                out_specs=[whole(slots, width)]
                + [grad_spec(k) for k in range(2) for _ in range(2)]
                + [whole(slots, width), whole(16, width)]
                + [whole(own_cols, slots)] * parts,
                scratch_shapes=[
                    pltpu.VMEM((width, blocks * width), LOW),
                    pltpu.VMEM((width, slots), LOW),
                    pltpu.VMEM((slots, width), HIGH),
                    pltpu.VMEM((slots, width), LOW),
                    pltpu.VMEM((width, slots), LOW),
                    pltpu.VMEM((slots, width), LOW),
                    pltpu.VMEM((width, slots), LOW),
                    pltpu.VMEM((slots, width), HIGH),
                    pltpu.VMEM((slots, width), HIGH),
                    pltpu.VMEM((slots, width), LOW),
                    pltpu.SemaphoreType.DMA((2, 6)),
                ],
            ),
            out_shape=[jax.ShapeDtypeStruct((slots, width), LOW)]
            + [jax.ShapeDtypeStruct((parts // 2, rows, c), LOW) for c in grad_columns for _ in range(2)]
            + [jax.ShapeDtypeStruct((slots, width), HIGH), jax.ShapeDtypeStruct((16, width), HIGH)]
            + [jax.ShapeDtypeStruct((own_cols, slots), LOW)] * parts,
            compiler_params=params("arbitrary"),
            cost_estimate=cost(2 * slots * width * (6 * hidden + 3 * width), 30e6, slots * hidden),
            name="mlp",
        )(prefetch, side, live_own, tokens, cotangent, vectors, *mixed_own, *wide)
        block_out, keep_a, send_a, keep_b, send_b, grad_resid, mid_grads, *do_pieces = out

        do_own = deal(do_pieces, parts)
        got_a = swap(send_a, "shard", 1, parts)
        got_b = swap(send_b, "shard", 1, parts)
        own_a, other_a = [add_low(keep_a[n], got_a[n]) for n in range(2)]
        own_b, other_b = halve(add_low(keep_b, got_b), half, 1)
        *do_own, own_a, other_a, own_b, other_b = lax.optimization_barrier(
            (*do_own, own_a, other_a, own_b, other_b)
        )
        got_a = swap(other_a, "shard", parts // 2, parts)
        got_b = swap(other_b, "dp", 1, replicas)

        def attend_back(h, qkv):
            return pl.pallas_call(
                functools.partial(attend_back_kernel, scale),
                grid_spec=pltpu.PrefetchScalarGridSpec(
                    num_scalar_prefetch=1,
                    grid=(1,),
                    in_specs=head_specs(h)
                    + [whole(total, 1), whole(1, total), whole(1, total, 1)]
                    + [pl.BlockSpec((head_size, slots), lambda *_: (h, 0))] * parts,
                    out_specs=whole(3, head_size, total),
                    scratch_shapes=[
                        pltpu.VMEM((total, head_size), LOW),
                        pltpu.VMEM((parts, head_size, slots), LOW),
                        pltpu.VMEM((head_size, total), HIGH),
                        pltpu.VMEM((head_size, total), HIGH),
                    ],
                ),
                out_shape=jax.ShapeDtypeStruct((3, head_size, total), LOW),
                compiler_params=params("arbitrary"),
                cost_estimate=cost(
                    5 * pair_flops, 4e6, total * total // 2
                ),
                name="attend_back",
            )(prefetch, qkv, qkv, qkv, seg_col, seg_row, lse[h], *do_own)

        dqkv = [attend_back(h, qkv) for h in range(own_heads)]
        *dqkv, got_a = lax.optimization_barrier((*dqkv, got_a))
        own_a, other_a = halve(add_low(own_a, got_a), half, 0)
        dqkv[0] = after(dqkv[0], other_a)
        got_a = swap(other_a, "dp", 1, replicas)

        q_cols = 3 * own_cols
        extra = vec_w.shape[0]
        half_rows = rows // 2
        da1_keep, da1_send, own_q, other_q = pl.pallas_call(
            functools.partial(projection_back_kernel, own_heads, parts),
            grid_spec=pltpu.PrefetchScalarGridSpec(
                num_scalar_prefetch=2,
                grid=(parts,),
                in_specs=[
                    *[pl.BlockSpec(memory_space=pl.ANY)] * parts,
                    pl.BlockSpec((slots, width), lambda i, p, _: (p[0] ^ i, 0)),
                ]
                + [pl.BlockSpec((3, head_size, slots), lambda i, p, _: (0, 0, p[0] ^ i))] * own_heads
                + [whole(q_cols, width), whole(16, width), whole(16, width)],
                out_specs=[pl.BlockSpec((1, slots, width), lambda i, *_: (i // 2, 0, 0))] * 2
                + [whole(parts, half_rows, q_cols + extra)] * 2,
                scratch_shapes=[
                    pltpu.VMEM((q_cols, width), HIGH),
                    pltpu.VMEM((16, width), HIGH),
                    pltpu.VMEM((q_cols, 1), HIGH),
                    pltpu.VMEM((width, 16), HIGH),
                    pltpu.VMEM((width, q_cols + 64), HIGH),
                    pltpu.VMEM((parts, slots, width), LOW),
                    pltpu.SemaphoreType.DMA((parts,)),
                ],
            ),
            out_shape=[jax.ShapeDtypeStruct((parts // 2, slots, width), LOW)] * 2
            + [jax.ShapeDtypeStruct((parts, half_rows, q_cols + extra), LOW)] * 2,
            compiler_params=params("arbitrary"),
            cost_estimate=cost(4 * total * width * 3 * own_cols * 2, 16e6),
            name="projection_back",
        )(prefetch, side, *x_all, a1, *dqkv, w_t, vectors, mid_grads)

        share = rows // replicas
        z_bits = [bit for bit in (1 << n for n in range(1, 20)) if bit < replicas]
        got_q = swap(other_q, "dp", 1, replicas)
        got_b = after(got_b, own_q)
        sum_b = add_low(own_b, got_b)
        got_b = swap(sum_b[1], "shard", parts // 2, parts)
        da1_got = swap(da1_send, "shard", 1, parts)

        got_a = after(got_a, sum_b)
        sum_a = add_low(own_a, got_a)
        states = {"a": sum_a}
        dims = {"a": 0, "q": 1, "b": 0}
        pending = {"q": (own_q, got_q), "b": (sum_b[0], got_b)}
        last = sum_a
        pending["a"] = scatter_half(sum_a, 0, z_bits[0], replica, replicas)
        for name in ("q", "b"):
            keep, got = pending[name]
            last = add_low(keep, after(got, last))
            pending[name] = scatter_half(last, dims[name], z_bits[0], replica, replicas)
        parts_done = {}
        for bit in z_bits[1:]:
            for name in ("a", "q", "b"):
                keep, got = pending[name]
                last = add_low(keep, after(got, last))
                pending[name] = scatter_half(last, dims[name], bit, replica, replicas)
        for name in ("a", "q", "b"):
            keep, got = pending[name]
            last = add_low(keep, after(got, last))
            parts_done[name] = last
        part_a, part_q, part_b = (parts_done[name] for name in ("a", "q", "b"))
        all_a = lax.all_gather(part_a, "dp", axis=0)
        all_b = lax.all_gather(part_b, "dp", axis=0)

        def as_pair(value):
            high = lax.reduce_precision(value, 8, 7)
            return jnp.stack([high, value - high]).astype(LOW)

        main = part_q[:, :, :q_cols]
        squares = sum(jnp.sum(jnp.square(p.astype(HIGH))) for p in (part_a, part_b, main))
        vec_parts = part_q[:, :, q_cols:].transpose(1, 0, 2).reshape(1, share, parts * extra)
        shared = jnp.concatenate(
            [vec_parts, jnp.broadcast_to(as_pair(squares), (1, share, 2))], axis=2
        )
        pieces = jnp.concatenate([main, jnp.broadcast_to(shared, (parts,) + shared.shape[1:])], axis=2)
        dealt = in_order(deal([pick(pieces, place ^ j) for j in range(parts)], parts), place, parts)
        q_rows = (
            dealt[:, :, :q_cols]
            .reshape(parts, share, 3, own_cols)
            .transpose(1, 2, 0, 3)
            .reshape(share, 3 * width)
        )
        summed = jnp.sum(dealt[:, :, q_cols:].astype(HIGH), axis=0)
        vec_parts = summed[:, : parts * extra].reshape(share, parts, extra).astype(LOW)
        squares = jnp.sum(summed[0, parts * extra :]) + jnp.sum(jnp.square(vec_parts.astype(HIGH)))
        vec_own = lax.dynamic_index_in_dim(vec_parts, place, 1, keepdims=False)
        near_q = jnp.concatenate(
            [q_rows, vec_own, jnp.broadcast_to(as_pair(squares), (share, 2))], axis=1
        )[None]
        for bit in z_bits[::-1]:
            near_q = jnp.concatenate([near_q, swap(near_q, "dp", bit, replicas)], axis=0)
        far_q = swap(near_q, "dp", 1, replicas)

        def block_of(index):
            block = index % 2
            for bit in z_bits:
                block = block * 2 + index // bit % 2
            return block

        def index_of(block):
            index = 0
            for bit in z_bits[::-1]:
                index = index + block % 2 * bit
                block = block // 2
            return index + block

        turn = block_of(replica)
        small = jnp.concatenate([near_q[:, :, 3 * width :], far_q[:, :, 3 * width :]], axis=0)
        small = jnp.stack([pick(small, turn ^ r) for r in range(replicas)]).astype(HIGH)
        summed_vec = small[:, :, :extra].reshape(rows, extra).T
        squares = jnp.sum(small[:, 0, extra:])

        own_da1 = da1_keep[0].astype(HIGH) + da1_got[0].astype(HIGH)
        da1 = own_da1 + swap(add_low(da1_keep[1], da1_got[1]), "shard", 2, parts).astype(HIGH)
        unit, inverse = normalize(tokens.astype(HIGH))
        grad_input = grad_resid + normalize_back(unit, inverse, da1 * vectors[0:1])
        live_rows = jnp.arange(slots, dtype=jnp.int32) < live_own[0]
        grad_in = jnp.where(live_rows[:, None], grad_input, 0.0).astype(LOW)

        norm_total = jnp.sqrt(squares)
        factor = jnp.minimum(1.0, CLIP_LIMIT / (norm_total + 1e-06))
        near_count = replicas // 2
        q_block = (1,) + near_q.shape[1:]

        def gathered_spec(array):
            return pl.BlockSpec((1,) + array.shape[1:], lambda i, _, p: (index_of(i ^ p[0]), 0, 0))

        attn_shape = (replicas, share, 4 * width)
        mlp_shape = (2, replicas, share, hidden)
        attn_spec = pl.BlockSpec((1, share, 4 * width), lambda i, _, p: (i ^ p[0], 0, 0))
        mlp_spec = pl.BlockSpec((2, 1, share, hidden), lambda i, _, p: (0, i ^ p[0], 0, 0))
        updated = pl.pallas_call(
            functools.partial(adam_kernel, fc_rows),
            grid_spec=pltpu.PrefetchScalarGridSpec(
                num_scalar_prefetch=2,
                grid=(replicas,),
                in_specs=[gathered_spec(all_a), gathered_spec(all_b)]
                + [
                    pl.BlockSpec(q_block, lambda i, *_: (jnp.minimum(i, near_count - 1), 0, 0)),
                    pl.BlockSpec(q_block, lambda i, *_: (jnp.maximum(i - near_count, 0), 0, 0)),
                ]
                + [attn_spec] * 3
                + [mlp_spec] * 3,
                out_specs=[attn_spec] * 4 + [mlp_spec] * 4,
            ),
            out_shape=[jax.ShapeDtypeStruct(attn_shape, HIGH)] * 4
            + [jax.ShapeDtypeStruct(mlp_shape, HIGH)] * 4,
            compiler_params=params("arbitrary"),
            cost_estimate=cost(30 * 9 * rows * width, 54e6),
            name="adam",
        )(
            factor.reshape(1),
            turn.reshape(1).astype(jnp.int32),
            all_a,
            all_b,
            near_q,
            far_q,
            *[array.reshape(attn_shape) for array in (attn_w, attn_m, attn_v)],
            *[array.reshape(mlp_shape) for array in (mlp_w, mlp_m, mlp_v)],
        )
        attn_grad, attn_w_new, attn_m_new, attn_v_new = [u.reshape(attn_w.shape) for u in updated[:4]]
        mlp_grad, mlp_w_new, mlp_m_new, mlp_v_new = [u.reshape(mlp_w.shape) for u in updated[4:]]
        vec_grad, vec_w_new, vec_m_new, vec_v_new = adam_update(
            vec_w, vec_m, vec_v, summed_vec, factor, RATE_VECTOR, 0.0
        )
        return (
            block_out, grad_in, attn_grad, mlp_grad, vec_grad,
            attn_w_new, attn_m_new, attn_v_new, mlp_w_new, mlp_m_new, mlp_v_new,
            vec_w_new, vec_m_new, vec_v_new, norm_total.reshape(1),
        )

    return on_device


def solution(mesh):
    tokens = P(("dp", "shard"), None)
    groups = P("dp", None)
    attn = P("shard", None)
    mlp = P(None, "shard", None)
    vec = P(None, "shard")
    return jax.shard_map(
        make_on_device(mesh.shape["shard"], mesh.shape["dp"]),
        mesh=mesh,
        in_specs=(tokens, tokens, groups, groups) + (attn,) * 3 + (mlp,) * 3 + (vec,) * 3,
        out_specs=(tokens, tokens, attn, mlp, vec) + (attn,) * 3 + (mlp,) * 3 + (vec,) * 3 + (P(),),
        check_vma=False,
    )
```

```python
import functools

import jax
import jax.numpy as jnp
from jax import lax
from jax.experimental import pallas as pl
from jax.experimental.pallas import tpu as pltpu
from jax.sharding import PartitionSpec as P

HEADS = 12
STEP = 10
NORM_EPSILON = 1e-05
BETA_FIRST = 0.9
BETA_SECOND = 0.999
ADAM_EPSILON = 1e-08
RATE_MATRIX = 0.1
RATE_VECTOR = 0.2
DECAY_MATRIX = 0.1
CLIP_LIMIT = 1.0
MASKED_SCORE = -1e30
QUERY_BLOCK = 256
VMEM_LIMIT = 60 * 1024 * 1024
LOW = jnp.bfloat16
HIGH = jnp.float32


def dot_nn(a, b):
    return lax.dot_general(a, b, (((1,), (0,)), ((), ())), preferred_element_type=HIGH)


def dot_nt(a, b):
    return lax.dot_general(a, b, (((1,), (1,)), ((), ())), preferred_element_type=HIGH)


def low_t(a):
    return a.astype(HIGH).T.astype(LOW)


def normalize(features):
    centered = features - jnp.mean(features, axis=-1, keepdims=True)
    variance = jnp.mean(centered * centered, axis=-1, keepdims=True)
    inverse = lax.rsqrt(variance + NORM_EPSILON)
    return centered * inverse, inverse


def normalize_back(unit, inverse, grad_unit):
    first = jnp.mean(grad_unit, axis=-1, keepdims=True)
    second = jnp.mean(grad_unit * unit, axis=-1, keepdims=True)
    return inverse * (grad_unit - first - unit * second)


def cut_kernel(place, w_ref, vec_ref, *out_refs):
    parts = len(out_refs)
    rows, columns = w_ref.shape
    width = columns // 3
    cols = width // parts
    vec = vec_ref[...]
    tail = [
        jnp.concatenate([vec[3 * k + m : 3 * k + m + 1, :] for m in range(3)], axis=1)
        for k in range(vec.shape[0] // 3)
    ]
    tail.append(jnp.zeros((16 - len(tail), 3 * cols), HIGH))
    tail = jnp.concatenate(tail, axis=0).astype(LOW)
    for r in range(parts):
        starts = [k * width + r * cols for k in range(3)]
        piece = jnp.concatenate([w_ref[:, c : c + cols] for c in starts], axis=1).astype(LOW)
        for j in range(parts):

            @pl.when((place[0] ^ j) == r)
            def _():
                out_refs[j][:rows, :] = piece
                out_refs[j][rows:, :] = tail


def widen_kernel(half, out_ref, mlp_ref, wide_ref, *half_refs):
    rows, width = out_ref.shape
    start = pl.multiple_of(half[0] * (rows // 2), 16)
    near = pl.ds(start, rows // 2)
    sources = [(out_ref[...], out_ref[near, :])]
    for f in range(mlp_ref.shape[2] // width):
        span = slice(f * width, (f + 1) * width)
        sources += [(mlp_ref[n, :, span], mlp_ref[n, near, span]) for n in range(2)]
    split = half_refs[0].shape[1] // width
    for n, (block, part) in enumerate(sources):
        wide_ref[:, n * width : (n + 1) * width] = block.astype(LOW)
        k = int(n >= split)
        at = (n - k * split) * width
        half_refs[k][:, at : at + width] = part.astype(LOW)


def project_kernel(parts, place, *refs):
    x_refs, w_refs, refs = refs[:parts], refs[parts : 2 * parts], refs[2 * parts :]
    bias_ref, a1_ref, qkv_ref, wt_ref, vec_ref, w_scr, x_scr, sems = refs
    step = pl.program_id(0)
    rows = vec_ref.shape[1] // parts

    def copy(j):
        return pltpu.make_async_copy(x_refs[j], x_scr.at[j], sems.at[j])

    @pl.when(step == 0)
    def _():
        for j in range(parts):
            copy(j).start()
        vec_ref[...] = jnp.zeros_like(vec_ref)
        for j in range(parts):
            start = pl.multiple_of((place[0] ^ j) * rows, 16)
            w_scr[pl.ds(start, rows), :] = w_refs[j][:rows, :].astype(HIGH)
            tail = w_refs[j][rows:, :].astype(HIGH)
            for r in range(parts):

                @pl.when((place[0] ^ j) == r)
                def _():
                    for n in range(12):
                        piece = tail[n // 3 : n // 3 + 1, n % 3 * rows : (n % 3 + 1) * rows]
                        vec_ref[n : n + 1, r * rows : (r + 1) * rows] = piece

        wt_ref[...] = w_scr[...].T.astype(LOW)

    for j in range(parts):

        @pl.when(step == j)
        def _():
            copy(j).wait()

    unit, _ = normalize(x_scr[step].astype(HIGH))
    a1 = (unit * vec_ref[0:1, :] + vec_ref[1:2, :]).astype(LOW)
    a1_ref[...] = a1
    qkv_ref[...] = (dot_nt(wt_ref[...], a1) + bias_ref[...]).astype(LOW)


def masked_scores(q, kt, seg_q, seg_k, start):
    block = q.shape[0]
    out = []
    if start:
        s = dot_nn(q, kt[:, :start])
        out.append(jnp.where(seg_q == seg_k[:, :start], s, MASKED_SCORE))
    s = dot_nn(q, kt[:, start : start + block])
    row = lax.broadcasted_iota(jnp.int32, (block, block), 0)
    col = lax.broadcasted_iota(jnp.int32, (block, block), 1)
    allowed = (seg_q == seg_k[:, start : start + block]) & (col <= row)
    out.append(jnp.where(allowed, s, MASKED_SCORE))
    return out


def attend_kernel(scale, place, qt_ref, kt_ref, vt_ref, segc_ref, segr_ref, o_ref, lse_ref, v_scr):
    total = qt_ref.shape[1]
    per_part = o_ref.shape[2]
    block = min(QUERY_BLOCK, per_part)
    v_scr[...] = low_t(vt_ref[...])
    for start in range(0, total, block):
        span = slice(start, start + block)
        q = (qt_ref[:, span].astype(HIGH) * scale).T.astype(LOW)
        pieces = masked_scores(q, kt_ref, segc_ref[span, :], segr_ref, start)
        top = functools.reduce(jnp.maximum, [jnp.max(s, axis=1, keepdims=True) for s in pieces])
        weights = [jnp.exp(s - top) for s in pieces]
        mass = sum(jnp.sum(w, axis=1, keepdims=True) for w in weights)
        lse_ref[0, span, :] = top + jnp.log(mass)
        inverse = 1.0 / mass
        mixed = dot_nn((weights[-1] * inverse).astype(LOW), v_scr[span, :])
        if start:
            mixed += dot_nn((weights[0] * inverse).astype(LOW), v_scr[:start, :])
        inner = start % per_part
        o_ref[place[0] ^ (start // per_part), :, inner : inner + block] = mixed.T.astype(LOW)


def attend_back_kernel(
    scale, place, qt_ref, kt_ref, vt_ref, segc_ref, segr_ref, lse_ref, *refs
):
    *do_refs, out_ref, k_scr, do_scr, dk_scr, dv_scr = refs
    total = qt_ref.shape[1]
    parts, per_part = len(do_refs), do_refs[0].shape[1]
    block = min(QUERY_BLOCK, per_part)
    k_scr[...] = low_t(kt_ref[...])
    for j in range(parts):
        do_scr[place[0] ^ j] = do_refs[j][...]
    dk_scr[...] = jnp.zeros_like(dk_scr)
    dv_scr[...] = jnp.zeros_like(dv_scr)
    for start in range(0, total, block):
        span = slice(start, start + block)
        inner = start % per_part
        qt = qt_ref[:, span].astype(HIGH) * scale
        dot_ = do_scr[start // per_part, :, inner : inner + block]
        q = qt.T.astype(LOW)
        qt = qt.astype(LOW)
        do = low_t(dot_)
        pieces = masked_scores(q, kt_ref, segc_ref[span, :], segr_ref, start)
        spans = [slice(0, start), span] if start else [span]
        lse = lse_ref[0, span, :]
        weights = [jnp.exp(s - lse) for s in pieces]
        grads = [dot_nn(do, vt_ref[:, at]) for at in spans]
        delta = sum(jnp.sum(g * w, axis=1, keepdims=True) for g, w in zip(grads, weights))
        dq = None
        for at, w, g in zip(spans, weights, grads):
            ds = (w * (g - delta)).astype(LOW)
            term = dot_nn(ds, k_scr[at, :])
            dq = term if dq is None else dq + term
            dk_scr[:, at] += dot_nn(qt, ds)
            dv_scr[:, at] += dot_nn(dot_, w.astype(LOW))
        out_ref[0, :, span] = (dq * scale).T.astype(LOW)
    out_ref[1] = dk_scr[...].astype(LOW)
    out_ref[2] = dv_scr[...].astype(LOW)


def projection_back_kernel(heads, parts, place, half, *refs):
    x_refs, (a1_ref, *refs) = refs[:parts], refs[parts:]
    head_refs, refs = refs[:heads], refs[heads:]
    wt_ref, vec_ref, grads_ref, keep_ref, send_ref, qkeep_ref, qsend_ref, *scratch = refs
    g_scr, vec_scr, sums_scr, ext_scr, all_scr, x_scr, sems = scratch
    step = pl.program_id(0)
    cols = g_scr.shape[0] // 3
    extra = grads_ref.shape[0]
    count = qkeep_ref.shape[2] - 3 * cols

    def copy(j):
        return pltpu.make_async_copy(x_refs[j], x_scr.at[j], sems.at[j])

    @pl.when(step == 0)
    def _():
        for j in range(parts):
            copy(j).start()
        g_scr[...] = jnp.zeros_like(g_scr)
        vec_scr[...] = grads_ref[...]
        sums_scr[...] = jnp.zeros_like(sums_scr)

    for j in range(parts):

        @pl.when(step == j)
        def _():
            copy(j).wait()

    dqkv = jnp.concatenate([ref[k] for k in range(3) for ref in head_refs], axis=0)
    da1 = dot_nn(low_t(dqkv), wt_ref[...])

    @pl.when(step % 2 == 0)
    def _():
        keep_ref[0] = da1.astype(LOW)

    @pl.when(step % 2 == 1)
    def _():
        send_ref[0] = da1.astype(LOW)

    g_scr[...] += dot_nn(dqkv, a1_ref[...])
    unit, _ = normalize(x_scr[step].astype(HIGH))
    vec_scr[0:1, :] += jnp.sum(da1 * unit, axis=0, keepdims=True)
    vec_scr[1:2, :] += jnp.sum(da1, axis=0, keepdims=True)
    sums_scr[...] += jnp.sum(dqkv.astype(HIGH), axis=1, keepdims=True)

    @pl.when(step == pl.num_programs(0) - 1)
    def _():
        ext_scr[...] = vec_scr[...].T
        own = pl.ds(pl.multiple_of(place[0] * cols, 16), cols)
        ext_scr[own, 2:3] = sums_scr[:cols, :]
        ext_scr[own, 3:4] = sums_scr[2 * cols :, :]
        all_scr[:, : 3 * cols] = g_scr[...].T
        all_scr[:, 3 * cols : 3 * cols + extra] = ext_scr[...]
        rows = all_scr.shape[0] // parts
        for r in range(parts):
            for ref, side in ((qkeep_ref, half[0]), (qsend_ref, 1 - half[0])):
                start = pl.multiple_of(r * rows + side * (rows // 2), 16)
                ref[r] = all_scr[pl.ds(start, rows // 2), : 3 * cols + count].astype(LOW)


GELU_C = 0.7978845608028654
GELU_A = 0.044715


def mlp_kernel(
    parts, first_blocks, place, half, live_ref, x_ref, cot_ref, vec_ref, *refs
):
    o_refs, refs = refs[:parts], refs[parts:]
    own_ref, core_ref, *wide_refs = refs[:10]
    out_ref, *grad_refs = refs[10:15]
    dr1_ref, vecg_ref, *refs = refs[15:]
    do_refs, scratch = refs[:parts], refs[parts:]
    wide, ot_scr, r1_scr, a2_scr, a2t_scr, dy_scr, dyt_scr, y_scr, da2_scr, act_scr, sems = scratch
    step = pl.program_id(0)
    rows = o_refs[0].shape[0]
    slots, width = x_ref.shape
    bo, gain, shift, bp = (vec_ref[r : r + 1, :] for r in (4, 5, 6, 11))
    split = wide_refs[0].shape[1]
    live = lax.broadcasted_iota(jnp.int32, (slots, 1), 0) < live_ref[0]

    def copies(k):
        half_rows = rows // 2
        near, far = half[0] * half_rows, (1 - half[0]) * half_rows
        span = slice(0, split) if k == 0 else slice(split, wide.shape[1])
        sources = [(own_ref.at[:, span], 0, 0), (core_ref.at[:, span], 1, 0)]
        spots = [(2, near), (2, far), (3, near), (3, far)]
        sources += [(wide_refs[4 * k + n], *spot) for n, spot in enumerate(spots)]
        for n, (source, j, offset) in enumerate(sources):
            start = pl.multiple_of((place[0] ^ j) * rows + offset, 16)
            target = wide.at[pl.ds(start, source.shape[0]), span]
            yield pltpu.make_async_copy(source, target, sems.at[k, n])

    def block(n):
        return wide[:, pl.ds(pl.multiple_of(n * width, 128), width)]

    def permuted(scratch, value):
        for j in range(parts):
            scratch[j * rows : (j + 1) * rows, :] = value(pl.multiple_of((place[0] ^ j) * rows, 16))

    def put(value):
        value = value.astype(LOW)
        for k in range(2):

            @pl.when((step >= first_blocks) == bool(k))
            def _():
                keep, send = grad_refs[2 * k : 2 * k + 2]
                for j in range(parts):
                    (send if j % 2 else keep)[j // 2] = value[j * rows : (j + 1) * rows, :]

    @pl.when(step == 0)
    def _():
        for k in range(2):
            for copy in copies(k):
                copy.start()
        for j in range(parts):
            start = pl.multiple_of((place[0] ^ j) * rows, 16)
            ot_scr[pl.ds(start, rows), :] = o_refs[j][...]
        mixed = low_t(ot_scr[...])
        dy = jnp.where(live, cot_ref[...].astype(HIGH), 0.0)
        dy_scr[...] = dy.astype(LOW)
        ot_scr[...] = dy.T.astype(LOW)
        permuted(dyt_scr, lambda start: ot_scr[pl.ds(start, rows), :])
        for copy in copies(0):
            copy.wait()
        r1 = x_ref[...].astype(HIGH) + dot_nn(mixed, wide[:, :width]) + bo
        r1_scr[...] = r1
        unit, _ = normalize(r1)
        a2 = unit * gain + shift
        a2_scr[...] = a2.astype(LOW)
        ot_scr[...] = a2.T.astype(LOW)
        permuted(a2t_scr, lambda start: ot_scr[pl.ds(start, rows), :])
        vecg_ref[...] = jnp.zeros_like(vecg_ref)
        vecg_ref[11:12, :] = jnp.sum(dy, axis=0, keepdims=True)
        y_scr[...] = r1 + bp
        da2_scr[...] = jnp.zeros_like(da2_scr)

    @pl.when(step == first_blocks)
    def _():
        for copy in copies(1):
            copy.wait()

    last = pl.num_programs(0) - 1

    @pl.when((step < last) & (step % 2 == 0))
    def _():
        w_fc, w_pt = block(1 + step), block(2 + step)
        u = dot_nn(a2_scr[...], w_fc) + vec_ref[pl.ds(7 + step // 2, 1), :]
        square = u * u
        t = jnp.tanh(GELU_C * (u + GELU_A * (square * u)))
        grown = 0.5 * (1.0 + t)
        act = (u * grown).astype(LOW)
        act_scr[...] = act
        y_scr[...] += dot_nt(act, w_pt)
        slope = grown + 0.5 * u * (1.0 - t * t) * (GELU_C + (3.0 * GELU_C * GELU_A) * square)
        du = (dot_nn(dy_scr[...], w_pt) * slope).astype(LOW)
        vecg_ref[pl.ds(7 + step // 2, 1), :] = jnp.sum(du.astype(HIGH), axis=0, keepdims=True)
        da2_scr[...] += dot_nt(du, w_fc)
        put(dot_nn(a2t_scr[...], du))

    @pl.when((step < last) & (step % 2 == 1))
    def _():
        put(dot_nn(dyt_scr[...], act_scr[...]))

    @pl.when(step == last)
    def _():
        out_ref[...] = jnp.where(live, y_scr[...], 0.0).astype(LOW)
        unit, inverse = normalize(r1_scr[...])
        da2 = da2_scr[...]
        vecg_ref[5:6, :] = jnp.sum(da2 * unit, axis=0, keepdims=True)
        vecg_ref[6:7, :] = jnp.sum(da2, axis=0, keepdims=True)
        dr1 = dy_scr[...].astype(HIGH) + normalize_back(unit, inverse, da2 * gain)
        dr1_ref[...] = dr1
        low = dr1.astype(LOW)
        vecg_ref[4:5, :] = jnp.sum(low.astype(HIGH), axis=0, keepdims=True)
        put(dot_nn(jnp.concatenate([ref[...] for ref in o_refs], axis=0), low))
        for j in range(parts):
            start = pl.multiple_of((place[0] ^ j) * rows, 16)
            do_refs[j][...] = dot_nt(wide[pl.ds(start, rows), :width], low).astype(LOW)


def group_layout(length_row, count_row, slots):
    starts = jnp.cumsum(count_row) - count_row
    within = jnp.arange(slots, dtype=jnp.int32)
    position = (starts[:, None] + within[None, :]).reshape(-1)
    live_rows = (within[None, :] < count_row[:, None]).reshape(-1)
    boundary = jnp.cumsum(length_row)
    segment = jnp.sum((position[:, None] >= boundary[None, :]).astype(jnp.int32), axis=1)
    buffer_slot = jnp.arange(position.shape[0], dtype=jnp.int32)
    return jnp.where(live_rows, segment, -1 - buffer_slot)


def adam_update(master, first, second, gradient, factor, rate, decay):
    clipped = gradient * factor
    first_new = BETA_FIRST * first + (1.0 - BETA_FIRST) * clipped
    second_new = BETA_SECOND * second + (1.0 - BETA_SECOND) * clipped * clipped
    first_hat = first_new / (1.0 - BETA_FIRST**STEP)
    second_hat = second_new / (1.0 - BETA_SECOND**STEP)
    master_new = master - rate * (
        first_hat / (jnp.sqrt(second_hat) + ADAM_EPSILON) + decay * master
    )
    return (clipped, master_new, first_new, second_new)


def adam_kernel(fc_rows, factor_ref, _, *refs):
    grads, states, outs = refs[:5], refs[5:11], refs[11:]
    near = pl.program_id(0) < pl.num_programs(0) // 2
    first, second = grads[0][0], jnp.where(near, grads[1][0], grads[2][0])
    factor = factor_ref[0]
    width = outs[0].shape[-1] // fc_rows
    qkv = jnp.where(near, grads[3][0], grads[4][0])[:, : 3 * width]

    def update(gradient, at, base):
        results = adam_update(
            *[states[base + n][at] for n in range(3)],
            gradient.astype(HIGH), factor, RATE_MATRIX, DECAY_MATRIX,
        )
        for n, result in enumerate(results):
            outs[base // 3 * 4 + n][at] = result

    blocks = [first[:, n : n + width] for n in range(0, first.shape[1], width)]
    blocks += [second[:, n : n + width] for n in range(0, second.shape[1], width)]
    for f in range(fc_rows):
        span = slice(f * width, (f + 1) * width)
        for n in range(2):
            update(blocks[2 * f + n], (n, 0, slice(None), span), 3)
    update(qkv, (0, slice(None), slice(0, 3 * width)), 0)
    update(blocks[-1], (0, slice(None), slice(3 * width, 4 * width)), 0)


def swap(array, axis, bit, count):
    return lax.ppermute(array, axis, [(i, i ^ bit) for i in range(count)])


def pick(array, index):
    return lax.dynamic_index_in_dim(array, index, 0, keepdims=False)


def deal(pieces, parts):
    return list(pieces[:1]) + [swap(pieces[j], "shard", j, parts) for j in range(1, parts)]


def in_order(relative, place, parts):
    relative = jnp.stack(relative)
    return jnp.stack([pick(relative, place ^ r) for r in range(parts)])


def collect(own, parts):
    have = [own]
    bit = parts // 2
    slots = [0]
    while bit:
        have = have + [swap(piece, "shard", bit, parts) for piece in have]
        slots = slots + [s ^ bit for s in slots]
        bit //= 2
    return [have[slots.index(j)] for j in range(parts)]


def after(value, *others):
    return lax.optimization_barrier((value, *others))[0]


def add_low(a, b):
    return (a.astype(HIGH) + b.astype(HIGH)).astype(LOW)


def bits_of(count):
    return [1 << n for n in range(count.bit_length() - 1)]


def halve(array, upper, dim):
    length = array.shape[dim] // 2
    keep = lax.dynamic_slice_in_dim(array, upper * length, length, dim)
    return keep, lax.dynamic_slice_in_dim(array, (1 - upper) * length, length, dim)


def scatter_half(array, dim, bit, replica, replicas):
    keep, send = halve(array, (replica // bit) % 2, dim)
    return keep, swap(send, "dp", bit, replicas)


def params(*semantics):
    return pltpu.CompilerParams(dimension_semantics=semantics, vmem_limit_bytes=VMEM_LIMIT)


def cost(flops, moved, special=0):
    return pl.CostEstimate(flops=int(flops), bytes_accessed=int(moved), transcendentals=int(special))


def whole(*shape):
    zeros = (0,) * len(shape)
    return pl.BlockSpec(shape, lambda *_: zeros)


def make_on_device(parts, replicas):
    def on_device(
        tokens, cotangent, lengths, counts,
        attn_w, attn_m, attn_v, mlp_w, mlp_m, mlp_v, vec_w, vec_m, vec_v,
    ):
        slots, width = tokens.shape
        rows = attn_w.shape[0]
        hidden = mlp_w.shape[2]
        fc_rows = hidden // width
        total = parts * slots
        head_size = width // HEADS
        own_heads = HEADS // parts
        own_cols = own_heads * head_size
        scale = head_size ** (-0.5)
        place = lax.axis_index("shard")
        replica = lax.axis_index("dp")
        prefetch = place.reshape(1).astype(jnp.int32)

        half = replica % 2
        side = half.reshape(1).astype(jnp.int32)

        x_all = collect(tokens, parts)
        w_pieces = pl.pallas_call(
            cut_kernel,
            grid_spec=pltpu.PrefetchScalarGridSpec(
                num_scalar_prefetch=1,
                grid=(1,),
                in_specs=[whole(rows, 3 * width), whole(vec_w.shape[0], rows)],
                out_specs=[whole(rows + 16, 3 * own_cols)] * parts,
            ),
            out_shape=[jax.ShapeDtypeStruct((rows + 16, 3 * own_cols), LOW)] * parts,
            compiler_params=params("arbitrary"),
            cost_estimate=cost(0, 4e6),
            name="cut",
        )(prefetch, attn_w, vec_w)
        w_local = deal(w_pieces, parts)

        blocks = 2 * fc_rows + 1
        split = (fc_rows // 2 * 2 + 1) * width
        wide_own, *wide_half = pl.pallas_call(
            widen_kernel,
            grid_spec=pltpu.PrefetchScalarGridSpec(
                num_scalar_prefetch=1,
                grid=(1,),
                in_specs=[
                    pl.BlockSpec((rows, width), lambda *_: (0, 3)),
                    whole(2, rows, hidden),
                ],
                out_specs=[
                    whole(rows, blocks * width),
                    whole(rows // 2, split),
                    whole(rows // 2, blocks * width - split),
                ],
            ),
            out_shape=[
                jax.ShapeDtypeStruct((rows, blocks * width), LOW),
                jax.ShapeDtypeStruct((rows // 2, split), LOW),
                jax.ShapeDtypeStruct((rows // 2, blocks * width - split), LOW),
            ],
            compiler_params=params("arbitrary"),
            cost_estimate=cost(0, 12e6),
            name="widen",
        )(side, attn_w, mlp_w)
        wide_own, *wide_half = lax.optimization_barrier((wide_own, *wide_half, *w_local, *x_all))[:3]
        near = [swap(mine, "shard", parts // 2, parts) for mine in wide_half]
        wide_core = swap(wide_own, "shard", 1, parts)

        segment = group_layout(lengths[0], counts[0], slots)
        seg_col = segment[:, None]
        seg_row = segment[None, :]
        own_vec = vec_w.astype(LOW).astype(HIGH)
        bias_local = jnp.concatenate(
            [own_vec[2], jnp.zeros((own_cols,), HIGH), own_vec[3]]
        )[:, None]

        a1, qkv, w_t, vectors = pl.pallas_call(
            functools.partial(project_kernel, parts),
            grid_spec=pltpu.PrefetchScalarGridSpec(
                num_scalar_prefetch=1,
                grid=(parts,),
                in_specs=[
                    *[pl.BlockSpec(memory_space=pl.ANY)] * parts,
                    *[whole(rows + 16, 3 * own_cols)] * parts,
                    whole(3 * own_cols, 1),
                ],
                out_specs=[
                    pl.BlockSpec((slots, width), lambda i, p: (p[0] ^ i, 0)),
                    pl.BlockSpec((3 * own_cols, slots), lambda i, p: (0, p[0] ^ i)),
                    whole(3 * own_cols, width),
                    whole(16, width),
                ],
                scratch_shapes=[
                    pltpu.VMEM((width, 3 * own_cols), HIGH),
                    pltpu.VMEM((parts, slots, width), LOW),
                    pltpu.SemaphoreType.DMA((parts,)),
                ],
            ),
            out_shape=[
                jax.ShapeDtypeStruct((total, width), LOW),
                jax.ShapeDtypeStruct((3 * own_cols, total), LOW),
                jax.ShapeDtypeStruct((3 * own_cols, width), LOW),
                jax.ShapeDtypeStruct((16, width), HIGH),
            ],
            compiler_params=params("arbitrary"),
            cost_estimate=cost(2 * total * width * 3 * own_cols * 3, 12e6),
            name="project",
        )(prefetch, *x_all, *w_local, bias_local)

        pair_flops = 2 * total * total * head_size * 4 // 2

        def head_specs(h):
            return [
                pl.BlockSpec((head_size, total), functools.partial(lambda k, *_: (k * own_heads + h, 0), k))
                for k in range(3)
            ]

        def attend(h, qkv):
            return pl.pallas_call(
                functools.partial(attend_kernel, scale),
                grid_spec=pltpu.PrefetchScalarGridSpec(
                    num_scalar_prefetch=1,
                    grid=(1,),
                    in_specs=head_specs(h) + [whole(total, 1), whole(1, total)],
                    out_specs=[whole(parts, head_size, slots), whole(1, total, 1)],
                    scratch_shapes=[pltpu.VMEM((total, head_size), LOW)],
                ),
                out_shape=[
                    jax.ShapeDtypeStruct((parts, head_size, slots), LOW),
                    jax.ShapeDtypeStruct((1, total, 1), HIGH),
                ],
                compiler_params=params("arbitrary"),
                cost_estimate=cost(2 * pair_flops, 4e6, total * total // 2),
                name="attend",
            )(prefetch, qkv, qkv, qkv, seg_col, seg_row)

        mixed, lse = [], []
        for h in range(own_heads):
            if h == 1:
                qkv, near[0] = lax.optimization_barrier((qkv, near[0]))
                far = [swap(near[0], "dp", 1, replicas)]
                turned = [swap(near[0], "shard", 1, parts)]
            head_mixed, head_lse = attend(h, qkv)
            mixed.append(head_mixed)
            lse.append(head_lse)
        near[1] = after(near[1], mixed[-1])
        far.append(swap(near[1], "dp", 1, replicas))
        mixed_own = deal(
            [jnp.concatenate([head[j] for head in mixed], axis=0) for j in range(parts)], parts
        )
        turned.append(swap(near[1], "shard", 1, parts))
        wide = [wide_own, wide_core]
        for k in range(2):
            wide += [near[k], far[k], turned[k], swap(far[k], "shard", 1, parts)]

        steps = blocks
        live_own = lax.dynamic_index_in_dim(counts[0], place, 0, keepdims=True)
        first_blocks = fc_rows // 2 * 2

        def grad_spec(k):
            first, last = ((0, first_blocks - 1), (first_blocks, steps - 1))[k]
            return pl.BlockSpec(
                (parts // 2, rows, width), lambda i, *_: (0, 0, jnp.clip(i, first, last) - first)
            )

        grad_columns = [first_blocks * width, (steps - first_blocks) * width]

        in_hbm = pl.BlockSpec(memory_space=pltpu.HBM)
        out = pl.pallas_call(
            functools.partial(mlp_kernel, parts, first_blocks),
            grid_spec=pltpu.PrefetchScalarGridSpec(
                num_scalar_prefetch=3,
                grid=(steps,),
                in_specs=[whole(slots, width), whole(slots, width), whole(16, width)]
                + [whole(own_cols, slots)] * parts
                + [in_hbm] * len(wide),
                out_specs=[whole(slots, width)]
                + [grad_spec(k) for k in range(2) for _ in range(2)]
                + [whole(slots, width), whole(16, width)]
                + [whole(own_cols, slots)] * parts,
                scratch_shapes=[
                    pltpu.VMEM((width, blocks * width), LOW),
                    pltpu.VMEM((width, slots), LOW),
                    pltpu.VMEM((slots, width), HIGH),
                    pltpu.VMEM((slots, width), LOW),
                    pltpu.VMEM((width, slots), LOW),
                    pltpu.VMEM((slots, width), LOW),
                    pltpu.VMEM((width, slots), LOW),
                    pltpu.VMEM((slots, width), HIGH),
                    pltpu.VMEM((slots, width), HIGH),
                    pltpu.VMEM((slots, width), LOW),
                    pltpu.SemaphoreType.DMA((2, 6)),
                ],
            ),
            out_shape=[jax.ShapeDtypeStruct((slots, width), LOW)]
            + [jax.ShapeDtypeStruct((parts // 2, rows, c), LOW) for c in grad_columns for _ in range(2)]
            + [jax.ShapeDtypeStruct((slots, width), HIGH), jax.ShapeDtypeStruct((16, width), HIGH)]
            + [jax.ShapeDtypeStruct((own_cols, slots), LOW)] * parts,
            compiler_params=params("arbitrary"),
            cost_estimate=cost(2 * slots * width * (6 * hidden + 3 * width), 30e6, slots * hidden),
            name="mlp",
        )(prefetch, side, live_own, tokens, cotangent, vectors, *mixed_own, *wide)
        block_out, keep_a, send_a, keep_b, send_b, grad_resid, mid_grads, *do_pieces = out

        do_own = deal(do_pieces, parts)
        got_a = swap(send_a, "shard", 1, parts)
        got_b = swap(send_b, "shard", 1, parts)
        own_a, other_a = [add_low(keep_a[n], got_a[n]) for n in range(2)]
        own_b, other_b = halve(add_low(keep_b, got_b), half, 1)
        *do_own, own_a, other_a, own_b, other_b = lax.optimization_barrier(
            (*do_own, own_a, other_a, own_b, other_b)
        )
        got_a = swap(other_a, "shard", parts // 2, parts)
        got_b = swap(other_b, "dp", 1, replicas)

        def attend_back(h, qkv):
            return pl.pallas_call(
                functools.partial(attend_back_kernel, scale),
                grid_spec=pltpu.PrefetchScalarGridSpec(
                    num_scalar_prefetch=1,
                    grid=(1,),
                    in_specs=head_specs(h)
                    + [whole(total, 1), whole(1, total), whole(1, total, 1)]
                    + [pl.BlockSpec((head_size, slots), lambda *_: (h, 0))] * parts,
                    out_specs=whole(3, head_size, total),
                    scratch_shapes=[
                        pltpu.VMEM((total, head_size), LOW),
                        pltpu.VMEM((parts, head_size, slots), LOW),
                        pltpu.VMEM((head_size, total), HIGH),
                        pltpu.VMEM((head_size, total), HIGH),
                    ],
                ),
                out_shape=jax.ShapeDtypeStruct((3, head_size, total), LOW),
                compiler_params=params("arbitrary"),
                cost_estimate=cost(
                    5 * pair_flops, 4e6, total * total // 2
                ),
                name="attend_back",
            )(prefetch, qkv, qkv, qkv, seg_col, seg_row, lse[h], *do_own)

        dqkv = [attend_back(h, qkv) for h in range(own_heads)]
        *dqkv, got_a = lax.optimization_barrier((*dqkv, got_a))
        own_a, other_a = halve(add_low(own_a, got_a), half, 0)
        dqkv[0] = after(dqkv[0], other_a)
        got_a = swap(other_a, "dp", 1, replicas)

        q_cols = 3 * own_cols
        extra = vec_w.shape[0]
        half_rows = rows // 2
        da1_keep, da1_send, own_q, other_q = pl.pallas_call(
            functools.partial(projection_back_kernel, own_heads, parts),
            grid_spec=pltpu.PrefetchScalarGridSpec(
                num_scalar_prefetch=2,
                grid=(parts,),
                in_specs=[
                    *[pl.BlockSpec(memory_space=pl.ANY)] * parts,
                    pl.BlockSpec((slots, width), lambda i, p, _: (p[0] ^ i, 0)),
                ]
                + [pl.BlockSpec((3, head_size, slots), lambda i, p, _: (0, 0, p[0] ^ i))] * own_heads
                + [whole(q_cols, width), whole(16, width), whole(16, width)],
                out_specs=[pl.BlockSpec((1, slots, width), lambda i, *_: (i // 2, 0, 0))] * 2
                + [whole(parts, half_rows, q_cols + extra)] * 2,
                scratch_shapes=[
                    pltpu.VMEM((q_cols, width), HIGH),
                    pltpu.VMEM((16, width), HIGH),
                    pltpu.VMEM((q_cols, 1), HIGH),
                    pltpu.VMEM((width, 16), HIGH),
                    pltpu.VMEM((width, q_cols + 64), HIGH),
                    pltpu.VMEM((parts, slots, width), LOW),
                    pltpu.SemaphoreType.DMA((parts,)),
                ],
            ),
            out_shape=[jax.ShapeDtypeStruct((parts // 2, slots, width), LOW)] * 2
            + [jax.ShapeDtypeStruct((parts, half_rows, q_cols + extra), LOW)] * 2,
            compiler_params=params("arbitrary"),
            cost_estimate=cost(4 * total * width * 3 * own_cols * 2, 16e6),
            name="projection_back",
        )(prefetch, side, *x_all, a1, *dqkv, w_t, vectors, mid_grads)

        share = rows // replicas
        z_bits = [bit for bit in (1 << n for n in range(1, 20)) if bit < replicas]
        tokens_seen = [own_q]

        def seen(*values):
            *values, _ = lax.optimization_barrier((*values, tokens_seen[-1]))
            return values[0] if len(values) == 1 else values

        def event(value):
            tokens_seen.append(value)
            return value

        def scatter_on(name, keep, got, bit):
            array = event(add_low(keep, seen(got)))
            return scatter_half(array, {"q": 1}.get(name, 0), bit, replica, replicas)

        last_bit = z_bits[-1]

        def scatter_rest(name, state):
            for bit in z_bits[1:]:
                state = scatter_on(name, *state, bit)
            return state

        got_q = swap(other_q, "dp", 1, replicas)
        sum_b = event(add_low(own_b, seen(got_b)))
        got_b = swap(sum_b[1], "shard", parts // 2, parts)
        da1_got = swap(da1_send, "shard", 1, parts)
        state_a = scatter_on("a", own_a, got_a, z_bits[0])
        state_a = scatter_rest("a", state_a)
        state_q = scatter_on("q", own_q, got_q, z_bits[0])
        state_b = scatter_on("b", sum_b[0], got_b, z_bits[0])
        part_a = event(add_low(state_a[0], seen(state_a[1])))
        all_a = lax.all_gather(part_a, "dp", axis=0)
        state_q = scatter_rest("q", state_q)
        state_b = scatter_rest("b", state_b)
        part_q = event(add_low(state_q[0], seen(state_q[1])))

        main = part_q[:, :, :q_cols]
        vec_parts = part_q[:, :, q_cols:].transpose(1, 0, 2).reshape(1, share, parts * extra)
        vec_parts = jnp.broadcast_to(vec_parts, (parts,) + vec_parts.shape[1:])
        pieces = jnp.concatenate([main, vec_parts], axis=2)
        dealt = deal([pick(pieces, place ^ j) for j in range(parts)], parts)
        dealt = in_order(seen(*dealt), place, parts)
        q_rows = (
            dealt[:, :, :q_cols]
            .reshape(parts, share, 3, own_cols)
            .transpose(1, 2, 0, 3)
            .reshape(share, 3 * width)
        )
        vec_parts = jnp.sum(dealt[:, :, q_cols:].astype(HIGH), axis=0).astype(LOW)
        vec_own = lax.dynamic_index_in_dim(
            vec_parts.reshape(share, parts, extra), place, 1, keepdims=False
        )
        near_q = event(jnp.concatenate([q_rows, vec_own], axis=1)[None])
        got_q = swap(near_q, "dp", last_bit, replicas)
        near_b = event(add_low(state_b[0], seen(state_b[1])))[None]
        got_b = swap(near_b, "dp", last_bit, replicas)
        squares = sum(jnp.sum(jnp.square(p.astype(HIGH))) for p in (part_a, near_b, main))
        squares += jnp.where(place == 0, jnp.sum(jnp.square(vec_parts.astype(HIGH))), 0.0)
        squares = squares.reshape(1, 1)
        hops = [("shard", bit, parts) for bit in (1 << n for n in range(20)) if bit < parts]
        hops += [("dp", bit, replicas) for bit in (1 << n for n in range(20)) if bit < replicas]
        hops = iter(hops)
        pending = swap(squares, *next(hops))

        def norm_hop():
            nonlocal squares, pending
            if pending is None:
                return
            squares = event(squares + seen(pending))
            hop = next(hops, None)
            pending = None if hop is None else swap(squares, *hop)

        for bit in z_bits[-2::-1] + [1]:
            near_q = event(jnp.concatenate([near_q, seen(got_q)], axis=0))
            got_q = swap(near_q, "dp", bit, replicas)
            near_b = event(jnp.concatenate([near_b, seen(got_b)], axis=0))
            got_b = swap(near_b, "dp", bit, replicas)
            norm_hop()
        while pending is not None:
            norm_hop()
        far_q, far_b = seen(got_q, got_b)

        def block_of(index):
            block = index % 2
            for bit in z_bits:
                block = block * 2 + index // bit % 2
            return block

        def index_of(block):
            index = 0
            for bit in z_bits[::-1]:
                index = index + block % 2 * bit
                block = block // 2
            return index + block

        turn = block_of(replica)
        small = jnp.concatenate([near_q[:, :, 3 * width :], far_q[:, :, 3 * width :]], axis=0)
        small = jnp.stack([pick(small, turn ^ r) for r in range(replicas)]).astype(HIGH)
        summed_vec = small[:, :, :extra].reshape(rows, extra).T

        own_da1 = da1_keep[0].astype(HIGH) + da1_got[0].astype(HIGH)
        da1 = own_da1 + swap(add_low(da1_keep[1], da1_got[1]), "shard", 2, parts).astype(HIGH)
        unit, inverse = normalize(tokens.astype(HIGH))
        grad_input = grad_resid + normalize_back(unit, inverse, da1 * vectors[0:1])
        live_rows = jnp.arange(slots, dtype=jnp.int32) < live_own[0]
        grad_in = jnp.where(live_rows[:, None], grad_input, 0.0).astype(LOW)

        norm_total = jnp.sqrt(squares[0, 0])
        factor = jnp.minimum(1.0, CLIP_LIMIT / (norm_total + 1e-06))
        near_count = replicas // 2
        def near_spec(array):
            block = (1,) + array.shape[1:]
            return pl.BlockSpec(block, lambda i, *_: (jnp.minimum(i, near_count - 1), 0, 0))

        def far_spec(array):
            block = (1,) + array.shape[1:]
            return pl.BlockSpec(block, lambda i, *_: (jnp.maximum(i - near_count, 0), 0, 0))

        def gathered_spec(array):
            return pl.BlockSpec((1,) + array.shape[1:], lambda i, _, p: (index_of(i ^ p[0]), 0, 0))

        attn_shape = (replicas, share, 4 * width)
        mlp_shape = (2, replicas, share, hidden)
        attn_spec = pl.BlockSpec((1, share, 4 * width), lambda i, _, p: (i ^ p[0], 0, 0))
        mlp_spec = pl.BlockSpec((2, 1, share, hidden), lambda i, _, p: (0, i ^ p[0], 0, 0))
        updated = pl.pallas_call(
            functools.partial(adam_kernel, fc_rows),
            grid_spec=pltpu.PrefetchScalarGridSpec(
                num_scalar_prefetch=2,
                grid=(replicas,),
                in_specs=[gathered_spec(all_a)]
                + [near_spec(near_b), far_spec(far_b), near_spec(near_q), far_spec(far_q)]
                + [attn_spec] * 3
                + [mlp_spec] * 3,
                out_specs=[attn_spec] * 4 + [mlp_spec] * 4,
            ),
            out_shape=[jax.ShapeDtypeStruct(attn_shape, HIGH)] * 4
            + [jax.ShapeDtypeStruct(mlp_shape, HIGH)] * 4,
            compiler_params=params("arbitrary"),
            cost_estimate=cost(30 * 9 * rows * width, 54e6),
            name="adam",
        )(
            factor.reshape(1),
            turn.reshape(1).astype(jnp.int32),
            all_a,
            near_b,
            far_b,
            near_q,
            far_q,
            *[array.reshape(attn_shape) for array in (attn_w, attn_m, attn_v)],
            *[array.reshape(mlp_shape) for array in (mlp_w, mlp_m, mlp_v)],
        )
        attn_grad, attn_w_new, attn_m_new, attn_v_new = [u.reshape(attn_w.shape) for u in updated[:4]]
        mlp_grad, mlp_w_new, mlp_m_new, mlp_v_new = [u.reshape(mlp_w.shape) for u in updated[4:]]
        vec_grad, vec_w_new, vec_m_new, vec_v_new = adam_update(
            vec_w, vec_m, vec_v, summed_vec, factor, RATE_VECTOR, 0.0
        )
        return (
            block_out, grad_in, attn_grad, mlp_grad, vec_grad,
            attn_w_new, attn_m_new, attn_v_new, mlp_w_new, mlp_m_new, mlp_v_new,
            vec_w_new, vec_m_new, vec_v_new, norm_total.reshape(1),
        )

    return on_device


def solution(mesh):
    tokens = P(("dp", "shard"), None)
    groups = P("dp", None)
    attn = P("shard", None)
    mlp = P(None, "shard", None)
    vec = P(None, "shard")
    return jax.shard_map(
        make_on_device(mesh.shape["shard"], mesh.shape["dp"]),
        mesh=mesh,
        in_specs=(tokens, tokens, groups, groups) + (attn,) * 3 + (mlp,) * 3 + (vec,) * 3,
        out_specs=(tokens, tokens, attn, mlp, vec) + (attn,) * 3 + (mlp,) * 3 + (vec,) * 3 + (P(),),
        check_vma=False,
    )
```

```python
import functools

import jax
import jax.numpy as jnp
from jax import lax
from jax.experimental import pallas as pl
from jax.experimental.pallas import tpu as pltpu
from jax.sharding import PartitionSpec as P

HEADS = 12
STEP = 10
NORM_EPSILON = 1e-05
BETA_FIRST = 0.9
BETA_SECOND = 0.999
ADAM_EPSILON = 1e-08
RATE_MATRIX = 0.1
RATE_VECTOR = 0.2
DECAY_MATRIX = 0.1
CLIP_LIMIT = 1.0
MASKED_SCORE = -1e30
QUERY_BLOCK = 256
VMEM_LIMIT = 50 * 1024 * 1024
LOW = jnp.bfloat16
HIGH = jnp.float32


def dot_nn(a, b):
    return lax.dot_general(a, b, (((1,), (0,)), ((), ())), preferred_element_type=HIGH)


def dot_nt(a, b):
    return lax.dot_general(a, b, (((1,), (1,)), ((), ())), preferred_element_type=HIGH)


def low_t(a):
    return a.astype(HIGH).T.astype(LOW)


def normalize(features):
    centered = features - jnp.mean(features, axis=-1, keepdims=True)
    variance = jnp.mean(centered * centered, axis=-1, keepdims=True)
    inverse = lax.rsqrt(variance + NORM_EPSILON)
    return centered * inverse, inverse


def normalize_back(unit, inverse, grad_unit):
    first = jnp.mean(grad_unit, axis=-1, keepdims=True)
    second = jnp.mean(grad_unit * unit, axis=-1, keepdims=True)
    return inverse * (grad_unit - first - unit * second)


def cut_kernel(place, w_ref, vec_ref, *out_refs):
    parts = len(out_refs)
    rows, columns = w_ref.shape
    width = columns // 3
    cols = width // parts
    vec = vec_ref[...]
    tail = [
        jnp.concatenate([vec[3 * k + m : 3 * k + m + 1, :] for m in range(3)], axis=1)
        for k in range(vec.shape[0] // 3)
    ]
    tail.append(jnp.zeros((16 - len(tail), 3 * cols), HIGH))
    tail = jnp.concatenate(tail, axis=0).astype(LOW)
    for r in range(parts):
        starts = [k * width + r * cols for k in range(3)]
        piece = jnp.concatenate([w_ref[:, c : c + cols] for c in starts], axis=1).astype(LOW)
        for j in range(parts):

            @pl.when((place[0] ^ j) == r)
            def _():
                out_refs[j][:rows, :] = piece
                out_refs[j][rows:, :] = tail


def widen_kernel(half, out_ref, mlp_ref, wide_ref, *half_refs):
    rows, width = out_ref.shape
    start = pl.multiple_of(half[0] * (rows // 2), 16)
    near = pl.ds(start, rows // 2)
    sources = [(out_ref[...], out_ref[near, :])]
    for f in range(mlp_ref.shape[2] // width):
        span = slice(f * width, (f + 1) * width)
        sources += [(mlp_ref[n, :, span], mlp_ref[n, near, span]) for n in range(2)]
    split = half_refs[0].shape[1] // width
    for n, (block, part) in enumerate(sources):
        wide_ref[:, n * width : (n + 1) * width] = block.astype(LOW)
        k = int(n >= split)
        at = (n - k * split) * width
        half_refs[k][:, at : at + width] = part.astype(LOW)


def project_kernel(parts, place, *refs):
    x_refs, w_refs, refs = refs[:parts], refs[parts : 2 * parts], refs[2 * parts :]
    bias_ref, a1_ref, qkv_ref, wt_ref, vec_ref, w_scr, x_scr, sems = refs
    step = pl.program_id(0)
    rows = vec_ref.shape[1] // parts

    def copy(j):
        return pltpu.make_async_copy(x_refs[j], x_scr.at[j], sems.at[j])

    @pl.when(step == 0)
    def _():
        for j in range(parts):
            copy(j).start()
        vec_ref[...] = jnp.zeros_like(vec_ref)
        for j in range(parts):
            start = pl.multiple_of((place[0] ^ j) * rows, 16)
            w_scr[pl.ds(start, rows), :] = w_refs[j][:rows, :].astype(HIGH)
            tail = w_refs[j][rows:, :].astype(HIGH)
            for r in range(parts):

                @pl.when((place[0] ^ j) == r)
                def _():
                    for n in range(12):
                        piece = tail[n // 3 : n // 3 + 1, n % 3 * rows : (n % 3 + 1) * rows]
                        vec_ref[n : n + 1, r * rows : (r + 1) * rows] = piece

        wt_ref[...] = w_scr[...].T.astype(LOW)

    for j in range(parts):

        @pl.when(step == j)
        def _():
            copy(j).wait()

    unit, _ = normalize(x_scr[step].astype(HIGH))
    a1 = (unit * vec_ref[0:1, :] + vec_ref[1:2, :]).astype(LOW)
    a1_ref[...] = a1
    qkv_ref[...] = (dot_nt(wt_ref[...], a1) + bias_ref[...]).astype(LOW)


def masked_scores(q, kt, seg_q, seg_k, start):
    block = q.shape[0]
    out = []
    if start:
        s = dot_nn(q, kt[:, :start])
        out.append(jnp.where(seg_q == seg_k[:, :start], s, MASKED_SCORE))
    s = dot_nn(q, kt[:, start : start + block])
    row = lax.broadcasted_iota(jnp.int32, (block, block), 0)
    col = lax.broadcasted_iota(jnp.int32, (block, block), 1)
    allowed = (seg_q == seg_k[:, start : start + block]) & (col <= row)
    out.append(jnp.where(allowed, s, MASKED_SCORE))
    return out


def attend_kernel(scale, place, qt_ref, kt_ref, vt_ref, segc_ref, segr_ref, o_ref, lse_ref, v_scr):
    total = qt_ref.shape[1]
    per_part = o_ref.shape[2]
    block = min(QUERY_BLOCK, per_part)
    v_scr[...] = low_t(vt_ref[...])
    for start in range(0, total, block):
        span = slice(start, start + block)
        q = (qt_ref[:, span].astype(HIGH) * scale).T.astype(LOW)
        pieces = masked_scores(q, kt_ref, segc_ref[span, :], segr_ref, start)
        top = functools.reduce(jnp.maximum, [jnp.max(s, axis=1, keepdims=True) for s in pieces])
        weights = [jnp.exp(s - top) for s in pieces]
        mass = sum(jnp.sum(w, axis=1, keepdims=True) for w in weights)
        lse_ref[0, span, :] = top + jnp.log(mass)
        inverse = 1.0 / mass
        mixed = dot_nn((weights[-1] * inverse).astype(LOW), v_scr[span, :])
        if start:
            mixed += dot_nn((weights[0] * inverse).astype(LOW), v_scr[:start, :])
        inner = start % per_part
        o_ref[place[0] ^ (start // per_part), :, inner : inner + block] = mixed.T.astype(LOW)


def attend_back_kernel(
    scale, place, qt_ref, kt_ref, vt_ref, segc_ref, segr_ref, lse_ref, *refs
):
    *do_refs, out_ref, k_scr, do_scr, dk_scr, dv_scr = refs
    total = qt_ref.shape[1]
    parts, per_part = len(do_refs), do_refs[0].shape[1]
    block = min(QUERY_BLOCK, per_part)
    k_scr[...] = low_t(kt_ref[...])
    for j in range(parts):
        do_scr[place[0] ^ j] = do_refs[j][...]
    dk_scr[...] = jnp.zeros_like(dk_scr)
    dv_scr[...] = jnp.zeros_like(dv_scr)
    for start in range(0, total, block):
        span = slice(start, start + block)
        inner = start % per_part
        qt = qt_ref[:, span].astype(HIGH) * scale
        dot_ = do_scr[start // per_part, :, inner : inner + block]
        q = qt.T.astype(LOW)
        qt = qt.astype(LOW)
        do = low_t(dot_)
        pieces = masked_scores(q, kt_ref, segc_ref[span, :], segr_ref, start)
        spans = [slice(0, start), span] if start else [span]
        lse = lse_ref[0, span, :]
        weights = [jnp.exp(s - lse) for s in pieces]
        grads = [dot_nn(do, vt_ref[:, at]) for at in spans]
        delta = sum(jnp.sum(g * w, axis=1, keepdims=True) for g, w in zip(grads, weights))
        dq = None
        for at, w, g in zip(spans, weights, grads):
            ds = (w * (g - delta)).astype(LOW)
            term = dot_nn(ds, k_scr[at, :])
            dq = term if dq is None else dq + term
            dk_scr[:, at] += dot_nn(qt, ds)
            dv_scr[:, at] += dot_nn(dot_, w.astype(LOW))
        out_ref[0, :, span] = (dq * scale).T.astype(LOW)
    out_ref[1] = dk_scr[...].astype(LOW)
    out_ref[2] = dv_scr[...].astype(LOW)


def projection_back_kernel(heads, parts, place, half, *refs):
    x_refs, (a1_ref, *refs) = refs[:parts], refs[parts:]
    head_refs, refs = refs[:heads], refs[heads:]
    wt_ref, vec_ref, grads_ref, keep_ref, send_ref, qkeep_ref, qsend_ref, *scratch = refs
    g_scr, vec_scr, sums_scr, ext_scr, all_scr, x_scr, sems = scratch
    step = pl.program_id(0)
    cols = g_scr.shape[0] // 3
    extra = grads_ref.shape[0]
    count = qkeep_ref.shape[2] - 3 * cols

    def copy(j):
        return pltpu.make_async_copy(x_refs[j], x_scr.at[j], sems.at[j])

    @pl.when(step == 0)
    def _():
        for j in range(parts):
            copy(j).start()
        g_scr[...] = jnp.zeros_like(g_scr)
        vec_scr[...] = grads_ref[...]
        sums_scr[...] = jnp.zeros_like(sums_scr)

    for j in range(parts):

        @pl.when(step == j)
        def _():
            copy(j).wait()

    dqkv = jnp.concatenate([ref[k] for k in range(3) for ref in head_refs], axis=0)
    da1 = dot_nn(low_t(dqkv), wt_ref[...])

    @pl.when(step % 2 == 0)
    def _():
        keep_ref[0] = da1.astype(LOW)

    @pl.when(step % 2 == 1)
    def _():
        send_ref[0] = da1.astype(LOW)

    g_scr[...] += dot_nn(dqkv, a1_ref[...])
    unit, _ = normalize(x_scr[step].astype(HIGH))
    vec_scr[0:1, :] += jnp.sum(da1 * unit, axis=0, keepdims=True)
    vec_scr[1:2, :] += jnp.sum(da1, axis=0, keepdims=True)
    sums_scr[...] += jnp.sum(dqkv.astype(HIGH), axis=1, keepdims=True)

    @pl.when(step == pl.num_programs(0) - 1)
    def _():
        ext_scr[...] = vec_scr[...].T
        own = pl.ds(pl.multiple_of(place[0] * cols, 16), cols)
        ext_scr[own, 2:3] = sums_scr[:cols, :]
        ext_scr[own, 3:4] = sums_scr[2 * cols :, :]
        all_scr[:, : 3 * cols] = g_scr[...].T
        all_scr[:, 3 * cols : 3 * cols + extra] = ext_scr[...]
        rows = all_scr.shape[0] // parts
        for r in range(parts):
            for ref, side in ((qkeep_ref, half[0]), (qsend_ref, 1 - half[0])):
                start = pl.multiple_of(r * rows + side * (rows // 2), 16)
                ref[r] = all_scr[pl.ds(start, rows // 2), : 3 * cols + count].astype(LOW)


GELU_C = 0.7978845608028654
GELU_A = 0.044715


def weight_copies(place, half, sources, wide, span, offset, sems):
    rows = sources[0].shape[0]
    near, far = half[0] * (rows // 2), (1 - half[0]) * (rows // 2)
    spots = [(0, 0), (1, 0), (2, near), (2, far), (3, near), (3, far)]
    for n, ((j, inner), source) in enumerate(zip(spots, sources)):
        base = offset if n < 2 else 0
        start = pl.multiple_of((place[0] ^ j) * rows + inner, 16)
        source = source.at[:, base + span[0] : base + span[1]]
        target = wide.at[pl.ds(start, source.shape[0]), span[0] : span[1]]
        yield pltpu.make_async_copy(source, target, sems.at[n])


def put(keep, send, value):
    parts = 2 * keep.shape[0]
    rows = value.shape[0] // parts
    value = value.astype(LOW)
    for j in range(parts):
        (send if j % 2 else keep)[j // 2] = value[j * rows : (j + 1) * rows, :]


def mlp_chunk(a2, a2t, dy, w_fc, w_pt, bias, y_ref, da2_ref, act_scr, keep, send):
    u = dot_nn(a2[...], w_fc) + bias
    square = u * u
    t = jnp.tanh(GELU_C * (u + GELU_A * (square * u)))
    grown = 0.5 * (1.0 + t)
    act = (u * grown).astype(LOW)
    act_scr[...] = act
    y_ref[...] += dot_nt(act, w_pt)
    slope = grown + 0.5 * u * (1.0 - t * t) * (GELU_C + (3.0 * GELU_C * GELU_A) * square)
    du = (dot_nn(dy[...], w_pt) * slope).astype(LOW)
    da2_ref[...] += dot_nt(du, w_fc)
    put(keep, send, dot_nn(a2t[...], du))
    return jnp.sum(du.astype(HIGH), axis=0, keepdims=True)


def mlp_first_kernel(parts, place, half, live_ref, x_ref, cot_ref, vec_ref, *refs):
    o_refs, sources, refs = refs[:parts], refs[parts : parts + 6], refs[parts + 6 :]
    keep, send, r1_ref, a2_ref, a2t_ref, dy_ref, dyt_ref, y_ref, da2_ref, wout_ref, vecg_ref = refs[:11]
    wide, ot_scr, act_scr, sems = refs[11:]
    step = pl.program_id(0)
    rows = o_refs[0].shape[0]
    slots, width = x_ref.shape
    bo, gain, shift, bp = (vec_ref[r : r + 1, :] for r in (4, 5, 6, 11))

    def copies(k):
        span = ((0, width), (width, wide.shape[1]))[k]
        return weight_copies(place, half, sources, wide, span, 0, sems.at[k])

    def permuted(ref):
        for j in range(parts):
            start = pl.multiple_of((place[0] ^ j) * rows, 16)
            ref[j * rows : (j + 1) * rows, :] = ot_scr[pl.ds(start, rows), :]

    @pl.when(step == 0)
    def _():
        for k in range(2):
            for copy in copies(k):
                copy.start()
        for j in range(parts):
            start = pl.multiple_of((place[0] ^ j) * rows, 16)
            ot_scr[pl.ds(start, rows), :] = o_refs[j][...]
        mixed = low_t(ot_scr[...])
        live = lax.broadcasted_iota(jnp.int32, (slots, 1), 0) < live_ref[0]
        dy = jnp.where(live, cot_ref[...].astype(HIGH), 0.0)
        dy_ref[...] = dy.astype(LOW)
        ot_scr[...] = dy.T.astype(LOW)
        permuted(dyt_ref)
        for copy in copies(0):
            copy.wait()
        w_out = wide[:, :width]
        wout_ref[...] = w_out
        r1 = x_ref[...].astype(HIGH) + dot_nn(mixed, w_out) + bo
        r1_ref[...] = r1
        unit, _ = normalize(r1)
        a2 = unit * gain + shift
        a2_ref[...] = a2.astype(LOW)
        ot_scr[...] = a2.T.astype(LOW)
        permuted(a2t_ref)
        vecg_ref[...] = jnp.zeros_like(vecg_ref)
        vecg_ref[11:12, :] = jnp.sum(dy, axis=0, keepdims=True)
        y_ref[...] = r1 + bp
        da2_ref[...] = jnp.zeros_like(da2_ref)
        for copy in copies(1):
            copy.wait()

    def block(n):
        return wide[:, pl.ds(pl.multiple_of(n * width, 128), width)]

    @pl.when(step % 2 == 0)
    def _():
        row = pl.ds(7 + step // 2, 1)
        vecg_ref[row, :] = mlp_chunk(
            a2_ref, a2t_ref, dy_ref, block(1 + step), block(2 + step), vec_ref[row, :],
            y_ref, da2_ref, act_scr, keep, send,
        )

    @pl.when(step % 2 == 1)
    def _():
        put(keep, send, dot_nn(dyt_ref[...], act_scr[...]))


def mlp_last_kernel(parts, done, place, half, live_ref, vec_ref, *refs):
    r1_ref, a2_ref, a2t_ref, dy_ref, dyt_ref, y_ref, da2_ref, wout_ref, vecg_in, *refs = refs
    o_refs, sources, refs = refs[:parts], refs[parts : parts + 6], refs[parts + 6 :]
    out_ref, keep, send, dr1_ref, vecg_ref = refs[:5]
    do_refs, (wide, act_scr, y_scr, da2_scr, sems) = refs[5 : 5 + parts], refs[5 + parts :]
    step = pl.program_id(0)
    last = pl.num_programs(0) - 1
    rows = o_refs[0].shape[0]
    slots, width = r1_ref.shape
    split = 2 * width

    def copies(k):
        span = ((0, split), (split, wide.shape[1]))[k]
        return weight_copies(place, half, sources, wide, span, (1 + 2 * done) * width, sems.at[k])

    def block(n):
        return wide[:, pl.ds(pl.multiple_of(n * width, 128), width)]

    @pl.when(step == 0)
    def _():
        for k in range(2):
            for copy in copies(k):
                copy.start()
        y_scr[...] = y_ref[...]
        da2_scr[...] = da2_ref[...]
        vecg_ref[...] = vecg_in[...]
        for copy in copies(0):
            copy.wait()

    @pl.when(step == 2)
    def _():
        for copy in copies(1):
            copy.wait()

    @pl.when((step < last) & (step % 2 == 0))
    def _():
        row = pl.ds(7 + done + step // 2, 1)
        vecg_ref[row, :] = mlp_chunk(
            a2_ref, a2t_ref, dy_ref, block(step), block(1 + step), vec_ref[row, :],
            y_scr, da2_scr, act_scr, keep, send,
        )

    @pl.when((step < last) & (step % 2 == 1))
    def _():
        put(keep, send, dot_nn(dyt_ref[...], act_scr[...]))

    @pl.when(step == last)
    def _():
        live = lax.broadcasted_iota(jnp.int32, (slots, 1), 0) < live_ref[0]
        out_ref[...] = jnp.where(live, y_scr[...], 0.0).astype(LOW)
        unit, inverse = normalize(r1_ref[...])
        da2 = da2_scr[...]
        vecg_ref[5:6, :] = jnp.sum(da2 * unit, axis=0, keepdims=True)
        vecg_ref[6:7, :] = jnp.sum(da2, axis=0, keepdims=True)
        dr1 = dy_ref[...].astype(HIGH) + normalize_back(unit, inverse, da2 * vec_ref[5:6, :])
        dr1_ref[...] = dr1
        low = dr1.astype(LOW)
        vecg_ref[4:5, :] = jnp.sum(low.astype(HIGH), axis=0, keepdims=True)
        for j in range(parts):
            start = pl.multiple_of((place[0] ^ j) * rows, 16)
            do_refs[j][...] = dot_nt(wout_ref[pl.ds(start, rows), :], low).astype(LOW)
        put(keep, send, dot_nn(jnp.concatenate([ref[...] for ref in o_refs], axis=0), low))


def group_layout(length_row, count_row, slots):
    starts = jnp.cumsum(count_row) - count_row
    within = jnp.arange(slots, dtype=jnp.int32)
    position = (starts[:, None] + within[None, :]).reshape(-1)
    live_rows = (within[None, :] < count_row[:, None]).reshape(-1)
    boundary = jnp.cumsum(length_row)
    segment = jnp.sum((position[:, None] >= boundary[None, :]).astype(jnp.int32), axis=1)
    buffer_slot = jnp.arange(position.shape[0], dtype=jnp.int32)
    return jnp.where(live_rows, segment, -1 - buffer_slot)


def adam_update(master, first, second, gradient, factor, rate, decay):
    clipped = gradient * factor
    first_new = BETA_FIRST * first + (1.0 - BETA_FIRST) * clipped
    second_new = BETA_SECOND * second + (1.0 - BETA_SECOND) * clipped * clipped
    first_hat = first_new / (1.0 - BETA_FIRST**STEP)
    second_hat = second_new / (1.0 - BETA_SECOND**STEP)
    master_new = master - rate * (
        first_hat / (jnp.sqrt(second_hat) + ADAM_EPSILON) + decay * master
    )
    return (clipped, master_new, first_new, second_new)


def adam_kernel(fc_rows, factor_ref, _, *refs):
    grads, states, outs = refs[:5], refs[5:11], refs[11:]
    near = pl.program_id(0) < pl.num_programs(0) // 2
    first, second = grads[0][0], jnp.where(near, grads[1][0], grads[2][0])
    factor = factor_ref[0]
    width = outs[0].shape[-1] // fc_rows
    qkv = jnp.where(near, grads[3][0], grads[4][0])[:, : 3 * width]

    def update(gradient, at, base):
        results = adam_update(
            *[states[base + n][at] for n in range(3)],
            gradient.astype(HIGH), factor, RATE_MATRIX, DECAY_MATRIX,
        )
        for n, result in enumerate(results):
            outs[base // 3 * 4 + n][at] = result

    blocks = [first[:, n : n + width] for n in range(0, first.shape[1], width)]
    blocks += [second[:, n : n + width] for n in range(0, second.shape[1], width)]
    for f in range(fc_rows):
        span = slice(f * width, (f + 1) * width)
        for n in range(2):
            update(blocks[2 * f + n], (n, 0, slice(None), span), 3)
    update(qkv, (0, slice(None), slice(0, 3 * width)), 0)
    update(blocks[-1], (0, slice(None), slice(3 * width, 4 * width)), 0)


def swap(array, axis, bit, count):
    return lax.ppermute(array, axis, [(i, i ^ bit) for i in range(count)])


def pick(array, index):
    return lax.dynamic_index_in_dim(array, index, 0, keepdims=False)


def deal(pieces, parts):
    return list(pieces[:1]) + [swap(pieces[j], "shard", j, parts) for j in range(1, parts)]


def in_order(relative, place, parts):
    relative = jnp.stack(relative)
    return jnp.stack([pick(relative, place ^ r) for r in range(parts)])


def collect(own, parts):
    have = [own]
    bit = parts // 2
    slots = [0]
    while bit:
        have = have + [swap(piece, "shard", bit, parts) for piece in have]
        slots = slots + [s ^ bit for s in slots]
        bit //= 2
    return [have[slots.index(j)] for j in range(parts)]


def after(value, *others):
    return lax.optimization_barrier((value, *others))[0]


def add_low(a, b):
    return (a.astype(HIGH) + b.astype(HIGH)).astype(LOW)


def bits_of(count):
    return [1 << n for n in range(count.bit_length() - 1)]


def halve(array, upper, dim):
    length = array.shape[dim] // 2
    keep = lax.dynamic_slice_in_dim(array, upper * length, length, dim)
    return keep, lax.dynamic_slice_in_dim(array, (1 - upper) * length, length, dim)


def scatter_half(array, dim, bit, replica, replicas):
    keep, send = halve(array, (replica // bit) % 2, dim)
    return keep, swap(send, "dp", bit, replicas)


def params(*semantics):
    return pltpu.CompilerParams(dimension_semantics=semantics, vmem_limit_bytes=VMEM_LIMIT)


def cost(flops, moved, special=0):
    return pl.CostEstimate(flops=int(flops), bytes_accessed=int(moved), transcendentals=int(special))


def whole(*shape):
    zeros = (0,) * len(shape)
    return pl.BlockSpec(shape, lambda *_: zeros)


def make_on_device(parts, replicas):
    def on_device(
        tokens, cotangent, lengths, counts,
        attn_w, attn_m, attn_v, mlp_w, mlp_m, mlp_v, vec_w, vec_m, vec_v,
    ):
        slots, width = tokens.shape
        rows = attn_w.shape[0]
        hidden = mlp_w.shape[2]
        fc_rows = hidden // width
        total = parts * slots
        head_size = width // HEADS
        own_heads = HEADS // parts
        own_cols = own_heads * head_size
        scale = head_size ** (-0.5)
        place = lax.axis_index("shard")
        replica = lax.axis_index("dp")
        prefetch = place.reshape(1).astype(jnp.int32)

        half = replica % 2
        side = half.reshape(1).astype(jnp.int32)

        x_all = collect(tokens, parts)
        w_pieces = pl.pallas_call(
            cut_kernel,
            grid_spec=pltpu.PrefetchScalarGridSpec(
                num_scalar_prefetch=1,
                grid=(1,),
                in_specs=[whole(rows, 3 * width), whole(vec_w.shape[0], rows)],
                out_specs=[whole(rows + 16, 3 * own_cols)] * parts,
            ),
            out_shape=[jax.ShapeDtypeStruct((rows + 16, 3 * own_cols), LOW)] * parts,
            compiler_params=params("arbitrary"),
            cost_estimate=cost(0, 4e6),
            name="cut",
        )(prefetch, attn_w, vec_w)
        w_local = deal(w_pieces, parts)

        blocks = 2 * fc_rows + 1
        split = (fc_rows // 2 * 2 + 1) * width
        wide_own, *wide_half = pl.pallas_call(
            widen_kernel,
            grid_spec=pltpu.PrefetchScalarGridSpec(
                num_scalar_prefetch=1,
                grid=(1,),
                in_specs=[
                    pl.BlockSpec((rows, width), lambda *_: (0, 3)),
                    whole(2, rows, hidden),
                ],
                out_specs=[
                    whole(rows, blocks * width),
                    whole(rows // 2, split),
                    whole(rows // 2, blocks * width - split),
                ],
            ),
            out_shape=[
                jax.ShapeDtypeStruct((rows, blocks * width), LOW),
                jax.ShapeDtypeStruct((rows // 2, split), LOW),
                jax.ShapeDtypeStruct((rows // 2, blocks * width - split), LOW),
            ],
            compiler_params=params("arbitrary"),
            cost_estimate=cost(0, 12e6),
            name="widen",
        )(side, attn_w, mlp_w)
        wide_own, *wide_half = lax.optimization_barrier((wide_own, *wide_half, *w_local, *x_all))[:3]
        near = [swap(mine, "shard", parts // 2, parts) for mine in wide_half]
        wide_core = swap(wide_own, "shard", 1, parts)

        segment = group_layout(lengths[0], counts[0], slots)
        seg_col = segment[:, None]
        seg_row = segment[None, :]
        own_vec = vec_w.astype(LOW).astype(HIGH)
        bias_local = jnp.concatenate(
            [own_vec[2], jnp.zeros((own_cols,), HIGH), own_vec[3]]
        )[:, None]

        a1, qkv, w_t, vectors = pl.pallas_call(
            functools.partial(project_kernel, parts),
            grid_spec=pltpu.PrefetchScalarGridSpec(
                num_scalar_prefetch=1,
                grid=(parts,),
                in_specs=[
                    *[pl.BlockSpec(memory_space=pl.ANY)] * parts,
                    *[whole(rows + 16, 3 * own_cols)] * parts,
                    whole(3 * own_cols, 1),
                ],
                out_specs=[
                    pl.BlockSpec((slots, width), lambda i, p: (p[0] ^ i, 0)),
                    pl.BlockSpec((3 * own_cols, slots), lambda i, p: (0, p[0] ^ i)),
                    whole(3 * own_cols, width),
                    whole(16, width),
                ],
                scratch_shapes=[
                    pltpu.VMEM((width, 3 * own_cols), HIGH),
                    pltpu.VMEM((parts, slots, width), LOW),
                    pltpu.SemaphoreType.DMA((parts,)),
                ],
            ),
            out_shape=[
                jax.ShapeDtypeStruct((total, width), LOW),
                jax.ShapeDtypeStruct((3 * own_cols, total), LOW),
                jax.ShapeDtypeStruct((3 * own_cols, width), LOW),
                jax.ShapeDtypeStruct((16, width), HIGH),
            ],
            compiler_params=params("arbitrary"),
            cost_estimate=cost(2 * total * width * 3 * own_cols * 3, 12e6),
            name="project",
        )(prefetch, *x_all, *w_local, bias_local)

        pair_flops = 2 * total * total * head_size * 4 // 2

        def head_specs(h):
            return [
                pl.BlockSpec((head_size, total), functools.partial(lambda k, *_: (k * own_heads + h, 0), k))
                for k in range(3)
            ]

        def attend(h, qkv):
            return pl.pallas_call(
                functools.partial(attend_kernel, scale),
                grid_spec=pltpu.PrefetchScalarGridSpec(
                    num_scalar_prefetch=1,
                    grid=(1,),
                    in_specs=head_specs(h) + [whole(total, 1), whole(1, total)],
                    out_specs=[whole(parts, head_size, slots), whole(1, total, 1)],
                    scratch_shapes=[pltpu.VMEM((total, head_size), LOW)],
                ),
                out_shape=[
                    jax.ShapeDtypeStruct((parts, head_size, slots), LOW),
                    jax.ShapeDtypeStruct((1, total, 1), HIGH),
                ],
                compiler_params=params("arbitrary"),
                cost_estimate=cost(2 * pair_flops, 4e6, total * total // 2),
                name="attend",
            )(prefetch, qkv, qkv, qkv, seg_col, seg_row)

        mixed, lse = [], []
        for h in range(own_heads):
            if h == 1:
                qkv, near[0] = lax.optimization_barrier((qkv, near[0]))
                far = [swap(near[0], "dp", 1, replicas)]
                turned = [swap(near[0], "shard", 1, parts)]
            head_mixed, head_lse = attend(h, qkv)
            mixed.append(head_mixed)
            lse.append(head_lse)
        near[1] = after(near[1], mixed[-1])
        far.append(swap(near[1], "dp", 1, replicas))
        mixed_own = deal(
            [jnp.concatenate([head[j] for head in mixed], axis=0) for j in range(parts)], parts
        )
        turned.append(swap(near[1], "shard", 1, parts))
        far[1], mixed_own[0] = lax.optimization_barrier((far[1], mixed_own[0]))
        wide = [
            [wide_own, wide_core, near[k], far[k], turned[k], swap(far[k], "shard", 1, parts)]
            for k in range(2)
        ]
        live_own = lax.dynamic_index_in_dim(counts[0], place, 0, keepdims=True)
        scalars = (prefetch, side, live_own)
        in_hbm = pl.BlockSpec(memory_space=pltpu.HBM)
        done = fc_rows // 2

        def grad_outs(steps):
            spec = pl.BlockSpec((parts // 2, rows, width), lambda i, *_: (0, 0, i))
            shape = jax.ShapeDtypeStruct((parts // 2, rows, steps * width), LOW)
            return [spec] * 2, [shape] * 2

        def mlp_cost(steps):
            return cost(6 * slots * width * width * (steps + 1), 20e6, slots * hidden // 2)

        by_slot, by_width = (slots, width), (width, slots)
        kept = [by_slot, by_slot, by_width, by_slot, by_width, by_slot, by_slot, (width, width), (16, width)]
        kept_types = [HIGH, LOW, LOW, LOW, LOW, HIGH, HIGH, LOW, HIGH]
        specs, shapes = grad_outs(2 * done)
        keep_a, send_a, *state = pl.pallas_call(
            functools.partial(mlp_first_kernel, parts),
            grid_spec=pltpu.PrefetchScalarGridSpec(
                num_scalar_prefetch=3,
                grid=(2 * done,),
                in_specs=[whole(slots, width), whole(slots, width), whole(16, width)]
                + [whole(own_cols, slots)] * parts
                + [in_hbm] * 6,
                out_specs=specs + [whole(*shape) for shape in kept],
                scratch_shapes=[
                    pltpu.VMEM((width, split), LOW),
                    pltpu.VMEM((width, slots), LOW),
                    pltpu.VMEM((slots, width), LOW),
                    pltpu.SemaphoreType.DMA((2, 6)),
                ],
            ),
            out_shape=shapes
            + [jax.ShapeDtypeStruct(shape, kind) for shape, kind in zip(kept, kept_types)],
            compiler_params=params("arbitrary"),
            cost_estimate=mlp_cost(2 * done),
            name="mlp_first",
        )(*scalars, tokens, cotangent, vectors, *mixed_own, *wide[0])
        got_a = swap(send_a, "shard", 1, parts)

        specs, shapes = grad_outs(blocks - 2 * done)
        block_out, keep_b, send_b, grad_resid, mid_grads, *do_pieces = pl.pallas_call(
            functools.partial(mlp_last_kernel, parts, done),
            grid_spec=pltpu.PrefetchScalarGridSpec(
                num_scalar_prefetch=3,
                grid=(blocks - 2 * done,),
                in_specs=[whole(16, width)]
                + [whole(*shape) for shape in kept]
                + [whole(own_cols, slots)] * parts
                + [in_hbm] * 6,
                out_specs=[whole(slots, width)]
                + specs
                + [whole(slots, width), whole(16, width)]
                + [whole(own_cols, slots)] * parts,
                scratch_shapes=[
                    pltpu.VMEM((width, blocks * width - split), LOW),
                    pltpu.VMEM((slots, width), LOW),
                    pltpu.VMEM((slots, width), HIGH),
                    pltpu.VMEM((slots, width), HIGH),
                    pltpu.SemaphoreType.DMA((2, 6)),
                ],
            ),
            out_shape=[jax.ShapeDtypeStruct((slots, width), LOW)]
            + shapes
            + [jax.ShapeDtypeStruct((slots, width), HIGH), jax.ShapeDtypeStruct((16, width), HIGH)]
            + [jax.ShapeDtypeStruct((own_cols, slots), LOW)] * parts,
            compiler_params=params("arbitrary"),
            cost_estimate=mlp_cost(blocks - 2 * done),
            name="mlp_last",
        )(*scalars, vectors, *state, *mixed_own, *wide[1])

        do_own = deal(do_pieces, parts)
        got_b = swap(send_b, "shard", 1, parts)
        got_a = after(got_a, grad_resid)
        own_a, other_a = [add_low(keep_a[n], got_a[n]) for n in range(2)]
        got_a = swap(other_a, "shard", parts // 2, parts)
        got_b = after(got_b, other_a)
        own_b, other_b = halve(add_low(keep_b, got_b), half, 1)
        *do_own, own_a, own_b, other_b = lax.optimization_barrier((*do_own, own_a, own_b, other_b))
        got_b = swap(other_b, "dp", 1, replicas)

        def attend_back(h, qkv):
            return pl.pallas_call(
                functools.partial(attend_back_kernel, scale),
                grid_spec=pltpu.PrefetchScalarGridSpec(
                    num_scalar_prefetch=1,
                    grid=(1,),
                    in_specs=head_specs(h)
                    + [whole(total, 1), whole(1, total), whole(1, total, 1)]
                    + [pl.BlockSpec((head_size, slots), lambda *_: (h, 0))] * parts,
                    out_specs=whole(3, head_size, total),
                    scratch_shapes=[
                        pltpu.VMEM((total, head_size), LOW),
                        pltpu.VMEM((parts, head_size, slots), LOW),
                        pltpu.VMEM((head_size, total), HIGH),
                        pltpu.VMEM((head_size, total), HIGH),
                    ],
                ),
                out_shape=jax.ShapeDtypeStruct((3, head_size, total), LOW),
                compiler_params=params("arbitrary"),
                cost_estimate=cost(
                    5 * pair_flops, 4e6, total * total // 2
                ),
                name="attend_back",
            )(prefetch, qkv, qkv, qkv, seg_col, seg_row, lse[h], *do_own)

        dqkv = []
        for h in range(own_heads):
            if h == own_heads - 1:
                got_a, *dqkv = lax.optimization_barrier((got_a, *dqkv))
                own_a, other_a = halve(add_low(own_a, got_a), half, 0)
                qkv = after(qkv, other_a)
                got_a = swap(other_a, "dp", 1, replicas)
            dqkv.append(attend_back(h, qkv))
        z_bits = [bit for bit in (1 << n for n in range(1, 20)) if bit < replicas]
        got_a, got_b, dqkv[-1] = lax.optimization_barrier((got_a, got_b, dqkv[-1]))
        own_b, other_b = [add_low(own_b[n], got_b[n]) for n in range(2)]
        got_b = swap(other_b, "shard", parts // 2, parts)
        state_a = scatter_half(add_low(own_a, got_a), 0, z_bits[0], replica, replicas)
        dqkv[0] = after(dqkv[0], own_b, other_b, state_a[0])

        q_cols = 3 * own_cols
        extra = vec_w.shape[0]
        half_rows = rows // 2
        da1_keep, da1_send, own_q, other_q = pl.pallas_call(
            functools.partial(projection_back_kernel, own_heads, parts),
            grid_spec=pltpu.PrefetchScalarGridSpec(
                num_scalar_prefetch=2,
                grid=(parts,),
                in_specs=[
                    *[pl.BlockSpec(memory_space=pl.ANY)] * parts,
                    pl.BlockSpec((slots, width), lambda i, p, _: (p[0] ^ i, 0)),
                ]
                + [pl.BlockSpec((3, head_size, slots), lambda i, p, _: (0, 0, p[0] ^ i))] * own_heads
                + [whole(q_cols, width), whole(16, width), whole(16, width)],
                out_specs=[pl.BlockSpec((1, slots, width), lambda i, *_: (i // 2, 0, 0))] * 2
                + [whole(parts, half_rows, q_cols + extra)] * 2,
                scratch_shapes=[
                    pltpu.VMEM((q_cols, width), HIGH),
                    pltpu.VMEM((16, width), HIGH),
                    pltpu.VMEM((q_cols, 1), HIGH),
                    pltpu.VMEM((width, 16), HIGH),
                    pltpu.VMEM((width, q_cols + 64), HIGH),
                    pltpu.VMEM((parts, slots, width), LOW),
                    pltpu.SemaphoreType.DMA((parts,)),
                ],
            ),
            out_shape=[jax.ShapeDtypeStruct((parts // 2, slots, width), LOW)] * 2
            + [jax.ShapeDtypeStruct((parts, half_rows, q_cols + extra), LOW)] * 2,
            compiler_params=params("arbitrary"),
            cost_estimate=cost(4 * total * width * 3 * own_cols * 2, 16e6),
            name="projection_back",
        )(prefetch, side, *x_all, a1, *dqkv, w_t, vectors, mid_grads)

        share = rows // replicas
        tokens_seen = [own_q]

        def seen(*values):
            *values, _ = lax.optimization_barrier((*values, tokens_seen[-1]))
            return values[0] if len(values) == 1 else values

        def event(value):
            tokens_seen.append(value)
            return value

        def scatter_on(name, keep, got, bit):
            array = event(add_low(keep, seen(got)))
            return scatter_half(array, {"q": 1}.get(name, 0), bit, replica, replicas)

        last_bit = z_bits[-1]

        def scatter_rest(name, state):
            for bit in z_bits[1:]:
                state = scatter_on(name, *state, bit)
            return state

        got_q = swap(other_q, "dp", 1, replicas)
        da1_got = swap(da1_send, "shard", 1, parts)
        state_a = scatter_rest("a", state_a)
        state_b = scatter_on("b", own_b, got_b, z_bits[0])
        state_q = scatter_on("q", own_q, got_q, z_bits[0])
        part_a = event(add_low(state_a[0], seen(state_a[1])))
        all_a = lax.all_gather(part_a, "dp", axis=0)
        state_b = scatter_rest("b", state_b)
        state_q = scatter_rest("q", state_q)
        part_q = event(add_low(state_q[0], seen(state_q[1])))

        main = part_q[:, :, :q_cols]
        vec_parts = part_q[:, :, q_cols:].transpose(1, 0, 2).reshape(1, share, parts * extra)
        vec_parts = jnp.broadcast_to(vec_parts, (parts,) + vec_parts.shape[1:])
        pieces = jnp.concatenate([main, vec_parts], axis=2)
        dealt = deal([pick(pieces, place ^ j) for j in range(parts)], parts)
        dealt = in_order(seen(*dealt), place, parts)
        q_rows = (
            dealt[:, :, :q_cols]
            .reshape(parts, share, 3, own_cols)
            .transpose(1, 2, 0, 3)
            .reshape(share, 3 * width)
        )
        vec_parts = jnp.sum(dealt[:, :, q_cols:].astype(HIGH), axis=0).astype(LOW)
        vec_own = lax.dynamic_index_in_dim(
            vec_parts.reshape(share, parts, extra), place, 1, keepdims=False
        )
        near_q = event(jnp.concatenate([q_rows, vec_own], axis=1)[None])
        got_q = swap(near_q, "dp", last_bit, replicas)
        near_b = event(add_low(state_b[0], seen(state_b[1])))[None]
        got_b = swap(near_b, "dp", last_bit, replicas)
        squares = sum(jnp.sum(jnp.square(p.astype(HIGH))) for p in (part_a, near_b, main))
        squares += jnp.where(place == 0, jnp.sum(jnp.square(vec_parts.astype(HIGH))), 0.0)
        squares = squares.reshape(1, 1)
        hops = [("shard", bit, parts) for bit in (1 << n for n in range(20)) if bit < parts]
        hops += [("dp", bit, replicas) for bit in (1 << n for n in range(20)) if bit < replicas]
        hops = iter(hops)
        pending = swap(squares, *next(hops))

        def norm_hop():
            nonlocal squares, pending
            if pending is None:
                return
            squares = event(squares + seen(pending))
            hop = next(hops, None)
            pending = None if hop is None else swap(squares, *hop)

        for bit in z_bits[-2::-1] + [1]:
            near_q = event(jnp.concatenate([near_q, seen(got_q)], axis=0))
            got_q = swap(near_q, "dp", bit, replicas)
            near_b = event(jnp.concatenate([near_b, seen(got_b)], axis=0))
            got_b = swap(near_b, "dp", bit, replicas)
            norm_hop()
        while pending is not None:
            norm_hop()
        far_q, far_b = seen(got_q, got_b)

        def block_of(index):
            block = index % 2
            for bit in z_bits:
                block = block * 2 + index // bit % 2
            return block

        def index_of(block):
            index = 0
            for bit in z_bits[::-1]:
                index = index + block % 2 * bit
                block = block // 2
            return index + block

        turn = block_of(replica)
        small = jnp.concatenate([near_q[:, :, 3 * width :], far_q[:, :, 3 * width :]], axis=0)
        small = jnp.stack([pick(small, turn ^ r) for r in range(replicas)]).astype(HIGH)
        summed_vec = small[:, :, :extra].reshape(rows, extra).T

        own_da1 = da1_keep[0].astype(HIGH) + da1_got[0].astype(HIGH)
        da1 = own_da1 + swap(add_low(da1_keep[1], da1_got[1]), "shard", 2, parts).astype(HIGH)
        unit, inverse = normalize(tokens.astype(HIGH))
        grad_input = grad_resid + normalize_back(unit, inverse, da1 * vectors[0:1])
        live_rows = jnp.arange(slots, dtype=jnp.int32) < live_own[0]
        grad_in = jnp.where(live_rows[:, None], grad_input, 0.0).astype(LOW)

        norm_total = jnp.sqrt(squares[0, 0])
        factor = jnp.minimum(1.0, CLIP_LIMIT / (norm_total + 1e-06))
        near_count = replicas // 2
        def near_spec(array):
            block = (1,) + array.shape[1:]
            return pl.BlockSpec(block, lambda i, *_: (jnp.minimum(i, near_count - 1), 0, 0))

        def far_spec(array):
            block = (1,) + array.shape[1:]
            return pl.BlockSpec(block, lambda i, *_: (jnp.maximum(i - near_count, 0), 0, 0))

        def gathered_spec(array):
            return pl.BlockSpec((1,) + array.shape[1:], lambda i, _, p: (index_of(i ^ p[0]), 0, 0))

        attn_shape = (replicas, share, 4 * width)
        mlp_shape = (2, replicas, share, hidden)
        attn_spec = pl.BlockSpec((1, share, 4 * width), lambda i, _, p: (i ^ p[0], 0, 0))
        mlp_spec = pl.BlockSpec((2, 1, share, hidden), lambda i, _, p: (0, i ^ p[0], 0, 0))
        updated = pl.pallas_call(
            functools.partial(adam_kernel, fc_rows),
            grid_spec=pltpu.PrefetchScalarGridSpec(
                num_scalar_prefetch=2,
                grid=(replicas,),
                in_specs=[gathered_spec(all_a)]
                + [near_spec(near_b), far_spec(far_b), near_spec(near_q), far_spec(far_q)]
                + [attn_spec] * 3
                + [mlp_spec] * 3,
                out_specs=[attn_spec] * 4 + [mlp_spec] * 4,
            ),
            out_shape=[jax.ShapeDtypeStruct(attn_shape, HIGH)] * 4
            + [jax.ShapeDtypeStruct(mlp_shape, HIGH)] * 4,
            compiler_params=params("arbitrary"),
            cost_estimate=cost(30 * 9 * rows * width, 54e6),
            name="adam",
        )(
            factor.reshape(1),
            turn.reshape(1).astype(jnp.int32),
            all_a,
            near_b,
            far_b,
            near_q,
            far_q,
            *[array.reshape(attn_shape) for array in (attn_w, attn_m, attn_v)],
            *[array.reshape(mlp_shape) for array in (mlp_w, mlp_m, mlp_v)],
        )
        attn_grad, attn_w_new, attn_m_new, attn_v_new = [u.reshape(attn_w.shape) for u in updated[:4]]
        mlp_grad, mlp_w_new, mlp_m_new, mlp_v_new = [u.reshape(mlp_w.shape) for u in updated[4:]]
        vec_grad, vec_w_new, vec_m_new, vec_v_new = adam_update(
            vec_w, vec_m, vec_v, summed_vec, factor, RATE_VECTOR, 0.0
        )
        return (
            block_out, grad_in, attn_grad, mlp_grad, vec_grad,
            attn_w_new, attn_m_new, attn_v_new, mlp_w_new, mlp_m_new, mlp_v_new,
            vec_w_new, vec_m_new, vec_v_new, norm_total.reshape(1),
        )

    return on_device


def solution(mesh):
    tokens = P(("dp", "shard"), None)
    groups = P("dp", None)
    attn = P("shard", None)
    mlp = P(None, "shard", None)
    vec = P(None, "shard")
    return jax.shard_map(
        make_on_device(mesh.shape["shard"], mesh.shape["dp"]),
        mesh=mesh,
        in_specs=(tokens, tokens, groups, groups) + (attn,) * 3 + (mlp,) * 3 + (vec,) * 3,
        out_specs=(tokens, tokens, attn, mlp, vec) + (attn,) * 3 + (mlp,) * 3 + (vec,) * 3 + (P(),),
        check_vma=False,
    )
```

```python
import functools

import jax
import jax.numpy as jnp
from jax import lax
from jax.experimental import pallas as pl
from jax.experimental.pallas import tpu as pltpu
from jax.sharding import PartitionSpec as P

HEADS = 12
STEP = 10
NORM_EPSILON = 1e-05
BETA_FIRST = 0.9
BETA_SECOND = 0.999
ADAM_EPSILON = 1e-08
RATE_MATRIX = 0.1
RATE_VECTOR = 0.2
DECAY_MATRIX = 0.1
CLIP_LIMIT = 1.0
MASKED_SCORE = -1e30
QUERY_BLOCK = 256
VMEM_LIMIT = 50 * 1024 * 1024
LOW = jnp.bfloat16
HIGH = jnp.float32


def dot_nn(a, b):
    return lax.dot_general(a, b, (((1,), (0,)), ((), ())), preferred_element_type=HIGH)


def dot_nt(a, b):
    return lax.dot_general(a, b, (((1,), (1,)), ((), ())), preferred_element_type=HIGH)


def low_t(a):
    return a.astype(HIGH).T.astype(LOW)


def normalize(features):
    centered = features - jnp.mean(features, axis=-1, keepdims=True)
    variance = jnp.mean(centered * centered, axis=-1, keepdims=True)
    inverse = lax.rsqrt(variance + NORM_EPSILON)
    return centered * inverse, inverse


def normalize_back(unit, inverse, grad_unit):
    first = jnp.mean(grad_unit, axis=-1, keepdims=True)
    second = jnp.mean(grad_unit * unit, axis=-1, keepdims=True)
    return inverse * (grad_unit - first - unit * second)


def cut_kernel(place, w_ref, vec_ref, *out_refs):
    parts = len(out_refs)
    rows, columns = w_ref.shape
    width = columns // 3
    cols = width // parts
    vec = vec_ref[...]
    tail = [
        jnp.concatenate([vec[3 * k + m : 3 * k + m + 1, :] for m in range(3)], axis=1)
        for k in range(vec.shape[0] // 3)
    ]
    tail.append(jnp.zeros((16 - len(tail), 3 * cols), HIGH))
    tail = jnp.concatenate(tail, axis=0).astype(LOW)
    for r in range(parts):
        starts = [k * width + r * cols for k in range(3)]
        piece = jnp.concatenate([w_ref[:, c : c + cols] for c in starts], axis=1).astype(LOW)
        for j in range(parts):

            @pl.when((place[0] ^ j) == r)
            def _():
                out_refs[j][:rows, :] = piece
                out_refs[j][rows:, :] = tail


def widen_kernel(half, out_ref, mlp_ref, wide_ref, *half_refs):
    rows, width = out_ref.shape
    start = pl.multiple_of(half[0] * (rows // 2), 16)
    near = pl.ds(start, rows // 2)
    sources = [(out_ref[...], out_ref[near, :])]
    for f in range(mlp_ref.shape[2] // width):
        span = slice(f * width, (f + 1) * width)
        sources += [(mlp_ref[n, :, span], mlp_ref[n, near, span]) for n in range(2)]
    split = half_refs[0].shape[1] // width
    for n, (block, part) in enumerate(sources):
        wide_ref[:, n * width : (n + 1) * width] = block.astype(LOW)
        k = int(n >= split)
        at = (n - k * split) * width
        half_refs[k][:, at : at + width] = part.astype(LOW)


def project_kernel(parts, place, *refs):
    x_refs, w_refs, refs = refs[:parts], refs[parts : 2 * parts], refs[2 * parts :]
    bias_ref, a1_ref, qkv_ref, wt_ref, vec_ref, w_scr, x_scr, sems = refs
    step = pl.program_id(0)
    rows = vec_ref.shape[1] // parts

    def copy(j):
        return pltpu.make_async_copy(x_refs[j], x_scr.at[j], sems.at[j])

    @pl.when(step == 0)
    def _():
        for j in range(parts):
            copy(j).start()
        vec_ref[...] = jnp.zeros_like(vec_ref)
        for j in range(parts):
            start = pl.multiple_of((place[0] ^ j) * rows, 16)
            w_scr[pl.ds(start, rows), :] = w_refs[j][:rows, :].astype(HIGH)
            tail = w_refs[j][rows:, :].astype(HIGH)
            for r in range(parts):

                @pl.when((place[0] ^ j) == r)
                def _():
                    for n in range(12):
                        piece = tail[n // 3 : n // 3 + 1, n % 3 * rows : (n % 3 + 1) * rows]
                        vec_ref[n : n + 1, r * rows : (r + 1) * rows] = piece

        wt_ref[...] = w_scr[...].T.astype(LOW)

    for j in range(parts):

        @pl.when(step == j)
        def _():
            copy(j).wait()

    unit, _ = normalize(x_scr[step].astype(HIGH))
    a1 = (unit * vec_ref[0:1, :] + vec_ref[1:2, :]).astype(LOW)
    a1_ref[...] = a1
    qkv_ref[...] = (dot_nt(wt_ref[...], a1) + bias_ref[...]).astype(LOW)


def masked_scores(q, kt, seg_q, seg_k, start):
    block = q.shape[0]
    out = []
    if start:
        s = dot_nn(q, kt[:, :start])
        out.append(jnp.where(seg_q == seg_k[:, :start], s, MASKED_SCORE))
    s = dot_nn(q, kt[:, start : start + block])
    row = lax.broadcasted_iota(jnp.int32, (block, block), 0)
    col = lax.broadcasted_iota(jnp.int32, (block, block), 1)
    allowed = (seg_q == seg_k[:, start : start + block]) & (col <= row)
    out.append(jnp.where(allowed, s, MASKED_SCORE))
    return out


def attend_kernel(scale, place, qt_ref, kt_ref, vt_ref, segc_ref, segr_ref, o_ref, lse_ref, v_scr):
    total = qt_ref.shape[1]
    per_part = o_ref.shape[2]
    block = min(QUERY_BLOCK, per_part)
    v_scr[...] = low_t(vt_ref[...])
    for start in range(0, total, block):
        span = slice(start, start + block)
        q = (qt_ref[:, span].astype(HIGH) * scale).T.astype(LOW)
        pieces = masked_scores(q, kt_ref, segc_ref[span, :], segr_ref, start)
        top = functools.reduce(jnp.maximum, [jnp.max(s, axis=1, keepdims=True) for s in pieces])
        weights = [jnp.exp(s - top) for s in pieces]
        mass = sum(jnp.sum(w, axis=1, keepdims=True) for w in weights)
        lse_ref[0, span, :] = top + jnp.log(mass)
        inverse = 1.0 / mass
        mixed = dot_nn((weights[-1] * inverse).astype(LOW), v_scr[span, :])
        if start:
            mixed += dot_nn((weights[0] * inverse).astype(LOW), v_scr[:start, :])
        inner = start % per_part
        o_ref[place[0] ^ (start // per_part), :, inner : inner + block] = mixed.T.astype(LOW)


def attend_back_kernel(
    scale, place, qt_ref, kt_ref, vt_ref, segc_ref, segr_ref, lse_ref, *refs
):
    *do_refs, out_ref, k_scr, do_scr, dk_scr, dv_scr = refs
    total = qt_ref.shape[1]
    parts, per_part = len(do_refs), do_refs[0].shape[1]
    block = min(QUERY_BLOCK, per_part)
    k_scr[...] = low_t(kt_ref[...])
    for j in range(parts):
        do_scr[place[0] ^ j] = do_refs[j][...]
    dk_scr[...] = jnp.zeros_like(dk_scr)
    dv_scr[...] = jnp.zeros_like(dv_scr)
    for start in range(0, total, block):
        span = slice(start, start + block)
        inner = start % per_part
        qt = qt_ref[:, span].astype(HIGH) * scale
        dot_ = do_scr[start // per_part, :, inner : inner + block]
        q = qt.T.astype(LOW)
        qt = qt.astype(LOW)
        do = low_t(dot_)
        pieces = masked_scores(q, kt_ref, segc_ref[span, :], segr_ref, start)
        spans = [slice(0, start), span] if start else [span]
        lse = lse_ref[0, span, :]
        weights = [jnp.exp(s - lse) for s in pieces]
        grads = [dot_nn(do, vt_ref[:, at]) for at in spans]
        delta = sum(jnp.sum(g * w, axis=1, keepdims=True) for g, w in zip(grads, weights))
        dq = None
        for at, w, g in zip(spans, weights, grads):
            ds = (w * (g - delta)).astype(LOW)
            term = dot_nn(ds, k_scr[at, :])
            dq = term if dq is None else dq + term
            dk_scr[:, at] += dot_nn(qt, ds)
            dv_scr[:, at] += dot_nn(dot_, w.astype(LOW))
        out_ref[0, :, span] = (dq * scale).T.astype(LOW)
    out_ref[1] = dk_scr[...].astype(LOW)
    out_ref[2] = dv_scr[...].astype(LOW)


def projection_back_kernel(heads, parts, place, half, *refs):
    x_refs, (a1_ref, *refs) = refs[:parts], refs[parts:]
    head_refs, refs = refs[:heads], refs[heads:]
    wt_ref, vec_ref, grads_ref, keep_ref, send_ref, qkeep_ref, qsend_ref, *scratch = refs
    g_scr, vec_scr, sums_scr, ext_scr, all_scr, x_scr, sems = scratch
    step = pl.program_id(0)
    cols = g_scr.shape[0] // 3
    extra = grads_ref.shape[0]
    count = qkeep_ref.shape[2] - 3 * cols

    def copy(j):
        return pltpu.make_async_copy(x_refs[j], x_scr.at[j], sems.at[j])

    @pl.when(step == 0)
    def _():
        for j in range(parts):
            copy(j).start()
        g_scr[...] = jnp.zeros_like(g_scr)
        vec_scr[...] = grads_ref[...]
        sums_scr[...] = jnp.zeros_like(sums_scr)

    for j in range(parts):

        @pl.when(step == j)
        def _():
            copy(j).wait()

    dqkv = jnp.concatenate([ref[k] for k in range(3) for ref in head_refs], axis=0)
    da1 = dot_nn(low_t(dqkv), wt_ref[...])

    @pl.when(step % 2 == 0)
    def _():
        keep_ref[0] = da1.astype(LOW)

    @pl.when(step % 2 == 1)
    def _():
        send_ref[0] = da1.astype(LOW)

    g_scr[...] += dot_nn(dqkv, a1_ref[...])
    unit, _ = normalize(x_scr[step].astype(HIGH))
    vec_scr[0:1, :] += jnp.sum(da1 * unit, axis=0, keepdims=True)
    vec_scr[1:2, :] += jnp.sum(da1, axis=0, keepdims=True)
    sums_scr[...] += jnp.sum(dqkv.astype(HIGH), axis=1, keepdims=True)

    @pl.when(step == pl.num_programs(0) - 1)
    def _():
        ext_scr[...] = vec_scr[...].T
        own = pl.ds(pl.multiple_of(place[0] * cols, 16), cols)
        ext_scr[own, 2:3] = sums_scr[:cols, :]
        ext_scr[own, 3:4] = sums_scr[2 * cols :, :]
        all_scr[:, : 3 * cols] = g_scr[...].T
        all_scr[:, 3 * cols : 3 * cols + extra] = ext_scr[...]
        rows = all_scr.shape[0] // parts
        for r in range(parts):
            for ref, side in ((qkeep_ref, half[0]), (qsend_ref, 1 - half[0])):
                start = pl.multiple_of(r * rows + side * (rows // 2), 16)
                ref[r] = all_scr[pl.ds(start, rows // 2), : 3 * cols + count].astype(LOW)


GELU_C = 0.7978845608028654
GELU_A = 0.044715


def mlp_kernel(
    parts, first_blocks, place, half, live_ref, x_ref, cot_ref, vec_ref, *refs
):
    o_refs, refs = refs[:parts], refs[parts:]
    own_ref, core_ref, *wide_refs = refs[:10]
    out_ref, *grad_refs = refs[10:15]
    dr1_ref, vecg_ref, *refs = refs[15:]
    do_refs, scratch = refs[:parts], refs[parts:]
    wide, ot_scr, r1_scr, a2_scr, a2t_scr, dy_scr, dyt_scr, y_scr, da2_scr, act_scr, sems = scratch
    step = pl.program_id(0)
    rows = o_refs[0].shape[0]
    slots, width = x_ref.shape
    bo, gain, shift, bp = (vec_ref[r : r + 1, :] for r in (4, 5, 6, 11))
    split = wide_refs[0].shape[1]
    live = lax.broadcasted_iota(jnp.int32, (slots, 1), 0) < live_ref[0]

    def copies(k):
        half_rows = rows // 2
        near, far = half[0] * half_rows, (1 - half[0]) * half_rows
        span = slice(0, split) if k == 0 else slice(split, wide.shape[1])
        sources = [(own_ref.at[:, span], 0, 0), (core_ref.at[:, span], 1, 0)]
        spots = [(2, near), (2, far), (3, near), (3, far)]
        sources += [(wide_refs[4 * k + n], *spot) for n, spot in enumerate(spots)]
        for n, (source, j, offset) in enumerate(sources):
            start = pl.multiple_of((place[0] ^ j) * rows + offset, 16)
            target = wide.at[pl.ds(start, source.shape[0]), span]
            yield pltpu.make_async_copy(source, target, sems.at[k, n])

    def block(n):
        return wide[:, pl.ds(pl.multiple_of(n * width, 128), width)]

    def permuted(scratch, value):
        for j in range(parts):
            scratch[j * rows : (j + 1) * rows, :] = value(pl.multiple_of((place[0] ^ j) * rows, 16))

    def put(value):
        value = value.astype(LOW)
        for k in range(2):

            @pl.when((step >= first_blocks) == bool(k))
            def _():
                keep, send = grad_refs[2 * k : 2 * k + 2]
                for j in range(parts):
                    (send if j % 2 else keep)[j // 2] = value[j * rows : (j + 1) * rows, :]

    @pl.when(step == 0)
    def _():
        for k in range(2):
            for copy in copies(k):
                copy.start()
        for j in range(parts):
            start = pl.multiple_of((place[0] ^ j) * rows, 16)
            ot_scr[pl.ds(start, rows), :] = o_refs[j][...]
        mixed = low_t(ot_scr[...])
        dy = jnp.where(live, cot_ref[...].astype(HIGH), 0.0)
        dy_scr[...] = dy.astype(LOW)
        ot_scr[...] = dy.T.astype(LOW)
        permuted(dyt_scr, lambda start: ot_scr[pl.ds(start, rows), :])
        for copy in copies(0):
            copy.wait()
        r1 = x_ref[...].astype(HIGH) + dot_nn(mixed, wide[:, :width]) + bo
        r1_scr[...] = r1
        unit, _ = normalize(r1)
        a2 = unit * gain + shift
        a2_scr[...] = a2.astype(LOW)
        ot_scr[...] = a2.T.astype(LOW)
        permuted(a2t_scr, lambda start: ot_scr[pl.ds(start, rows), :])
        vecg_ref[...] = jnp.zeros_like(vecg_ref)
        vecg_ref[11:12, :] = jnp.sum(dy, axis=0, keepdims=True)
        y_scr[...] = r1 + bp
        da2_scr[...] = jnp.zeros_like(da2_scr)

    @pl.when(step == first_blocks)
    def _():
        for copy in copies(1):
            copy.wait()

    last = pl.num_programs(0) - 1

    @pl.when((step < last) & (step % 2 == 0))
    def _():
        w_fc, w_pt = block(1 + step), block(2 + step)
        u = dot_nn(a2_scr[...], w_fc) + vec_ref[pl.ds(7 + step // 2, 1), :]
        square = u * u
        t = jnp.tanh(GELU_C * (u + GELU_A * (square * u)))
        grown = 0.5 * (1.0 + t)
        act = (u * grown).astype(LOW)
        act_scr[...] = act
        y_scr[...] += dot_nt(act, w_pt)
        slope = grown + 0.5 * u * (1.0 - t * t) * (GELU_C + (3.0 * GELU_C * GELU_A) * square)
        du = (dot_nn(dy_scr[...], w_pt) * slope).astype(LOW)
        vecg_ref[pl.ds(7 + step // 2, 1), :] = jnp.sum(du.astype(HIGH), axis=0, keepdims=True)
        da2_scr[...] += dot_nt(du, w_fc)
        put(dot_nn(a2t_scr[...], du))

    @pl.when((step < last) & (step % 2 == 1))
    def _():
        put(dot_nn(dyt_scr[...], act_scr[...]))

    @pl.when(step == last)
    def _():
        out_ref[...] = jnp.where(live, y_scr[...], 0.0).astype(LOW)
        unit, inverse = normalize(r1_scr[...])
        da2 = da2_scr[...]
        vecg_ref[5:6, :] = jnp.sum(da2 * unit, axis=0, keepdims=True)
        vecg_ref[6:7, :] = jnp.sum(da2, axis=0, keepdims=True)
        dr1 = dy_scr[...].astype(HIGH) + normalize_back(unit, inverse, da2 * gain)
        dr1_ref[...] = dr1
        low = dr1.astype(LOW)
        vecg_ref[4:5, :] = jnp.sum(low.astype(HIGH), axis=0, keepdims=True)
        put(dot_nn(jnp.concatenate([ref[...] for ref in o_refs], axis=0), low))
        for j in range(parts):
            start = pl.multiple_of((place[0] ^ j) * rows, 16)
            do_refs[j][...] = dot_nt(wide[pl.ds(start, rows), :width], low).astype(LOW)


def group_layout(length_row, count_row, slots):
    starts = jnp.cumsum(count_row) - count_row
    within = jnp.arange(slots, dtype=jnp.int32)
    position = (starts[:, None] + within[None, :]).reshape(-1)
    live_rows = (within[None, :] < count_row[:, None]).reshape(-1)
    boundary = jnp.cumsum(length_row)
    segment = jnp.sum((position[:, None] >= boundary[None, :]).astype(jnp.int32), axis=1)
    buffer_slot = jnp.arange(position.shape[0], dtype=jnp.int32)
    return jnp.where(live_rows, segment, -1 - buffer_slot)


def adam_update(master, first, second, gradient, factor, rate, decay):
    clipped = gradient * factor
    first_new = BETA_FIRST * first + (1.0 - BETA_FIRST) * clipped
    second_new = BETA_SECOND * second + (1.0 - BETA_SECOND) * clipped * clipped
    first_hat = first_new / (1.0 - BETA_FIRST**STEP)
    second_hat = second_new / (1.0 - BETA_SECOND**STEP)
    master_new = master - rate * (
        first_hat / (jnp.sqrt(second_hat) + ADAM_EPSILON) + decay * master
    )
    return (clipped, master_new, first_new, second_new)


def adam_kernel(fc_rows, factor_ref, _, *refs):
    grads, states, outs = refs[:3], refs[3:9], refs[9:]
    near = pl.program_id(0) < pl.num_programs(0) // 2
    factor = factor_ref[0]
    width = outs[0].shape[-1] // fc_rows
    qkv = jnp.where(near, grads[1][0], grads[2][0])[:, : 3 * width]

    def update(gradient, at, base):
        results = adam_update(
            *[states[base + n][at] for n in range(3)],
            gradient.astype(HIGH), factor, RATE_MATRIX, DECAY_MATRIX,
        )
        for n, result in enumerate(results):
            outs[base // 3 * 4 + n][at] = result

    blocks = [grads[0][0, :, n : n + width] for n in range(0, grads[0].shape[2], width)]
    for f in range(fc_rows):
        span = slice(f * width, (f + 1) * width)
        for n in range(2):
            update(blocks[2 * f + n], (n, 0, slice(None), span), 3)
    update(qkv, (0, slice(None), slice(0, 3 * width)), 0)
    update(blocks[-1], (0, slice(None), slice(3 * width, 4 * width)), 0)


def swap(array, axis, bit, count):
    return lax.ppermute(array, axis, [(i, i ^ bit) for i in range(count)])


def pick(array, index):
    return lax.dynamic_index_in_dim(array, index, 0, keepdims=False)


def deal(pieces, parts):
    return list(pieces[:1]) + [swap(pieces[j], "shard", j, parts) for j in range(1, parts)]


def in_order(relative, place, parts):
    relative = jnp.stack(relative)
    return jnp.stack([pick(relative, place ^ r) for r in range(parts)])


def collect(own, parts):
    have = [own]
    bit = parts // 2
    slots = [0]
    while bit:
        have = have + [swap(piece, "shard", bit, parts) for piece in have]
        slots = slots + [s ^ bit for s in slots]
        bit //= 2
    return [have[slots.index(j)] for j in range(parts)]


def after(value, *others):
    return lax.optimization_barrier((value, *others))[0]


def add_low(a, b):
    return (a.astype(HIGH) + b.astype(HIGH)).astype(LOW)


def bits_of(count):
    return [1 << n for n in range(count.bit_length() - 1)]


def halve(array, upper, dim):
    length = array.shape[dim] // 2
    keep = lax.dynamic_slice_in_dim(array, upper * length, length, dim)
    return keep, lax.dynamic_slice_in_dim(array, (1 - upper) * length, length, dim)


def scatter_half(array, dim, bit, replica, replicas):
    keep, send = halve(array, (replica // bit) % 2, dim)
    return keep, swap(send, "dp", bit, replicas)


def params(*semantics):
    return pltpu.CompilerParams(dimension_semantics=semantics, vmem_limit_bytes=VMEM_LIMIT)


def cost(flops, moved, special=0):
    return pl.CostEstimate(flops=int(flops), bytes_accessed=int(moved), transcendentals=int(special))


def whole(*shape):
    zeros = (0,) * len(shape)
    return pl.BlockSpec(shape, lambda *_: zeros)


def make_on_device(parts, replicas):
    def on_device(
        tokens, cotangent, lengths, counts,
        attn_w, attn_m, attn_v, mlp_w, mlp_m, mlp_v, vec_w, vec_m, vec_v,
    ):
        slots, width = tokens.shape
        rows = attn_w.shape[0]
        hidden = mlp_w.shape[2]
        fc_rows = hidden // width
        total = parts * slots
        head_size = width // HEADS
        own_heads = HEADS // parts
        own_cols = own_heads * head_size
        scale = head_size ** (-0.5)
        place = lax.axis_index("shard")
        replica = lax.axis_index("dp")
        prefetch = place.reshape(1).astype(jnp.int32)

        half = replica % 2
        side = half.reshape(1).astype(jnp.int32)

        x_all = collect(tokens, parts)
        w_pieces = pl.pallas_call(
            cut_kernel,
            grid_spec=pltpu.PrefetchScalarGridSpec(
                num_scalar_prefetch=1,
                grid=(1,),
                in_specs=[whole(rows, 3 * width), whole(vec_w.shape[0], rows)],
                out_specs=[whole(rows + 16, 3 * own_cols)] * parts,
            ),
            out_shape=[jax.ShapeDtypeStruct((rows + 16, 3 * own_cols), LOW)] * parts,
            compiler_params=params("arbitrary"),
            cost_estimate=cost(0, 4e6),
            name="cut",
        )(prefetch, attn_w, vec_w)
        w_local = deal(w_pieces, parts)

        blocks = 2 * fc_rows + 1
        split = (fc_rows // 2 * 2 + 1) * width
        wide_own, *wide_half = pl.pallas_call(
            widen_kernel,
            grid_spec=pltpu.PrefetchScalarGridSpec(
                num_scalar_prefetch=1,
                grid=(1,),
                in_specs=[
                    pl.BlockSpec((rows, width), lambda *_: (0, 3)),
                    whole(2, rows, hidden),
                ],
                out_specs=[
                    whole(rows, blocks * width),
                    whole(rows // 2, split),
                    whole(rows // 2, blocks * width - split),
                ],
            ),
            out_shape=[
                jax.ShapeDtypeStruct((rows, blocks * width), LOW),
                jax.ShapeDtypeStruct((rows // 2, split), LOW),
                jax.ShapeDtypeStruct((rows // 2, blocks * width - split), LOW),
            ],
            compiler_params=params("arbitrary"),
            cost_estimate=cost(0, 12e6),
            name="widen",
        )(side, attn_w, mlp_w)
        wide_own, *wide_half = lax.optimization_barrier((wide_own, *wide_half, *w_local, *x_all))[:3]
        near = [swap(mine, "shard", parts // 2, parts) for mine in wide_half]
        wide_core = swap(wide_own, "shard", 1, parts)

        segment = group_layout(lengths[0], counts[0], slots)
        seg_col = segment[:, None]
        seg_row = segment[None, :]
        own_vec = vec_w.astype(LOW).astype(HIGH)
        bias_local = jnp.concatenate(
            [own_vec[2], jnp.zeros((own_cols,), HIGH), own_vec[3]]
        )[:, None]

        a1, qkv, w_t, vectors = pl.pallas_call(
            functools.partial(project_kernel, parts),
            grid_spec=pltpu.PrefetchScalarGridSpec(
                num_scalar_prefetch=1,
                grid=(parts,),
                in_specs=[
                    *[pl.BlockSpec(memory_space=pl.ANY)] * parts,
                    *[whole(rows + 16, 3 * own_cols)] * parts,
                    whole(3 * own_cols, 1),
                ],
                out_specs=[
                    pl.BlockSpec((slots, width), lambda i, p: (p[0] ^ i, 0)),
                    pl.BlockSpec((3 * own_cols, slots), lambda i, p: (0, p[0] ^ i)),
                    whole(3 * own_cols, width),
                    whole(16, width),
                ],
                scratch_shapes=[
                    pltpu.VMEM((width, 3 * own_cols), HIGH),
                    pltpu.VMEM((parts, slots, width), LOW),
                    pltpu.SemaphoreType.DMA((parts,)),
                ],
            ),
            out_shape=[
                jax.ShapeDtypeStruct((total, width), LOW),
                jax.ShapeDtypeStruct((3 * own_cols, total), LOW),
                jax.ShapeDtypeStruct((3 * own_cols, width), LOW),
                jax.ShapeDtypeStruct((16, width), HIGH),
            ],
            compiler_params=params("arbitrary"),
            cost_estimate=cost(2 * total * width * 3 * own_cols * 3, 12e6),
            name="project",
        )(prefetch, *x_all, *w_local, bias_local)

        pair_flops = 2 * total * total * head_size * 4 // 2

        def head_specs(h):
            return [
                pl.BlockSpec((head_size, total), functools.partial(lambda k, *_: (k * own_heads + h, 0), k))
                for k in range(3)
            ]

        def attend(h, qkv):
            return pl.pallas_call(
                functools.partial(attend_kernel, scale),
                grid_spec=pltpu.PrefetchScalarGridSpec(
                    num_scalar_prefetch=1,
                    grid=(1,),
                    in_specs=head_specs(h) + [whole(total, 1), whole(1, total)],
                    out_specs=[whole(parts, head_size, slots), whole(1, total, 1)],
                    scratch_shapes=[pltpu.VMEM((total, head_size), LOW)],
                ),
                out_shape=[
                    jax.ShapeDtypeStruct((parts, head_size, slots), LOW),
                    jax.ShapeDtypeStruct((1, total, 1), HIGH),
                ],
                compiler_params=params("arbitrary"),
                cost_estimate=cost(2 * pair_flops, 4e6, total * total // 2),
                name="attend",
            )(prefetch, qkv, qkv, qkv, seg_col, seg_row)

        mixed, lse = [], []
        for h in range(own_heads):
            if h == 1:
                qkv, near[0] = lax.optimization_barrier((qkv, near[0]))
                far = [swap(near[0], "dp", 1, replicas)]
                turned = [swap(near[0], "shard", 1, parts)]
            head_mixed, head_lse = attend(h, qkv)
            mixed.append(head_mixed)
            lse.append(head_lse)
        near[1] = after(near[1], mixed[-1])
        far.append(swap(near[1], "dp", 1, replicas))
        mixed_own = deal(
            [jnp.concatenate([head[j] for head in mixed], axis=0) for j in range(parts)], parts
        )
        turned.append(swap(near[1], "shard", 1, parts))
        wide = [wide_own, wide_core]
        for k in range(2):
            wide += [near[k], far[k], turned[k], swap(far[k], "shard", 1, parts)]

        steps = blocks
        live_own = lax.dynamic_index_in_dim(counts[0], place, 0, keepdims=True)
        first_blocks = fc_rows // 2 * 2

        def grad_spec(k):
            first, last = ((0, first_blocks - 1), (first_blocks, steps - 1))[k]
            return pl.BlockSpec(
                (parts // 2, rows, width), lambda i, *_: (0, 0, jnp.clip(i, first, last) - first)
            )

        grad_columns = [first_blocks * width, (steps - first_blocks) * width]

        in_hbm = pl.BlockSpec(memory_space=pltpu.HBM)
        out = pl.pallas_call(
            functools.partial(mlp_kernel, parts, first_blocks),
            grid_spec=pltpu.PrefetchScalarGridSpec(
                num_scalar_prefetch=3,
                grid=(steps,),
                in_specs=[whole(slots, width), whole(slots, width), whole(16, width)]
                + [whole(own_cols, slots)] * parts
                + [in_hbm] * len(wide),
                out_specs=[whole(slots, width)]
                + [grad_spec(k) for k in range(2) for _ in range(2)]
                + [whole(slots, width), whole(16, width)]
                + [whole(own_cols, slots)] * parts,
                scratch_shapes=[
                    pltpu.VMEM((width, blocks * width), LOW),
                    pltpu.VMEM((width, slots), LOW),
                    pltpu.VMEM((slots, width), HIGH),
                    pltpu.VMEM((slots, width), LOW),
                    pltpu.VMEM((width, slots), LOW),
                    pltpu.VMEM((slots, width), LOW),
                    pltpu.VMEM((width, slots), LOW),
                    pltpu.VMEM((slots, width), HIGH),
                    pltpu.VMEM((slots, width), HIGH),
                    pltpu.VMEM((slots, width), LOW),
                    pltpu.SemaphoreType.DMA((2, 6)),
                ],
            ),
            out_shape=[jax.ShapeDtypeStruct((slots, width), LOW)]
            + [jax.ShapeDtypeStruct((parts // 2, rows, c), LOW) for c in grad_columns for _ in range(2)]
            + [jax.ShapeDtypeStruct((slots, width), HIGH), jax.ShapeDtypeStruct((16, width), HIGH)]
            + [jax.ShapeDtypeStruct((own_cols, slots), LOW)] * parts,
            compiler_params=params("arbitrary"),
            cost_estimate=cost(2 * slots * width * (6 * hidden + 3 * width), 30e6, slots * hidden),
            name="mlp",
        )(prefetch, side, live_own, tokens, cotangent, vectors, *mixed_own, *wide)
        block_out, keep_a, send_a, keep_b, send_b, grad_resid, mid_grads, *do_pieces = out

        do_own = deal(do_pieces, parts)
        got_a = swap(send_a, "shard", 1, parts)
        got_b = swap(send_b, "shard", 1, parts)
        own_a, other_a = [add_low(keep_a[n], got_a[n]) for n in range(2)]
        own_b, other_b = halve(add_low(keep_b, got_b), half, 1)
        *do_own, own_a, other_a, own_b, other_b = lax.optimization_barrier(
            (*do_own, own_a, other_a, own_b, other_b)
        )
        got_a = swap(other_a, "shard", parts // 2, parts)
        got_b = swap(other_b, "dp", 1, replicas)

        def attend_back(h, qkv):
            return pl.pallas_call(
                functools.partial(attend_back_kernel, scale),
                grid_spec=pltpu.PrefetchScalarGridSpec(
                    num_scalar_prefetch=1,
                    grid=(1,),
                    in_specs=head_specs(h)
                    + [whole(total, 1), whole(1, total), whole(1, total, 1)]
                    + [pl.BlockSpec((head_size, slots), lambda *_: (h, 0))] * parts,
                    out_specs=whole(3, head_size, total),
                    scratch_shapes=[
                        pltpu.VMEM((total, head_size), LOW),
                        pltpu.VMEM((parts, head_size, slots), LOW),
                        pltpu.VMEM((head_size, total), HIGH),
                        pltpu.VMEM((head_size, total), HIGH),
                    ],
                ),
                out_shape=jax.ShapeDtypeStruct((3, head_size, total), LOW),
                compiler_params=params("arbitrary"),
                cost_estimate=cost(
                    5 * pair_flops, 4e6, total * total // 2
                ),
                name="attend_back",
            )(prefetch, qkv, qkv, qkv, seg_col, seg_row, lse[h], *do_own)

        dqkv = [attend_back(h, qkv) for h in range(own_heads)]
        *dqkv, got_a, got_b = lax.optimization_barrier((*dqkv, got_a, got_b))
        own_a, other_a = halve(add_low(own_a, got_a), half, 0)
        got_a = swap(other_a, "dp", 1, replicas)
        own_b, other_b = [add_low(own_b[n], got_b[n]) for n in range(2)]
        got_b = swap(other_b, "shard", parts // 2, parts)
        dqkv[0] = after(dqkv[0], other_a, own_b, other_b)

        q_cols = 3 * own_cols
        extra = vec_w.shape[0]
        half_rows = rows // 2
        da1_keep, da1_send, own_q, other_q = pl.pallas_call(
            functools.partial(projection_back_kernel, own_heads, parts),
            grid_spec=pltpu.PrefetchScalarGridSpec(
                num_scalar_prefetch=2,
                grid=(parts,),
                in_specs=[
                    *[pl.BlockSpec(memory_space=pl.ANY)] * parts,
                    pl.BlockSpec((slots, width), lambda i, p, _: (p[0] ^ i, 0)),
                ]
                + [pl.BlockSpec((3, head_size, slots), lambda i, p, _: (0, 0, p[0] ^ i))] * own_heads
                + [whole(q_cols, width), whole(16, width), whole(16, width)],
                out_specs=[pl.BlockSpec((1, slots, width), lambda i, *_: (i // 2, 0, 0))] * 2
                + [whole(parts, half_rows, q_cols + extra)] * 2,
                scratch_shapes=[
                    pltpu.VMEM((q_cols, width), HIGH),
                    pltpu.VMEM((16, width), HIGH),
                    pltpu.VMEM((q_cols, 1), HIGH),
                    pltpu.VMEM((width, 16), HIGH),
                    pltpu.VMEM((width, q_cols + 64), HIGH),
                    pltpu.VMEM((parts, slots, width), LOW),
                    pltpu.SemaphoreType.DMA((parts,)),
                ],
            ),
            out_shape=[jax.ShapeDtypeStruct((parts // 2, slots, width), LOW)] * 2
            + [jax.ShapeDtypeStruct((parts, half_rows, q_cols + extra), LOW)] * 2,
            compiler_params=params("arbitrary"),
            cost_estimate=cost(4 * total * width * 3 * own_cols * 2, 16e6),
            name="projection_back",
        )(prefetch, side, *x_all, a1, *dqkv, w_t, vectors, mid_grads)

        share = rows // replicas
        z_bits = [bit for bit in (1 << n for n in range(1, 20)) if bit < replicas]
        last_event = [own_q]

        def seen(value):
            return lax.optimization_barrier((value, last_event[0]))[0]

        def event(value):
            last_event[0] = value
            return value

        def next_half(keep, got, bit, dim):
            array = event(add_low(keep, seen(got)))
            return scatter_half(array, dim, bit, replica, replicas)

        got_q = swap(other_q, "dp", 1, replicas)
        da1_got = swap(da1_send, "shard", 1, parts)
        state_a = next_half(own_a, got_a, z_bits[0], 0)
        state_b = next_half(own_b, got_b, z_bits[0], 0)
        for bit in z_bits[1:]:
            state_a = next_half(*state_a, bit, 0)
        state_q = next_half(own_q, got_q, z_bits[0], 1)
        for bit in z_bits[1:]:
            state_b = next_half(*state_b, bit, 0)
        part_a = event(add_low(state_a[0], seen(state_a[1])))
        for bit in z_bits[1:]:
            state_q = next_half(*state_q, bit, 1)
        part_b = event(add_low(state_b[0], seen(state_b[1])))
        part_ab = event(jnp.concatenate([part_a, part_b], axis=1))
        all_ab = lax.all_gather(part_ab, "dp", axis=0)
        part_q = event(add_low(state_q[0], seen(state_q[1])))

        def as_pair(value):
            high = lax.reduce_precision(value, 8, 7)
            return jnp.stack([high, value - high]).astype(LOW)

        main = part_q[:, :, :q_cols]
        squares = sum(jnp.sum(jnp.square(p.astype(HIGH))) for p in (part_ab, main))
        vec_parts = part_q[:, :, q_cols:].transpose(1, 0, 2).reshape(1, share, parts * extra)
        shared = jnp.concatenate(
            [vec_parts, jnp.broadcast_to(as_pair(squares), (1, share, 2))], axis=2
        )
        pieces = jnp.concatenate([main, jnp.broadcast_to(shared, (parts,) + shared.shape[1:])], axis=2)
        dealt = in_order(deal([pick(pieces, place ^ j) for j in range(parts)], parts), place, parts)
        q_rows = (
            dealt[:, :, :q_cols]
            .reshape(parts, share, 3, own_cols)
            .transpose(1, 2, 0, 3)
            .reshape(share, 3 * width)
        )
        summed = jnp.sum(dealt[:, :, q_cols:].astype(HIGH), axis=0)
        vec_parts = summed[:, : parts * extra].reshape(share, parts, extra).astype(LOW)
        squares = jnp.sum(summed[0, parts * extra :]) + jnp.sum(jnp.square(vec_parts.astype(HIGH)))
        vec_own = lax.dynamic_index_in_dim(vec_parts, place, 1, keepdims=False)
        near_q = jnp.concatenate(
            [q_rows, vec_own, jnp.broadcast_to(as_pair(squares), (share, 2))], axis=1
        )[None]
        for bit in z_bits[::-1]:
            near_q = jnp.concatenate([near_q, swap(near_q, "dp", bit, replicas)], axis=0)
        far_q = swap(near_q, "dp", 1, replicas)

        def block_of(index):
            block = index % 2
            for bit in z_bits:
                block = block * 2 + index // bit % 2
            return block

        def index_of(block):
            index = 0
            for bit in z_bits[::-1]:
                index = index + block % 2 * bit
                block = block // 2
            return index + block

        turn = block_of(replica)
        small = jnp.concatenate([near_q[:, :, 3 * width :], far_q[:, :, 3 * width :]], axis=0)
        small = jnp.stack([pick(small, turn ^ r) for r in range(replicas)]).astype(HIGH)
        summed_vec = small[:, :, :extra].reshape(rows, extra).T
        squares = jnp.sum(small[:, 0, extra:])

        own_da1 = da1_keep[0].astype(HIGH) + da1_got[0].astype(HIGH)
        da1 = own_da1 + swap(add_low(da1_keep[1], da1_got[1]), "shard", 2, parts).astype(HIGH)
        unit, inverse = normalize(tokens.astype(HIGH))
        grad_input = grad_resid + normalize_back(unit, inverse, da1 * vectors[0:1])
        live_rows = jnp.arange(slots, dtype=jnp.int32) < live_own[0]
        grad_in = jnp.where(live_rows[:, None], grad_input, 0.0).astype(LOW)

        norm_total = jnp.sqrt(squares)
        factor = jnp.minimum(1.0, CLIP_LIMIT / (norm_total + 1e-06))
        near_count = replicas // 2
        q_block = (1,) + near_q.shape[1:]

        def gathered_spec(array):
            return pl.BlockSpec((1,) + array.shape[1:], lambda i, _, p: (index_of(i ^ p[0]), 0, 0))

        attn_shape = (replicas, share, 4 * width)
        mlp_shape = (2, replicas, share, hidden)
        attn_spec = pl.BlockSpec((1, share, 4 * width), lambda i, _, p: (i ^ p[0], 0, 0))
        mlp_spec = pl.BlockSpec((2, 1, share, hidden), lambda i, _, p: (0, i ^ p[0], 0, 0))
        updated = pl.pallas_call(
            functools.partial(adam_kernel, fc_rows),
            grid_spec=pltpu.PrefetchScalarGridSpec(
                num_scalar_prefetch=2,
                grid=(replicas,),
                in_specs=[gathered_spec(all_ab)]
                + [
                    pl.BlockSpec(q_block, lambda i, *_: (jnp.minimum(i, near_count - 1), 0, 0)),
                    pl.BlockSpec(q_block, lambda i, *_: (jnp.maximum(i - near_count, 0), 0, 0)),
                ]
                + [attn_spec] * 3
                + [mlp_spec] * 3,
                out_specs=[attn_spec] * 4 + [mlp_spec] * 4,
            ),
            out_shape=[jax.ShapeDtypeStruct(attn_shape, HIGH)] * 4
            + [jax.ShapeDtypeStruct(mlp_shape, HIGH)] * 4,
            compiler_params=params("arbitrary"),
            cost_estimate=cost(30 * 9 * rows * width, 54e6),
            name="adam",
        )(
            factor.reshape(1),
            turn.reshape(1).astype(jnp.int32),
            all_ab,
            near_q,
            far_q,
            *[array.reshape(attn_shape) for array in (attn_w, attn_m, attn_v)],
            *[array.reshape(mlp_shape) for array in (mlp_w, mlp_m, mlp_v)],
        )
        attn_grad, attn_w_new, attn_m_new, attn_v_new = [u.reshape(attn_w.shape) for u in updated[:4]]
        mlp_grad, mlp_w_new, mlp_m_new, mlp_v_new = [u.reshape(mlp_w.shape) for u in updated[4:]]
        vec_grad, vec_w_new, vec_m_new, vec_v_new = adam_update(
            vec_w, vec_m, vec_v, summed_vec, factor, RATE_VECTOR, 0.0
        )
        return (
            block_out, grad_in, attn_grad, mlp_grad, vec_grad,
            attn_w_new, attn_m_new, attn_v_new, mlp_w_new, mlp_m_new, mlp_v_new,
            vec_w_new, vec_m_new, vec_v_new, norm_total.reshape(1),
        )

    return on_device


def solution(mesh):
    tokens = P(("dp", "shard"), None)
    groups = P("dp", None)
    attn = P("shard", None)
    mlp = P(None, "shard", None)
    vec = P(None, "shard")
    return jax.shard_map(
        make_on_device(mesh.shape["shard"], mesh.shape["dp"]),
        mesh=mesh,
        in_specs=(tokens, tokens, groups, groups) + (attn,) * 3 + (mlp,) * 3 + (vec,) * 3,
        out_specs=(tokens, tokens, attn, mlp, vec) + (attn,) * 3 + (mlp,) * 3 + (vec,) * 3 + (P(),),
        check_vma=False,
    )
```

```python
import functools

import jax
import jax.numpy as jnp
from jax import lax
from jax.experimental import pallas as pl
from jax.experimental.pallas import tpu as pltpu
from jax.sharding import PartitionSpec as P

HEADS = 12
STEP = 10
NORM_EPSILON = 1e-05
BETA_FIRST = 0.9
BETA_SECOND = 0.999
ADAM_EPSILON = 1e-08
RATE_MATRIX = 0.1
RATE_VECTOR = 0.2
DECAY_MATRIX = 0.1
CLIP_LIMIT = 1.0
MASKED_SCORE = -1e30
QUERY_BLOCK = 256
LOW = jnp.bfloat16
HIGH = jnp.float32


def dot_nn(a, b):
    return lax.dot_general(a, b, (((1,), (0,)), ((), ())), preferred_element_type=HIGH)


def dot_nt(a, b):
    return lax.dot_general(a, b, (((1,), (1,)), ((), ())), preferred_element_type=HIGH)


def low_t(a):
    return a.astype(HIGH).T.astype(LOW)


def normalize(features):
    centered = features - jnp.mean(features, axis=-1, keepdims=True)
    variance = jnp.mean(centered * centered, axis=-1, keepdims=True)
    inverse = lax.rsqrt(variance + NORM_EPSILON)
    return centered * inverse, inverse


def normalize_back(unit, inverse, grad_unit):
    first = jnp.mean(grad_unit, axis=-1, keepdims=True)
    second = jnp.mean(grad_unit * unit, axis=-1, keepdims=True)
    return inverse * (grad_unit - first - unit * second)


def cut_kernel(place, w_ref, vec_ref, *out_refs):
    parts = len(out_refs)
    rows, columns = w_ref.shape
    width = columns // 3
    cols = width // parts
    vec = vec_ref[...]
    tail = [
        jnp.concatenate([vec[3 * k + m : 3 * k + m + 1, :] for m in range(3)], axis=1)
        for k in range(vec.shape[0] // 3)
    ]
    tail.append(jnp.zeros((16 - len(tail), 3 * cols), HIGH))
    tail = jnp.concatenate(tail, axis=0).astype(LOW)
    for r in range(parts):
        starts = [k * width + r * cols for k in range(3)]
        piece = jnp.concatenate([w_ref[:, c : c + cols] for c in starts], axis=1).astype(LOW)
        for j in range(parts):

            @pl.when((place[0] ^ j) == r)
            def _():
                out_refs[j][:rows, :] = piece
                out_refs[j][rows:, :] = tail


def widen_kernel(half, out_ref, mlp_ref, wide_ref, *half_refs):
    rows, width = out_ref.shape
    start = pl.multiple_of(half[0] * (rows // 2), 16)
    near = pl.ds(start, rows // 2)
    sources = [(out_ref[...], out_ref[near, :])]
    for f in range(mlp_ref.shape[2] // width):
        span = slice(f * width, (f + 1) * width)
        sources += [(mlp_ref[n, :, span], mlp_ref[n, near, span]) for n in range(2)]
    split = half_refs[0].shape[1] // width
    for n, (block, part) in enumerate(sources):
        wide_ref[:, n * width : (n + 1) * width] = block.astype(LOW)
        k = int(n >= split)
        at = (n - k * split) * width
        half_refs[k][:, at : at + width] = part.astype(LOW)


def project_kernel(parts, place, *refs):
    x_refs, w_refs, refs = refs[:parts], refs[parts : 2 * parts], refs[2 * parts :]
    bias_ref, a1_ref, qkv_ref, wt_ref, vec_ref, w_scr, x_scr, sems = refs
    step = pl.program_id(0)
    rows = vec_ref.shape[1] // parts

    def copy(j):
        return pltpu.make_async_copy(x_refs[j], x_scr.at[j], sems.at[j])

    @pl.when(step == 0)
    def _():
        for j in range(parts):
            copy(j).start()
        vec_ref[...] = jnp.zeros_like(vec_ref)
        for j in range(parts):
            start = pl.multiple_of((place[0] ^ j) * rows, 16)
            w_scr[pl.ds(start, rows), :] = w_refs[j][:rows, :].astype(HIGH)
            tail = w_refs[j][rows:, :].astype(HIGH)
            for r in range(parts):

                @pl.when((place[0] ^ j) == r)
                def _():
                    for n in range(12):
                        piece = tail[n // 3 : n // 3 + 1, n % 3 * rows : (n % 3 + 1) * rows]
                        vec_ref[n : n + 1, r * rows : (r + 1) * rows] = piece

        wt_ref[...] = w_scr[...].T.astype(LOW)

    for j in range(parts):

        @pl.when(step == j)
        def _():
            copy(j).wait()

    unit, _ = normalize(x_scr[step].astype(HIGH))
    a1 = (unit * vec_ref[0:1, :] + vec_ref[1:2, :]).astype(LOW)
    a1_ref[...] = a1
    qkv_ref[...] = (dot_nt(wt_ref[...], a1) + bias_ref[...]).astype(LOW)


def masked_scores(q, kt, seg_q, seg_k, start):
    block = q.shape[0]
    out = []
    if start:
        s = dot_nn(q, kt[:, :start])
        out.append(jnp.where(seg_q == seg_k[:, :start], s, MASKED_SCORE))
    s = dot_nn(q, kt[:, start : start + block])
    row = lax.broadcasted_iota(jnp.int32, (block, block), 0)
    col = lax.broadcasted_iota(jnp.int32, (block, block), 1)
    allowed = (seg_q == seg_k[:, start : start + block]) & (col <= row)
    out.append(jnp.where(allowed, s, MASKED_SCORE))
    return out


def attend_kernel(scale, place, qt_ref, kt_ref, vt_ref, segc_ref, segr_ref, o_ref, lse_ref, v_scr):
    total = qt_ref.shape[1]
    per_part = o_ref.shape[2]
    block = min(QUERY_BLOCK, per_part)
    v_scr[...] = low_t(vt_ref[...])
    for start in range(0, total, block):
        span = slice(start, start + block)
        q = (qt_ref[:, span].astype(HIGH) * scale).T.astype(LOW)
        pieces = masked_scores(q, kt_ref, segc_ref[span, :], segr_ref, start)
        top = functools.reduce(jnp.maximum, [jnp.max(s, axis=1, keepdims=True) for s in pieces])
        weights = [jnp.exp(s - top) for s in pieces]
        mass = sum(jnp.sum(w, axis=1, keepdims=True) for w in weights)
        lse_ref[0, span, :] = top + jnp.log(mass)
        inverse = 1.0 / mass
        mixed = dot_nn((weights[-1] * inverse).astype(LOW), v_scr[span, :])
        if start:
            mixed += dot_nn((weights[0] * inverse).astype(LOW), v_scr[:start, :])
        inner = start % per_part
        o_ref[place[0] ^ (start // per_part), :, inner : inner + block] = mixed.T.astype(LOW)


def attend_back_kernel(
    scale, place, qt_ref, kt_ref, vt_ref, segc_ref, segr_ref, lse_ref, *refs
):
    *do_refs, out_ref, k_scr, do_scr, dk_scr, dv_scr = refs
    total = qt_ref.shape[1]
    parts, per_part = len(do_refs), do_refs[0].shape[1]
    block = min(QUERY_BLOCK, per_part)
    k_scr[...] = low_t(kt_ref[...])
    for j in range(parts):
        do_scr[place[0] ^ j] = do_refs[j][...]
    dk_scr[...] = jnp.zeros_like(dk_scr)
    dv_scr[...] = jnp.zeros_like(dv_scr)
    for start in range(0, total, block):
        span = slice(start, start + block)
        inner = start % per_part
        qt = qt_ref[:, span].astype(HIGH) * scale
        dot_ = do_scr[start // per_part, :, inner : inner + block]
        q = qt.T.astype(LOW)
        qt = qt.astype(LOW)
        do = low_t(dot_)
        pieces = masked_scores(q, kt_ref, segc_ref[span, :], segr_ref, start)
        spans = [slice(0, start), span] if start else [span]
        lse = lse_ref[0, span, :]
        weights = [jnp.exp(s - lse) for s in pieces]
        grads = [dot_nn(do, vt_ref[:, at]) for at in spans]
        delta = sum(jnp.sum(g * w, axis=1, keepdims=True) for g, w in zip(grads, weights))
        dq = None
        for at, w, g in zip(spans, weights, grads):
            ds = (w * (g - delta)).astype(LOW)
            term = dot_nn(ds, k_scr[at, :])
            dq = term if dq is None else dq + term
            dk_scr[:, at] += dot_nn(qt, ds)
            dv_scr[:, at] += dot_nn(dot_, w.astype(LOW))
        out_ref[0, :, span] = (dq * scale).T.astype(LOW)
    out_ref[1] = dk_scr[...].astype(LOW)
    out_ref[2] = dv_scr[...].astype(LOW)


def projection_back_kernel(heads, parts, place, half, *refs):
    x_refs, (a1_ref, *refs) = refs[:parts], refs[parts:]
    head_refs, refs = refs[:heads], refs[heads:]
    wt_ref, vec_ref, grads_ref, keep_ref, send_ref, qkeep_ref, qsend_ref, *scratch = refs
    g_scr, vec_scr, sums_scr, ext_scr, all_scr, x_scr, sems = scratch
    step = pl.program_id(0)
    cols = g_scr.shape[0] // 3
    extra = grads_ref.shape[0]
    count = qkeep_ref.shape[2] - 3 * cols

    def copy(j):
        return pltpu.make_async_copy(x_refs[j], x_scr.at[j], sems.at[j])

    @pl.when(step == 0)
    def _():
        for j in range(parts):
            copy(j).start()
        g_scr[...] = jnp.zeros_like(g_scr)
        vec_scr[...] = grads_ref[...]
        sums_scr[...] = jnp.zeros_like(sums_scr)

    for j in range(parts):

        @pl.when(step == j)
        def _():
            copy(j).wait()

    dqkv = jnp.concatenate([ref[k] for k in range(3) for ref in head_refs], axis=0)
    da1 = dot_nn(low_t(dqkv), wt_ref[...])

    @pl.when(step % 2 == 0)
    def _():
        keep_ref[0] = da1.astype(LOW)

    @pl.when(step % 2 == 1)
    def _():
        send_ref[0] = da1.astype(LOW)

    g_scr[...] += dot_nn(dqkv, a1_ref[...])
    unit, _ = normalize(x_scr[step].astype(HIGH))
    vec_scr[0:1, :] += jnp.sum(da1 * unit, axis=0, keepdims=True)
    vec_scr[1:2, :] += jnp.sum(da1, axis=0, keepdims=True)
    sums_scr[...] += jnp.sum(dqkv.astype(HIGH), axis=1, keepdims=True)

    @pl.when(step == pl.num_programs(0) - 1)
    def _():
        ext_scr[...] = vec_scr[...].T
        own = pl.ds(pl.multiple_of(place[0] * cols, 16), cols)
        ext_scr[own, 2:3] = sums_scr[:cols, :]
        ext_scr[own, 3:4] = sums_scr[2 * cols :, :]
        all_scr[:, : 3 * cols] = g_scr[...].T
        all_scr[:, 3 * cols : 3 * cols + extra] = ext_scr[...]
        rows = all_scr.shape[0] // parts
        for r in range(parts):
            for ref, side in ((qkeep_ref, half[0]), (qsend_ref, 1 - half[0])):
                start = pl.multiple_of(r * rows + side * (rows // 2), 16)
                ref[r] = all_scr[pl.ds(start, rows // 2), : 3 * cols + count].astype(LOW)


GELU_C = 0.7978845608028654
GELU_A = 0.044715


def mlp_kernel(
    parts, first_blocks, place, half, live_ref, x_ref, cot_ref, vec_ref, *refs
):
    o_refs, refs = refs[:parts], refs[parts:]
    own_ref, core_ref, *wide_refs = refs[:10]
    out_ref, *grad_refs = refs[10:15]
    dr1_ref, vecg_ref, *refs = refs[15:]
    do_refs, scratch = refs[:parts], refs[parts:]
    wide, ot_scr, r1_scr, a2_scr, a2t_scr, dy_scr, dyt_scr, y_scr, da2_scr, act_scr, sems = scratch
    step = pl.program_id(0)
    rows = o_refs[0].shape[0]
    slots, width = x_ref.shape
    bo, gain, shift, bp = (vec_ref[r : r + 1, :] for r in (4, 5, 6, 11))
    split = wide_refs[0].shape[1]
    live = lax.broadcasted_iota(jnp.int32, (slots, 1), 0) < live_ref[0]

    def copies(k):
        half_rows = rows // 2
        near, far = half[0] * half_rows, (1 - half[0]) * half_rows
        span = slice(0, split) if k == 0 else slice(split, wide.shape[1])
        sources = [(own_ref.at[:, span], 0, 0), (core_ref.at[:, span], 1, 0)]
        spots = [(2, near), (2, far), (3, near), (3, far)]
        sources += [(wide_refs[4 * k + n], *spot) for n, spot in enumerate(spots)]
        for n, (source, j, offset) in enumerate(sources):
            start = pl.multiple_of((place[0] ^ j) * rows + offset, 16)
            target = wide.at[pl.ds(start, source.shape[0]), span]
            yield pltpu.make_async_copy(source, target, sems.at[k, n])

    def block(n):
        return wide[:, pl.ds(pl.multiple_of(n * width, 128), width)]

    def permuted(scratch, value):
        for j in range(parts):
            scratch[j * rows : (j + 1) * rows, :] = value(pl.multiple_of((place[0] ^ j) * rows, 16))

    def put(value):
        value = value.astype(LOW)
        for k in range(2):

            @pl.when((step >= first_blocks) == bool(k))
            def _():
                keep, send = grad_refs[2 * k : 2 * k + 2]
                for j in range(parts):
                    (send if j % 2 else keep)[j // 2] = value[j * rows : (j + 1) * rows, :]

    @pl.when(step == 0)
    def _():
        for k in range(2):
            for copy in copies(k):
                copy.start()
        for j in range(parts):
            start = pl.multiple_of((place[0] ^ j) * rows, 16)
            ot_scr[pl.ds(start, rows), :] = o_refs[j][...]
        mixed = low_t(ot_scr[...])
        dy = jnp.where(live, cot_ref[...].astype(HIGH), 0.0)
        dy_scr[...] = dy.astype(LOW)
        ot_scr[...] = dy.T.astype(LOW)
        permuted(dyt_scr, lambda start: ot_scr[pl.ds(start, rows), :])
        for copy in copies(0):
            copy.wait()
        r1 = x_ref[...].astype(HIGH) + dot_nn(mixed, wide[:, :width]) + bo
        r1_scr[...] = r1
        unit, _ = normalize(r1)
        a2 = unit * gain + shift
        a2_scr[...] = a2.astype(LOW)
        ot_scr[...] = a2.T.astype(LOW)
        permuted(a2t_scr, lambda start: ot_scr[pl.ds(start, rows), :])
        vecg_ref[...] = jnp.zeros_like(vecg_ref)
        vecg_ref[11:12, :] = jnp.sum(dy, axis=0, keepdims=True)
        y_scr[...] = r1 + bp
        da2_scr[...] = jnp.zeros_like(da2_scr)

    @pl.when(step == first_blocks)
    def _():
        for copy in copies(1):
            copy.wait()

    last = pl.num_programs(0) - 1

    @pl.when((step < last) & (step % 2 == 0))
    def _():
        w_fc, w_pt = block(1 + step), block(2 + step)
        u = dot_nn(a2_scr[...], w_fc) + vec_ref[pl.ds(7 + step // 2, 1), :]
        square = u * u
        t = jnp.tanh(GELU_C * (u + GELU_A * (square * u)))
        grown = 0.5 * (1.0 + t)
        act = (u * grown).astype(LOW)
        act_scr[...] = act
        y_scr[...] += dot_nt(act, w_pt)
        slope = grown + 0.5 * u * (1.0 - t * t) * (GELU_C + (3.0 * GELU_C * GELU_A) * square)
        du = (dot_nn(dy_scr[...], w_pt) * slope).astype(LOW)
        vecg_ref[pl.ds(7 + step // 2, 1), :] = jnp.sum(du.astype(HIGH), axis=0, keepdims=True)
        da2_scr[...] += dot_nt(du, w_fc)
        put(dot_nn(a2t_scr[...], du))

    @pl.when((step < last) & (step % 2 == 1))
    def _():
        put(dot_nn(dyt_scr[...], act_scr[...]))

    @pl.when(step == last)
    def _():
        out_ref[...] = jnp.where(live, y_scr[...], 0.0).astype(LOW)
        unit, inverse = normalize(r1_scr[...])
        da2 = da2_scr[...]
        vecg_ref[5:6, :] = jnp.sum(da2 * unit, axis=0, keepdims=True)
        vecg_ref[6:7, :] = jnp.sum(da2, axis=0, keepdims=True)
        dr1 = dy_scr[...].astype(HIGH) + normalize_back(unit, inverse, da2 * gain)
        dr1_ref[...] = dr1
        low = dr1.astype(LOW)
        vecg_ref[4:5, :] = jnp.sum(low.astype(HIGH), axis=0, keepdims=True)
        put(dot_nn(jnp.concatenate([ref[...] for ref in o_refs], axis=0), low))
        for j in range(parts):
            start = pl.multiple_of((place[0] ^ j) * rows, 16)
            do_refs[j][...] = dot_nt(wide[pl.ds(start, rows), :width], low).astype(LOW)


def group_layout(length_row, count_row, slots):
    starts = jnp.cumsum(count_row) - count_row
    within = jnp.arange(slots, dtype=jnp.int32)
    position = (starts[:, None] + within[None, :]).reshape(-1)
    live_rows = (within[None, :] < count_row[:, None]).reshape(-1)
    boundary = jnp.cumsum(length_row)
    segment = jnp.sum((position[:, None] >= boundary[None, :]).astype(jnp.int32), axis=1)
    buffer_slot = jnp.arange(position.shape[0], dtype=jnp.int32)
    return jnp.where(live_rows, segment, -1 - buffer_slot)


def adam_update(master, first, second, gradient, factor, rate, decay):
    clipped = gradient * factor
    first_new = BETA_FIRST * first + (1.0 - BETA_FIRST) * clipped
    second_new = BETA_SECOND * second + (1.0 - BETA_SECOND) * clipped * clipped
    first_hat = first_new / (1.0 - BETA_FIRST**STEP)
    second_hat = second_new / (1.0 - BETA_SECOND**STEP)
    master_new = master - rate * (
        first_hat / (jnp.sqrt(second_hat) + ADAM_EPSILON) + decay * master
    )
    return (clipped, master_new, first_new, second_new)


def adam_kernel(fc_rows, factor_ref, _, *refs):
    grads, states, outs = refs[:3], refs[3:9], refs[9:]
    near = pl.program_id(0) < pl.num_programs(0) // 2
    factor = factor_ref[0]
    width = outs[0].shape[-1] // fc_rows
    qkv = jnp.where(near, grads[1][0], grads[2][0])[:, : 3 * width]

    def update(gradient, at, base):
        results = adam_update(
            *[states[base + n][at] for n in range(3)],
            gradient.astype(HIGH), factor, RATE_MATRIX, DECAY_MATRIX,
        )
        for n, result in enumerate(results):
            outs[base // 3 * 4 + n][at] = result

    blocks = [grads[0][0, :, n : n + width] for n in range(0, grads[0].shape[2], width)]
    for f in range(fc_rows):
        span = slice(f * width, (f + 1) * width)
        for n in range(2):
            update(blocks[2 * f + n], (n, 0, slice(None), span), 3)
    update(qkv, (0, slice(None), slice(0, 3 * width)), 0)
    update(blocks[-1], (0, slice(None), slice(3 * width, 4 * width)), 0)


def swap(array, axis, bit, count):
    return lax.ppermute(array, axis, [(i, i ^ bit) for i in range(count)])


def pick(array, index):
    return lax.dynamic_index_in_dim(array, index, 0, keepdims=False)


def deal(pieces, parts):
    return list(pieces[:1]) + [swap(pieces[j], "shard", j, parts) for j in range(1, parts)]


def in_order(relative, place, parts):
    relative = jnp.stack(relative)
    return jnp.stack([pick(relative, place ^ r) for r in range(parts)])


def collect(own, parts):
    have = [own]
    bit = parts // 2
    slots = [0]
    while bit:
        have = have + [swap(piece, "shard", bit, parts) for piece in have]
        slots = slots + [s ^ bit for s in slots]
        bit //= 2
    return [have[slots.index(j)] for j in range(parts)]


def after(value, *others):
    return lax.optimization_barrier((value, *others))[0]


def add_low(a, b):
    return (a.astype(HIGH) + b.astype(HIGH)).astype(LOW)


def bits_of(count):
    return [1 << n for n in range(count.bit_length() - 1)]


def halve(array, upper, dim):
    length = array.shape[dim] // 2
    keep = lax.dynamic_slice_in_dim(array, upper * length, length, dim)
    return keep, lax.dynamic_slice_in_dim(array, (1 - upper) * length, length, dim)


def scatter_half(array, dim, bit, replica, replicas):
    keep, send = halve(array, (replica // bit) % 2, dim)
    return keep, swap(send, "dp", bit, replicas)


def params(mebibytes):
    return pltpu.CompilerParams(
        dimension_semantics=("arbitrary",), vmem_limit_bytes=mebibytes * 1024 * 1024
    )


def cost(flops, moved, special=0):
    return pl.CostEstimate(flops=int(flops), bytes_accessed=int(moved), transcendentals=int(special))


def whole(*shape):
    zeros = (0,) * len(shape)
    return pl.BlockSpec(shape, lambda *_: zeros)


def make_on_device(parts, replicas):
    def on_device(
        tokens, cotangent, lengths, counts,
        attn_w, attn_m, attn_v, mlp_w, mlp_m, mlp_v, vec_w, vec_m, vec_v,
    ):
        slots, width = tokens.shape
        rows = attn_w.shape[0]
        hidden = mlp_w.shape[2]
        fc_rows = hidden // width
        total = parts * slots
        head_size = width // HEADS
        own_heads = HEADS // parts
        own_cols = own_heads * head_size
        scale = head_size ** (-0.5)
        place = lax.axis_index("shard")
        replica = lax.axis_index("dp")
        prefetch = place.reshape(1).astype(jnp.int32)

        half = replica % 2
        side = half.reshape(1).astype(jnp.int32)

        x_all = collect(tokens, parts)
        w_pieces = pl.pallas_call(
            cut_kernel,
            grid_spec=pltpu.PrefetchScalarGridSpec(
                num_scalar_prefetch=1,
                grid=(1,),
                in_specs=[whole(rows, 3 * width), whole(vec_w.shape[0], rows)],
                out_specs=[whole(rows + 16, 3 * own_cols)] * parts,
            ),
            out_shape=[jax.ShapeDtypeStruct((rows + 16, 3 * own_cols), LOW)] * parts,
            compiler_params=params(12),
            cost_estimate=cost(0, 4e6),
            name="cut",
        )(prefetch, attn_w, vec_w)
        w_local = deal(w_pieces, parts)

        blocks = 2 * fc_rows + 1
        split = (fc_rows // 2 * 2 + 1) * width
        wide_own, *wide_half = pl.pallas_call(
            widen_kernel,
            grid_spec=pltpu.PrefetchScalarGridSpec(
                num_scalar_prefetch=1,
                grid=(1,),
                in_specs=[
                    pl.BlockSpec((rows, width), lambda *_: (0, 3)),
                    whole(2, rows, hidden),
                ],
                out_specs=[
                    whole(rows, blocks * width),
                    whole(rows // 2, split),
                    whole(rows // 2, blocks * width - split),
                ],
            ),
            out_shape=[
                jax.ShapeDtypeStruct((rows, blocks * width), LOW),
                jax.ShapeDtypeStruct((rows // 2, split), LOW),
                jax.ShapeDtypeStruct((rows // 2, blocks * width - split), LOW),
            ],
            compiler_params=params(28),
            cost_estimate=cost(0, 12e6),
            name="widen",
        )(side, attn_w, mlp_w)
        wide_own, *wide_half = lax.optimization_barrier((wide_own, *wide_half, *w_local, *x_all))[:3]
        near = [swap(mine, "shard", parts // 2, parts) for mine in wide_half]
        wide_core = swap(wide_own, "shard", 1, parts)

        segment = group_layout(lengths[0], counts[0], slots)
        seg_col = segment[:, None]
        seg_row = segment[None, :]
        own_vec = vec_w.astype(LOW).astype(HIGH)
        bias_local = jnp.concatenate(
            [own_vec[2], jnp.zeros((own_cols,), HIGH), own_vec[3]]
        )[:, None]

        a1, qkv, w_t, vectors = pl.pallas_call(
            functools.partial(project_kernel, parts),
            grid_spec=pltpu.PrefetchScalarGridSpec(
                num_scalar_prefetch=1,
                grid=(parts,),
                in_specs=[
                    *[pl.BlockSpec(memory_space=pl.ANY)] * parts,
                    *[whole(rows + 16, 3 * own_cols)] * parts,
                    whole(3 * own_cols, 1),
                ],
                out_specs=[
                    pl.BlockSpec((slots, width), lambda i, p: (p[0] ^ i, 0)),
                    pl.BlockSpec((3 * own_cols, slots), lambda i, p: (0, p[0] ^ i)),
                    whole(3 * own_cols, width),
                    whole(16, width),
                ],
                scratch_shapes=[
                    pltpu.VMEM((width, 3 * own_cols), HIGH),
                    pltpu.VMEM((parts, slots, width), LOW),
                    pltpu.SemaphoreType.DMA((parts,)),
                ],
            ),
            out_shape=[
                jax.ShapeDtypeStruct((total, width), LOW),
                jax.ShapeDtypeStruct((3 * own_cols, total), LOW),
                jax.ShapeDtypeStruct((3 * own_cols, width), LOW),
                jax.ShapeDtypeStruct((16, width), HIGH),
            ],
            compiler_params=params(24),
            cost_estimate=cost(2 * total * width * 3 * own_cols * 3, 12e6),
            name="project",
        )(prefetch, *x_all, *w_local, bias_local)

        pair_flops = 2 * total * total * head_size * 4 // 2

        def head_specs(h):
            return [
                pl.BlockSpec((head_size, total), functools.partial(lambda k, *_: (k * own_heads + h, 0), k))
                for k in range(3)
            ]

        def attend(h, qkv):
            return pl.pallas_call(
                functools.partial(attend_kernel, scale),
                grid_spec=pltpu.PrefetchScalarGridSpec(
                    num_scalar_prefetch=1,
                    grid=(1,),
                    in_specs=head_specs(h) + [whole(total, 1), whole(1, total)],
                    out_specs=[whole(parts, head_size, slots), whole(1, total, 1)],
                    scratch_shapes=[pltpu.VMEM((total, head_size), LOW)],
                ),
                out_shape=[
                    jax.ShapeDtypeStruct((parts, head_size, slots), LOW),
                    jax.ShapeDtypeStruct((1, total, 1), HIGH),
                ],
                compiler_params=params(24),
                cost_estimate=cost(2 * pair_flops, 4e6, total * total // 2),
                name="attend",
            )(prefetch, qkv, qkv, qkv, seg_col, seg_row)

        mixed, lse = [], []
        for h in range(own_heads):
            if h == 1:
                qkv, near[0] = lax.optimization_barrier((qkv, near[0]))
                far = [swap(near[0], "dp", 1, replicas)]
                turned = [swap(near[0], "shard", 1, parts)]
            head_mixed, head_lse = attend(h, qkv)
            mixed.append(head_mixed)
            lse.append(head_lse)
        near[1] = after(near[1], mixed[-1])
        far.append(swap(near[1], "dp", 1, replicas))
        mixed_own = deal(
            [jnp.concatenate([head[j] for head in mixed], axis=0) for j in range(parts)], parts
        )
        turned.append(swap(near[1], "shard", 1, parts))
        wide = [wide_own, wide_core]
        for k in range(2):
            wide += [near[k], far[k], turned[k], swap(far[k], "shard", 1, parts)]

        steps = blocks
        live_own = lax.dynamic_index_in_dim(counts[0], place, 0, keepdims=True)
        first_blocks = fc_rows // 2 * 2

        def grad_spec(k):
            first, last = ((0, first_blocks - 1), (first_blocks, steps - 1))[k]
            return pl.BlockSpec(
                (parts // 2, rows, width), lambda i, *_: (0, 0, jnp.clip(i, first, last) - first)
            )

        grad_columns = [first_blocks * width, (steps - first_blocks) * width]

        in_hbm = pl.BlockSpec(memory_space=pltpu.HBM)
        out = pl.pallas_call(
            functools.partial(mlp_kernel, parts, first_blocks),
            grid_spec=pltpu.PrefetchScalarGridSpec(
                num_scalar_prefetch=3,
                grid=(steps,),
                in_specs=[whole(slots, width), whole(slots, width), whole(16, width)]
                + [whole(own_cols, slots)] * parts
                + [in_hbm] * len(wide),
                out_specs=[whole(slots, width)]
                + [grad_spec(k) for k in range(2) for _ in range(2)]
                + [whole(slots, width), whole(16, width)]
                + [whole(own_cols, slots)] * parts,
                scratch_shapes=[
                    pltpu.VMEM((width, blocks * width), LOW),
                    pltpu.VMEM((width, slots), LOW),
                    pltpu.VMEM((slots, width), HIGH),
                    pltpu.VMEM((slots, width), LOW),
                    pltpu.VMEM((width, slots), LOW),
                    pltpu.VMEM((slots, width), LOW),
                    pltpu.VMEM((width, slots), LOW),
                    pltpu.VMEM((slots, width), HIGH),
                    pltpu.VMEM((slots, width), HIGH),
                    pltpu.VMEM((slots, width), LOW),
                    pltpu.SemaphoreType.DMA((2, 6)),
                ],
            ),
            out_shape=[jax.ShapeDtypeStruct((slots, width), LOW)]
            + [jax.ShapeDtypeStruct((parts // 2, rows, c), LOW) for c in grad_columns for _ in range(2)]
            + [jax.ShapeDtypeStruct((slots, width), HIGH), jax.ShapeDtypeStruct((16, width), HIGH)]
            + [jax.ShapeDtypeStruct((own_cols, slots), LOW)] * parts,
            compiler_params=params(50),
            cost_estimate=cost(2 * slots * width * (6 * hidden + 3 * width), 30e6, slots * hidden),
            name="mlp",
        )(prefetch, side, live_own, tokens, cotangent, vectors, *mixed_own, *wide)
        block_out, keep_a, send_a, keep_b, send_b, grad_resid, mid_grads, *do_pieces = out

        do_own = deal(do_pieces, parts)
        got_a = swap(send_a, "shard", 1, parts)
        got_b = swap(send_b, "shard", 1, parts)
        own_a, other_a = [add_low(keep_a[n], got_a[n]) for n in range(2)]
        own_b, other_b = halve(add_low(keep_b, got_b), half, 1)
        *do_own, own_a, other_a, own_b, other_b = lax.optimization_barrier(
            (*do_own, own_a, other_a, own_b, other_b)
        )
        got_a = swap(other_a, "shard", parts // 2, parts)
        got_b = swap(other_b, "dp", 1, replicas)

        def attend_back(h, qkv):
            return pl.pallas_call(
                functools.partial(attend_back_kernel, scale),
                grid_spec=pltpu.PrefetchScalarGridSpec(
                    num_scalar_prefetch=1,
                    grid=(1,),
                    in_specs=head_specs(h)
                    + [whole(total, 1), whole(1, total), whole(1, total, 1)]
                    + [pl.BlockSpec((head_size, slots), lambda *_: (h, 0))] * parts,
                    out_specs=whole(3, head_size, total),
                    scratch_shapes=[
                        pltpu.VMEM((total, head_size), LOW),
                        pltpu.VMEM((parts, head_size, slots), LOW),
                        pltpu.VMEM((head_size, total), HIGH),
                        pltpu.VMEM((head_size, total), HIGH),
                    ],
                ),
                out_shape=jax.ShapeDtypeStruct((3, head_size, total), LOW),
                compiler_params=params(28),
                cost_estimate=cost(
                    5 * pair_flops, 4e6, total * total // 2
                ),
                name="attend_back",
            )(prefetch, qkv, qkv, qkv, seg_col, seg_row, lse[h], *do_own)

        dqkv = [attend_back(h, qkv) for h in range(own_heads)]
        *dqkv, got_a, got_b = lax.optimization_barrier((*dqkv, got_a, got_b))
        own_a, other_a = halve(add_low(own_a, got_a), half, 0)
        got_a = swap(other_a, "dp", 1, replicas)
        own_b, other_b = [add_low(own_b[n], got_b[n]) for n in range(2)]
        got_b = swap(other_b, "shard", parts // 2, parts)
        dqkv[0] = after(dqkv[0], other_a, own_b, other_b)

        q_cols = 3 * own_cols
        extra = vec_w.shape[0]
        half_rows = rows // 2
        da1_keep, da1_send, own_q, other_q = pl.pallas_call(
            functools.partial(projection_back_kernel, own_heads, parts),
            grid_spec=pltpu.PrefetchScalarGridSpec(
                num_scalar_prefetch=2,
                grid=(parts,),
                in_specs=[
                    *[pl.BlockSpec(memory_space=pl.ANY)] * parts,
                    pl.BlockSpec((slots, width), lambda i, p, _: (p[0] ^ i, 0)),
                ]
                + [pl.BlockSpec((3, head_size, slots), lambda i, p, _: (0, 0, p[0] ^ i))] * own_heads
                + [whole(q_cols, width), whole(16, width), whole(16, width)],
                out_specs=[pl.BlockSpec((1, slots, width), lambda i, *_: (i // 2, 0, 0))] * 2
                + [whole(parts, half_rows, q_cols + extra)] * 2,
                scratch_shapes=[
                    pltpu.VMEM((q_cols, width), HIGH),
                    pltpu.VMEM((16, width), HIGH),
                    pltpu.VMEM((q_cols, 1), HIGH),
                    pltpu.VMEM((width, 16), HIGH),
                    pltpu.VMEM((width, q_cols + 64), HIGH),
                    pltpu.VMEM((parts, slots, width), LOW),
                    pltpu.SemaphoreType.DMA((parts,)),
                ],
            ),
            out_shape=[jax.ShapeDtypeStruct((parts // 2, slots, width), LOW)] * 2
            + [jax.ShapeDtypeStruct((parts, half_rows, q_cols + extra), LOW)] * 2,
            compiler_params=params(28),
            cost_estimate=cost(4 * total * width * 3 * own_cols * 2, 16e6),
            name="projection_back",
        )(prefetch, side, *x_all, a1, *dqkv, w_t, vectors, mid_grads)

        share = rows // replicas
        z_bits = [bit for bit in (1 << n for n in range(1, 20)) if bit < replicas]
        last_event = [own_q]

        def seen(value):
            return lax.optimization_barrier((value, last_event[0]))[0]

        def event(value):
            last_event[0] = value
            return value

        def next_half(keep, got, bit, dim):
            array = event(add_low(keep, seen(got)))
            return scatter_half(array, dim, bit, replica, replicas)

        got_q = swap(other_q, "dp", 1, replicas)
        da1_got = swap(da1_send, "shard", 1, parts)
        state_a = next_half(own_a, got_a, z_bits[0], 0)
        state_b = next_half(own_b, got_b, z_bits[0], 0)
        for bit in z_bits[1:]:
            state_a = next_half(*state_a, bit, 0)
        state_q = next_half(own_q, got_q, z_bits[0], 1)
        for bit in z_bits[1:]:
            state_b = next_half(*state_b, bit, 0)
        part_a = event(add_low(state_a[0], seen(state_a[1])))
        for bit in z_bits[1:]:
            state_q = next_half(*state_q, bit, 1)
        part_b = event(add_low(state_b[0], seen(state_b[1])))
        part_ab = event(jnp.concatenate([part_a, part_b], axis=1))
        all_ab = lax.all_gather(part_ab, "dp", axis=0)
        part_q = event(add_low(state_q[0], seen(state_q[1])))

        def as_pair(value):
            high = lax.reduce_precision(value, 8, 7)
            return jnp.stack([high, value - high]).astype(LOW)

        main = part_q[:, :, :q_cols]
        squares = sum(jnp.sum(jnp.square(p.astype(HIGH))) for p in (part_ab, main))
        vec_parts = part_q[:, :, q_cols:].transpose(1, 0, 2).reshape(1, share, parts * extra)
        shared = jnp.concatenate(
            [vec_parts, jnp.broadcast_to(as_pair(squares), (1, share, 2))], axis=2
        )
        pieces = jnp.concatenate([main, jnp.broadcast_to(shared, (parts,) + shared.shape[1:])], axis=2)
        dealt = in_order(deal([pick(pieces, place ^ j) for j in range(parts)], parts), place, parts)
        q_rows = (
            dealt[:, :, :q_cols]
            .reshape(parts, share, 3, own_cols)
            .transpose(1, 2, 0, 3)
            .reshape(share, 3 * width)
        )
        summed = jnp.sum(dealt[:, :, q_cols:].astype(HIGH), axis=0)
        vec_parts = summed[:, : parts * extra].reshape(share, parts, extra).astype(LOW)
        squares = jnp.sum(summed[0, parts * extra :]) + jnp.sum(jnp.square(vec_parts.astype(HIGH)))
        vec_own = lax.dynamic_index_in_dim(vec_parts, place, 1, keepdims=False)
        near_q = jnp.concatenate(
            [q_rows, vec_own, jnp.broadcast_to(as_pair(squares), (share, 2))], axis=1
        )[None]
        for bit in z_bits[::-1]:
            near_q = jnp.concatenate([near_q, swap(near_q, "dp", bit, replicas)], axis=0)
        far_q = swap(near_q, "dp", 1, replicas)

        def block_of(index):
            block = index % 2
            for bit in z_bits:
                block = block * 2 + index // bit % 2
            return block

        def index_of(block):
            index = 0
            for bit in z_bits[::-1]:
                index = index + block % 2 * bit
                block = block // 2
            return index + block

        turn = block_of(replica)
        small = jnp.concatenate([near_q[:, :, 3 * width :], far_q[:, :, 3 * width :]], axis=0)
        small = jnp.stack([pick(small, turn ^ r) for r in range(replicas)]).astype(HIGH)
        summed_vec = small[:, :, :extra].reshape(rows, extra).T
        squares = jnp.sum(small[:, 0, extra:])

        own_da1 = da1_keep[0].astype(HIGH) + da1_got[0].astype(HIGH)
        da1 = own_da1 + swap(add_low(da1_keep[1], da1_got[1]), "shard", 2, parts).astype(HIGH)
        unit, inverse = normalize(tokens.astype(HIGH))
        grad_input = grad_resid + normalize_back(unit, inverse, da1 * vectors[0:1])
        live_rows = jnp.arange(slots, dtype=jnp.int32) < live_own[0]
        grad_in = jnp.where(live_rows[:, None], grad_input, 0.0).astype(LOW)

        norm_total = jnp.sqrt(squares)
        factor = jnp.minimum(1.0, CLIP_LIMIT / (norm_total + 1e-06))
        near_count = replicas // 2
        q_block = (1,) + near_q.shape[1:]

        def gathered_spec(array):
            return pl.BlockSpec((1,) + array.shape[1:], lambda i, _, p: (index_of(i ^ p[0]), 0, 0))

        attn_shape = (replicas, share, 4 * width)
        mlp_shape = (2, replicas, share, hidden)
        attn_spec = pl.BlockSpec((1, share, 4 * width), lambda i, _, p: (i ^ p[0], 0, 0))
        mlp_spec = pl.BlockSpec((2, 1, share, hidden), lambda i, _, p: (0, i ^ p[0], 0, 0))
        updated = pl.pallas_call(
            functools.partial(adam_kernel, fc_rows),
            grid_spec=pltpu.PrefetchScalarGridSpec(
                num_scalar_prefetch=2,
                grid=(replicas,),
                in_specs=[gathered_spec(all_ab)]
                + [
                    pl.BlockSpec(q_block, lambda i, *_: (jnp.minimum(i, near_count - 1), 0, 0)),
                    pl.BlockSpec(q_block, lambda i, *_: (jnp.maximum(i - near_count, 0), 0, 0)),
                ]
                + [attn_spec] * 3
                + [mlp_spec] * 3,
                out_specs=[attn_spec] * 4 + [mlp_spec] * 4,
            ),
            out_shape=[jax.ShapeDtypeStruct(attn_shape, HIGH)] * 4
            + [jax.ShapeDtypeStruct(mlp_shape, HIGH)] * 4,
            compiler_params=params(20),
            cost_estimate=cost(30 * 9 * rows * width, 54e6),
            name="adam",
        )(
            factor.reshape(1),
            turn.reshape(1).astype(jnp.int32),
            all_ab,
            near_q,
            far_q,
            *[array.reshape(attn_shape) for array in (attn_w, attn_m, attn_v)],
            *[array.reshape(mlp_shape) for array in (mlp_w, mlp_m, mlp_v)],
        )
        attn_grad, attn_w_new, attn_m_new, attn_v_new = [u.reshape(attn_w.shape) for u in updated[:4]]
        mlp_grad, mlp_w_new, mlp_m_new, mlp_v_new = [u.reshape(mlp_w.shape) for u in updated[4:]]
        vec_grad, vec_w_new, vec_m_new, vec_v_new = adam_update(
            vec_w, vec_m, vec_v, summed_vec, factor, RATE_VECTOR, 0.0
        )
        return (
            block_out, grad_in, attn_grad, mlp_grad, vec_grad,
            attn_w_new, attn_m_new, attn_v_new, mlp_w_new, mlp_m_new, mlp_v_new,
            vec_w_new, vec_m_new, vec_v_new, norm_total.reshape(1),
        )

    return on_device


def solution(mesh):
    tokens = P(("dp", "shard"), None)
    groups = P("dp", None)
    attn = P("shard", None)
    mlp = P(None, "shard", None)
    vec = P(None, "shard")
    return jax.shard_map(
        make_on_device(mesh.shape["shard"], mesh.shape["dp"]),
        mesh=mesh,
        in_specs=(tokens, tokens, groups, groups) + (attn,) * 3 + (mlp,) * 3 + (vec,) * 3,
        out_specs=(tokens, tokens, attn, mlp, vec) + (attn,) * 3 + (mlp,) * 3 + (vec,) * 3 + (P(),),
        check_vma=False,
    )
```

```python
import functools

import jax
import jax.numpy as jnp
from jax import lax
from jax.experimental import pallas as pl
from jax.experimental.pallas import tpu as pltpu
from jax.sharding import PartitionSpec as P

HEADS = 12
STEP = 10
NORM_EPSILON = 1e-05
BETA_FIRST = 0.9
BETA_SECOND = 0.999
ADAM_EPSILON = 1e-08
RATE_MATRIX = 0.1
RATE_VECTOR = 0.2
DECAY_MATRIX = 0.1
CLIP_LIMIT = 1.0
MASKED_SCORE = -1e30
QUERY_BLOCK = 256
LOW = jnp.bfloat16
HIGH = jnp.float32


def dot_nn(a, b):
    return lax.dot_general(a, b, (((1,), (0,)), ((), ())), preferred_element_type=HIGH)


def dot_nt(a, b):
    return lax.dot_general(a, b, (((1,), (1,)), ((), ())), preferred_element_type=HIGH)


def low_t(a):
    return a.astype(HIGH).T.astype(LOW)


def normalize(features):
    centered = features - jnp.mean(features, axis=-1, keepdims=True)
    variance = jnp.mean(centered * centered, axis=-1, keepdims=True)
    inverse = lax.rsqrt(variance + NORM_EPSILON)
    return centered * inverse, inverse


def normalize_back(unit, inverse, grad_unit):
    first = jnp.mean(grad_unit, axis=-1, keepdims=True)
    second = jnp.mean(grad_unit * unit, axis=-1, keepdims=True)
    return inverse * (grad_unit - first - unit * second)


def cut_kernel(place, w_ref, vec_ref, *out_refs):
    parts = len(out_refs)
    rows, columns = w_ref.shape
    width = columns // 3
    cols = width // parts
    vec = vec_ref[...]
    tail = [
        jnp.concatenate([vec[3 * k + m : 3 * k + m + 1, :] for m in range(3)], axis=1)
        for k in range(vec.shape[0] // 3)
    ]
    tail.append(jnp.zeros((16 - len(tail), 3 * cols), HIGH))
    tail = jnp.concatenate(tail, axis=0).astype(LOW)
    for r in range(parts):
        starts = [k * width + r * cols for k in range(3)]
        piece = jnp.concatenate([w_ref[:, c : c + cols] for c in starts], axis=1).astype(LOW)
        for j in range(parts):

            @pl.when((place[0] ^ j) == r)
            def _():
                out_refs[j][:rows, :] = piece
                out_refs[j][rows:, :] = tail


def widen_kernel(half, out_ref, mlp_ref, wide_ref, *half_refs):
    rows, width = out_ref.shape
    start = pl.multiple_of(half[0] * (rows // 2), 16)
    near = pl.ds(start, rows // 2)
    sources = [(out_ref[...], out_ref[near, :])]
    for f in range(mlp_ref.shape[2] // width):
        span = slice(f * width, (f + 1) * width)
        sources += [(mlp_ref[n, :, span], mlp_ref[n, near, span]) for n in range(2)]
    split = half_refs[0].shape[1] // width
    for n, (block, part) in enumerate(sources):
        wide_ref[:, n * width : (n + 1) * width] = block.astype(LOW)
        k = int(n >= split)
        at = (n - k * split) * width
        half_refs[k][:, at : at + width] = part.astype(LOW)


def project_kernel(parts, place, *refs):
    x_refs, w_refs, refs = refs[:parts], refs[parts : 2 * parts], refs[2 * parts :]
    bias_ref, a1_ref, qkv_ref, wt_ref, vec_ref, w_scr, x_scr, sems = refs
    step = pl.program_id(0)
    rows = vec_ref.shape[1] // parts

    def copy(j):
        return pltpu.make_async_copy(x_refs[j], x_scr.at[j], sems.at[j])

    @pl.when(step == 0)
    def _():
        for j in range(parts):
            copy(j).start()
        vec_ref[...] = jnp.zeros_like(vec_ref)
        for j in range(parts):
            start = pl.multiple_of((place[0] ^ j) * rows, 16)
            w_scr[pl.ds(start, rows), :] = w_refs[j][:rows, :].astype(HIGH)
            tail = w_refs[j][rows:, :].astype(HIGH)
            for r in range(parts):

                @pl.when((place[0] ^ j) == r)
                def _():
                    for n in range(12):
                        piece = tail[n // 3 : n // 3 + 1, n % 3 * rows : (n % 3 + 1) * rows]
                        vec_ref[n : n + 1, r * rows : (r + 1) * rows] = piece

        wt_ref[...] = w_scr[...].T.astype(LOW)

    for j in range(parts):

        @pl.when(step == j)
        def _():
            copy(j).wait()

    unit, _ = normalize(x_scr[step].astype(HIGH))
    a1 = (unit * vec_ref[0:1, :] + vec_ref[1:2, :]).astype(LOW)
    a1_ref[...] = a1
    qkv_ref[...] = (dot_nt(wt_ref[...], a1) + bias_ref[...]).astype(LOW)


def masked_scores(q, kt, seg_q, seg_k, start):
    block = q.shape[0]
    out = []
    if start:
        s = dot_nn(q, kt[:, :start])
        out.append(jnp.where(seg_q == seg_k[:, :start], s, MASKED_SCORE))
    s = dot_nn(q, kt[:, start : start + block])
    row = lax.broadcasted_iota(jnp.int32, (block, block), 0)
    col = lax.broadcasted_iota(jnp.int32, (block, block), 1)
    allowed = (seg_q == seg_k[:, start : start + block]) & (col <= row)
    out.append(jnp.where(allowed, s, MASKED_SCORE))
    return out


def attend_kernel(scale, place, qt_ref, kt_ref, vt_ref, segc_ref, segr_ref, o_ref, lse_ref, v_scr):
    total = qt_ref.shape[1]
    per_part = o_ref.shape[2]
    block = min(QUERY_BLOCK, per_part)
    v_scr[...] = low_t(vt_ref[...])
    for start in range(0, total, block):
        span = slice(start, start + block)
        q = (qt_ref[:, span].astype(HIGH) * scale).T.astype(LOW)
        pieces = masked_scores(q, kt_ref, segc_ref[span, :], segr_ref, start)
        top = functools.reduce(jnp.maximum, [jnp.max(s, axis=1, keepdims=True) for s in pieces])
        weights = [jnp.exp(s - top) for s in pieces]
        mass = sum(jnp.sum(w, axis=1, keepdims=True) for w in weights)
        lse_ref[0, span, :] = top + jnp.log(mass)
        inverse = 1.0 / mass
        mixed = dot_nn((weights[-1] * inverse).astype(LOW), v_scr[span, :])
        if start:
            mixed += dot_nn((weights[0] * inverse).astype(LOW), v_scr[:start, :])
        inner = start % per_part
        o_ref[place[0] ^ (start // per_part), :, inner : inner + block] = mixed.T.astype(LOW)


def attend_back_kernel(
    scale, place, qt_ref, kt_ref, vt_ref, segc_ref, segr_ref, lse_ref, *refs
):
    *do_refs, out_ref, k_scr, do_scr, dk_scr, dv_scr = refs
    total = qt_ref.shape[1]
    parts, per_part = len(do_refs), do_refs[0].shape[1]
    block = min(QUERY_BLOCK, per_part)
    k_scr[...] = low_t(kt_ref[...])
    for j in range(parts):
        do_scr[place[0] ^ j] = do_refs[j][...]
    dk_scr[...] = jnp.zeros_like(dk_scr)
    dv_scr[...] = jnp.zeros_like(dv_scr)
    for start in range(0, total, block):
        span = slice(start, start + block)
        inner = start % per_part
        qt = qt_ref[:, span].astype(HIGH) * scale
        dot_ = do_scr[start // per_part, :, inner : inner + block]
        q = qt.T.astype(LOW)
        qt = qt.astype(LOW)
        do = low_t(dot_)
        pieces = masked_scores(q, kt_ref, segc_ref[span, :], segr_ref, start)
        spans = [slice(0, start), span] if start else [span]
        lse = lse_ref[0, span, :]
        weights = [jnp.exp(s - lse) for s in pieces]
        grads = [dot_nn(do, vt_ref[:, at]) for at in spans]
        delta = sum(jnp.sum(g * w, axis=1, keepdims=True) for g, w in zip(grads, weights))
        dq = None
        for at, w, g in zip(spans, weights, grads):
            ds = (w * (g - delta)).astype(LOW)
            term = dot_nn(ds, k_scr[at, :])
            dq = term if dq is None else dq + term
            dk_scr[:, at] += dot_nn(qt, ds)
            dv_scr[:, at] += dot_nn(dot_, w.astype(LOW))
        out_ref[0, :, span] = (dq * scale).T.astype(LOW)
    out_ref[1] = dk_scr[...].astype(LOW)
    out_ref[2] = dv_scr[...].astype(LOW)


def projection_back_kernel(heads, parts, place, half, *refs):
    x_refs, (a1_ref, *refs) = refs[:parts], refs[parts:]
    head_refs, refs = refs[:heads], refs[heads:]
    wt_ref, vec_ref, grads_ref, keep_ref, send_ref, qkeep_ref, qsend_ref, *scratch = refs
    g_scr, vec_scr, sums_scr, ext_scr, all_scr, x_scr, sems = scratch
    step = pl.program_id(0)
    cols = g_scr.shape[0] // 3
    extra = grads_ref.shape[0]
    count = qkeep_ref.shape[2] - 3 * cols

    def copy(j):
        return pltpu.make_async_copy(x_refs[j], x_scr.at[j], sems.at[j])

    @pl.when(step == 0)
    def _():
        for j in range(parts):
            copy(j).start()
        g_scr[...] = jnp.zeros_like(g_scr)
        vec_scr[...] = grads_ref[...]
        sums_scr[...] = jnp.zeros_like(sums_scr)

    for j in range(parts):

        @pl.when(step == j)
        def _():
            copy(j).wait()

    dqkv = jnp.concatenate([ref[k] for k in range(3) for ref in head_refs], axis=0)
    da1 = dot_nn(low_t(dqkv), wt_ref[...])

    @pl.when(step % 2 == 0)
    def _():
        keep_ref[0] = da1.astype(LOW)

    @pl.when(step % 2 == 1)
    def _():
        send_ref[0] = da1.astype(LOW)

    g_scr[...] += dot_nn(dqkv, a1_ref[...])
    unit, _ = normalize(x_scr[step].astype(HIGH))
    vec_scr[0:1, :] += jnp.sum(da1 * unit, axis=0, keepdims=True)
    vec_scr[1:2, :] += jnp.sum(da1, axis=0, keepdims=True)
    sums_scr[...] += jnp.sum(dqkv.astype(HIGH), axis=1, keepdims=True)

    @pl.when(step == pl.num_programs(0) - 1)
    def _():
        ext_scr[...] = vec_scr[...].T
        own = pl.ds(pl.multiple_of(place[0] * cols, 16), cols)
        ext_scr[own, 2:3] = sums_scr[:cols, :]
        ext_scr[own, 3:4] = sums_scr[2 * cols :, :]
        all_scr[:, : 3 * cols] = g_scr[...].T
        all_scr[:, 3 * cols : 3 * cols + extra] = ext_scr[...]
        rows = all_scr.shape[0] // parts
        for r in range(parts):
            for ref, side in ((qkeep_ref, half[0]), (qsend_ref, 1 - half[0])):
                start = pl.multiple_of(r * rows + side * (rows // 2), 16)
                ref[r] = all_scr[pl.ds(start, rows // 2), : 3 * cols + count].astype(LOW)


GELU_C = 0.7978845608028654
GELU_A = 0.044715


def mlp_kernel(
    parts, first_blocks, place, half, live_ref, x_ref, cot_ref, vec_ref, *refs
):
    o_refs, refs = refs[:parts], refs[parts:]
    own_ref, core_ref, *wide_refs = refs[:10]
    out_ref, *grad_refs = refs[10:15]
    dr1_ref, vecg_ref, *refs = refs[15:]
    do_refs, scratch = refs[:parts], refs[parts:]
    wide, ot_scr, r1_scr, a2_scr, a2t_scr, dy_scr, dyt_scr, y_scr, da2_scr, act_scr, sems = scratch
    step = pl.program_id(0)
    rows = o_refs[0].shape[0]
    slots, width = x_ref.shape
    bo, gain, shift, bp = (vec_ref[r : r + 1, :] for r in (4, 5, 6, 11))
    split = wide_refs[0].shape[1]
    live = lax.broadcasted_iota(jnp.int32, (slots, 1), 0) < live_ref[0]

    def copies(k):
        half_rows = rows // 2
        near, far = half[0] * half_rows, (1 - half[0]) * half_rows
        span = slice(0, split) if k == 0 else slice(split, wide.shape[1])
        sources = [(own_ref.at[:, span], 0, 0), (core_ref.at[:, span], 1, 0)]
        spots = [(2, near), (2, far), (3, near), (3, far)]
        sources += [(wide_refs[4 * k + n], *spot) for n, spot in enumerate(spots)]
        for n, (source, j, offset) in enumerate(sources):
            start = pl.multiple_of((place[0] ^ j) * rows + offset, 16)
            target = wide.at[pl.ds(start, source.shape[0]), span]
            yield pltpu.make_async_copy(source, target, sems.at[k, n])

    def block(n):
        return wide[:, pl.ds(pl.multiple_of(n * width, 128), width)]

    def permuted(scratch, value):
        for j in range(parts):
            scratch[j * rows : (j + 1) * rows, :] = value(pl.multiple_of((place[0] ^ j) * rows, 16))

    def put(value):
        value = value.astype(LOW)
        for k in range(2):

            @pl.when((step >= first_blocks) == bool(k))
            def _():
                keep, send = grad_refs[2 * k : 2 * k + 2]
                for j in range(parts):
                    (send if j % 2 else keep)[j // 2] = value[j * rows : (j + 1) * rows, :]

    @pl.when(step == 0)
    def _():
        for k in range(2):
            for copy in copies(k):
                copy.start()
        for j in range(parts):
            start = pl.multiple_of((place[0] ^ j) * rows, 16)
            ot_scr[pl.ds(start, rows), :] = o_refs[j][...]
        mixed = low_t(ot_scr[...])
        dy = jnp.where(live, cot_ref[...].astype(HIGH), 0.0)
        dy_scr[...] = dy.astype(LOW)
        ot_scr[...] = dy.T.astype(LOW)
        permuted(dyt_scr, lambda start: ot_scr[pl.ds(start, rows), :])
        for copy in copies(0):
            copy.wait()
        r1 = x_ref[...].astype(HIGH) + dot_nn(mixed, wide[:, :width]) + bo
        r1_scr[...] = r1
        unit, _ = normalize(r1)
        a2 = unit * gain + shift
        a2_scr[...] = a2.astype(LOW)
        ot_scr[...] = a2.T.astype(LOW)
        permuted(a2t_scr, lambda start: ot_scr[pl.ds(start, rows), :])
        vecg_ref[...] = jnp.zeros_like(vecg_ref)
        vecg_ref[11:12, :] = jnp.sum(dy, axis=0, keepdims=True)
        y_scr[...] = r1 + bp
        da2_scr[...] = jnp.zeros_like(da2_scr)

    @pl.when(step == first_blocks)
    def _():
        for copy in copies(1):
            copy.wait()

    last = pl.num_programs(0) - 1

    @pl.when((step < last) & (step % 2 == 0))
    def _():
        w_fc, w_pt = block(1 + step), block(2 + step)
        u = dot_nn(a2_scr[...], w_fc) + vec_ref[pl.ds(7 + step // 2, 1), :]
        square = u * u
        t = jnp.tanh(GELU_C * (u + GELU_A * (square * u)))
        grown = 0.5 * (1.0 + t)
        act = (u * grown).astype(LOW)
        act_scr[...] = act
        y_scr[...] += dot_nt(act, w_pt)
        slope = grown + 0.5 * u * (1.0 - t * t) * (GELU_C + (3.0 * GELU_C * GELU_A) * square)
        du = (dot_nn(dy_scr[...], w_pt) * slope).astype(LOW)
        vecg_ref[pl.ds(7 + step // 2, 1), :] = jnp.sum(du.astype(HIGH), axis=0, keepdims=True)
        da2_scr[...] += dot_nt(du, w_fc)
        put(dot_nn(a2t_scr[...], du))

    @pl.when((step < last) & (step % 2 == 1))
    def _():
        put(dot_nn(dyt_scr[...], act_scr[...]))

    @pl.when(step == last)
    def _():
        out_ref[...] = jnp.where(live, y_scr[...], 0.0).astype(LOW)
        unit, inverse = normalize(r1_scr[...])
        da2 = da2_scr[...]
        vecg_ref[5:6, :] = jnp.sum(da2 * unit, axis=0, keepdims=True)
        vecg_ref[6:7, :] = jnp.sum(da2, axis=0, keepdims=True)
        dr1 = dy_scr[...].astype(HIGH) + normalize_back(unit, inverse, da2 * gain)
        dr1_ref[...] = dr1
        low = dr1.astype(LOW)
        vecg_ref[4:5, :] = jnp.sum(low.astype(HIGH), axis=0, keepdims=True)
        put(dot_nn(jnp.concatenate([ref[...] for ref in o_refs], axis=0), low))
        for j in range(parts):
            start = pl.multiple_of((place[0] ^ j) * rows, 16)
            do_refs[j][...] = dot_nt(wide[pl.ds(start, rows), :width], low).astype(LOW)


def group_layout(length_row, count_row, slots):
    starts = jnp.cumsum(count_row) - count_row
    within = jnp.arange(slots, dtype=jnp.int32)
    position = (starts[:, None] + within[None, :]).reshape(-1)
    live_rows = (within[None, :] < count_row[:, None]).reshape(-1)
    boundary = jnp.cumsum(length_row)
    segment = jnp.sum((position[:, None] >= boundary[None, :]).astype(jnp.int32), axis=1)
    buffer_slot = jnp.arange(position.shape[0], dtype=jnp.int32)
    return jnp.where(live_rows, segment, -1 - buffer_slot)


def adam_update(master, first, second, gradient, factor, rate, decay):
    clipped = gradient * factor
    first_new = BETA_FIRST * first + (1.0 - BETA_FIRST) * clipped
    second_new = BETA_SECOND * second + (1.0 - BETA_SECOND) * clipped * clipped
    first_hat = first_new / (1.0 - BETA_FIRST**STEP)
    second_hat = second_new / (1.0 - BETA_SECOND**STEP)
    master_new = master - rate * (
        first_hat / (jnp.sqrt(second_hat) + ADAM_EPSILON) + decay * master
    )
    return (clipped, master_new, first_new, second_new)


def adam_kernel(fc_rows, factor_ref, _, *refs):
    grads, states, outs = refs[:3], refs[3:9], refs[9:]
    near = pl.program_id(0) < pl.num_programs(0) // 2
    factor = factor_ref[0]
    width = outs[0].shape[-1] // fc_rows
    qkv = jnp.where(near, grads[1][0], grads[2][0])[:, : 3 * width]

    def update(gradient, at, base):
        results = adam_update(
            *[states[base + n][at] for n in range(3)],
            gradient.astype(HIGH), factor, RATE_MATRIX, DECAY_MATRIX,
        )
        for n, result in enumerate(results):
            outs[base // 3 * 4 + n][at] = result

    blocks = [grads[0][0, :, n : n + width] for n in range(0, grads[0].shape[2], width)]
    for f in range(fc_rows):
        span = slice(f * width, (f + 1) * width)
        for n in range(2):
            update(blocks[2 * f + n], (n, 0, slice(None), span), 3)
    update(qkv, (0, slice(None), slice(0, 3 * width)), 0)
    update(blocks[-1], (0, slice(None), slice(3 * width, 4 * width)), 0)


def swap(array, axis, bit, count):
    return lax.ppermute(array, axis, [(i, i ^ bit) for i in range(count)])


def pick(array, index):
    return lax.dynamic_index_in_dim(array, index, 0, keepdims=False)


def deal(pieces, parts):
    return list(pieces[:1]) + [swap(pieces[j], "shard", j, parts) for j in range(1, parts)]


def in_order(relative, place, parts):
    relative = jnp.stack(relative)
    return jnp.stack([pick(relative, place ^ r) for r in range(parts)])


def collect(own, parts):
    have = [own]
    bit = parts // 2
    slots = [0]
    while bit:
        have = have + [swap(piece, "shard", bit, parts) for piece in have]
        slots = slots + [s ^ bit for s in slots]
        bit //= 2
    return [have[slots.index(j)] for j in range(parts)]


def after(value, *others):
    return lax.optimization_barrier((value, *others))[0]


def add_low(a, b):
    return (a.astype(HIGH) + b.astype(HIGH)).astype(LOW)


def bits_of(count):
    return [1 << n for n in range(count.bit_length() - 1)]


def halve(array, upper, dim):
    length = array.shape[dim] // 2
    keep = lax.dynamic_slice_in_dim(array, upper * length, length, dim)
    return keep, lax.dynamic_slice_in_dim(array, (1 - upper) * length, length, dim)


def scatter_half(array, dim, bit, replica, replicas):
    keep, send = halve(array, (replica // bit) % 2, dim)
    return keep, swap(send, "dp", bit, replicas)


def params(mebibytes):
    return pltpu.CompilerParams(
        dimension_semantics=("arbitrary",), vmem_limit_bytes=mebibytes * 1024 * 1024
    )


def cost(flops, moved, special=0):
    return pl.CostEstimate(flops=int(flops), bytes_accessed=int(moved), transcendentals=int(special))


def whole(*shape):
    zeros = (0,) * len(shape)
    return pl.BlockSpec(shape, lambda *_: zeros)


def make_on_device(parts, replicas):
    def on_device(
        tokens, cotangent, lengths, counts,
        attn_w, attn_m, attn_v, mlp_w, mlp_m, mlp_v, vec_w, vec_m, vec_v,
    ):
        slots, width = tokens.shape
        rows = attn_w.shape[0]
        hidden = mlp_w.shape[2]
        fc_rows = hidden // width
        total = parts * slots
        head_size = width // HEADS
        own_heads = HEADS // parts
        own_cols = own_heads * head_size
        scale = head_size ** (-0.5)
        place = lax.axis_index("shard")
        replica = lax.axis_index("dp")
        prefetch = place.reshape(1).astype(jnp.int32)

        half = replica % 2
        side = half.reshape(1).astype(jnp.int32)

        x_all = collect(tokens, parts)
        w_pieces = pl.pallas_call(
            cut_kernel,
            grid_spec=pltpu.PrefetchScalarGridSpec(
                num_scalar_prefetch=1,
                grid=(1,),
                in_specs=[whole(rows, 3 * width), whole(vec_w.shape[0], rows)],
                out_specs=[whole(rows + 16, 3 * own_cols)] * parts,
            ),
            out_shape=[jax.ShapeDtypeStruct((rows + 16, 3 * own_cols), LOW)] * parts,
            compiler_params=params(12),
            cost_estimate=cost(0, 4e6),
            name="cut",
        )(prefetch, attn_w, vec_w)
        w_local = deal(w_pieces, parts)

        blocks = 2 * fc_rows + 1
        split = (fc_rows // 2 * 2 + 1) * width
        wide_own, *wide_half = pl.pallas_call(
            widen_kernel,
            grid_spec=pltpu.PrefetchScalarGridSpec(
                num_scalar_prefetch=1,
                grid=(1,),
                in_specs=[
                    pl.BlockSpec((rows, width), lambda *_: (0, 3)),
                    whole(2, rows, hidden),
                ],
                out_specs=[
                    whole(rows, blocks * width),
                    whole(rows // 2, split),
                    whole(rows // 2, blocks * width - split),
                ],
            ),
            out_shape=[
                jax.ShapeDtypeStruct((rows, blocks * width), LOW),
                jax.ShapeDtypeStruct((rows // 2, split), LOW),
                jax.ShapeDtypeStruct((rows // 2, blocks * width - split), LOW),
            ],
            compiler_params=params(28),
            cost_estimate=cost(0, 12e6),
            name="widen",
        )(side, attn_w, mlp_w)
        wide_own, *wide_half = lax.optimization_barrier((wide_own, *wide_half, *w_local, *x_all))[:3]
        near = [swap(mine, "shard", parts // 2, parts) for mine in wide_half]
        wide_core = swap(wide_own, "shard", 1, parts)

        segment = group_layout(lengths[0], counts[0], slots)
        seg_col = segment[:, None]
        seg_row = segment[None, :]
        own_vec = vec_w.astype(LOW).astype(HIGH)
        bias_local = jnp.concatenate(
            [own_vec[2], jnp.zeros((own_cols,), HIGH), own_vec[3]]
        )[:, None]

        a1, qkv, w_t, vectors = pl.pallas_call(
            functools.partial(project_kernel, parts),
            grid_spec=pltpu.PrefetchScalarGridSpec(
                num_scalar_prefetch=1,
                grid=(parts,),
                in_specs=[
                    *[pl.BlockSpec(memory_space=pl.ANY)] * parts,
                    *[whole(rows + 16, 3 * own_cols)] * parts,
                    whole(3 * own_cols, 1),
                ],
                out_specs=[
                    pl.BlockSpec((slots, width), lambda i, p: (p[0] ^ i, 0)),
                    pl.BlockSpec((3 * own_cols, slots), lambda i, p: (0, p[0] ^ i)),
                    whole(3 * own_cols, width),
                    whole(16, width),
                ],
                scratch_shapes=[
                    pltpu.VMEM((width, 3 * own_cols), HIGH),
                    pltpu.VMEM((parts, slots, width), LOW),
                    pltpu.SemaphoreType.DMA((parts,)),
                ],
            ),
            out_shape=[
                jax.ShapeDtypeStruct((total, width), LOW),
                jax.ShapeDtypeStruct((3 * own_cols, total), LOW),
                jax.ShapeDtypeStruct((3 * own_cols, width), LOW),
                jax.ShapeDtypeStruct((16, width), HIGH),
            ],
            compiler_params=params(24),
            cost_estimate=cost(2 * total * width * 3 * own_cols * 3, 12e6),
            name="project",
        )(prefetch, *x_all, *w_local, bias_local)

        pair_flops = 2 * total * total * head_size * 4 // 2

        def head_specs(h):
            return [
                pl.BlockSpec((head_size, total), functools.partial(lambda k, *_: (k * own_heads + h, 0), k))
                for k in range(3)
            ]

        def attend(h, qkv):
            return pl.pallas_call(
                functools.partial(attend_kernel, scale),
                grid_spec=pltpu.PrefetchScalarGridSpec(
                    num_scalar_prefetch=1,
                    grid=(1,),
                    in_specs=head_specs(h) + [whole(total, 1), whole(1, total)],
                    out_specs=[whole(parts, head_size, slots), whole(1, total, 1)],
                    scratch_shapes=[pltpu.VMEM((total, head_size), LOW)],
                ),
                out_shape=[
                    jax.ShapeDtypeStruct((parts, head_size, slots), LOW),
                    jax.ShapeDtypeStruct((1, total, 1), HIGH),
                ],
                compiler_params=params(24),
                cost_estimate=cost(2 * pair_flops, 4e6, total * total // 2),
                name="attend",
            )(prefetch, qkv, qkv, qkv, seg_col, seg_row)

        mixed, lse = [], []
        for h in range(own_heads):
            if h == 1:
                qkv, near[0] = lax.optimization_barrier((qkv, near[0]))
                far = [swap(near[0], "dp", 1, replicas)]
                turned = [swap(near[0], "shard", 1, parts)]
            head_mixed, head_lse = attend(h, qkv)
            mixed.append(head_mixed)
            lse.append(head_lse)
        near[1] = after(near[1], mixed[-1])
        far.append(swap(near[1], "dp", 1, replicas))
        mixed_own = deal(
            [jnp.concatenate([head[j] for head in mixed], axis=0) for j in range(parts)], parts
        )
        turned.append(swap(near[1], "shard", 1, parts))
        wide = [wide_own, wide_core]
        for k in range(2):
            wide += [near[k], far[k], turned[k], swap(far[k], "shard", 1, parts)]

        steps = blocks
        live_own = lax.dynamic_index_in_dim(counts[0], place, 0, keepdims=True)
        first_blocks = fc_rows // 2 * 2

        def grad_spec(k):
            first, last = ((0, first_blocks - 1), (first_blocks, steps - 1))[k]
            return pl.BlockSpec(
                (parts // 2, rows, width), lambda i, *_: (0, 0, jnp.clip(i, first, last) - first)
            )

        grad_columns = [first_blocks * width, (steps - first_blocks) * width]

        in_hbm = pl.BlockSpec(memory_space=pltpu.HBM)
        out = pl.pallas_call(
            functools.partial(mlp_kernel, parts, first_blocks),
            grid_spec=pltpu.PrefetchScalarGridSpec(
                num_scalar_prefetch=3,
                grid=(steps,),
                in_specs=[whole(slots, width), whole(slots, width), whole(16, width)]
                + [whole(own_cols, slots)] * parts
                + [in_hbm] * len(wide),
                out_specs=[whole(slots, width)]
                + [grad_spec(k) for k in range(2) for _ in range(2)]
                + [whole(slots, width), whole(16, width)]
                + [whole(own_cols, slots)] * parts,
                scratch_shapes=[
                    pltpu.VMEM((width, blocks * width), LOW),
                    pltpu.VMEM((width, slots), LOW),
                    pltpu.VMEM((slots, width), HIGH),
                    pltpu.VMEM((slots, width), LOW),
                    pltpu.VMEM((width, slots), LOW),
                    pltpu.VMEM((slots, width), LOW),
                    pltpu.VMEM((width, slots), LOW),
                    pltpu.VMEM((slots, width), HIGH),
                    pltpu.VMEM((slots, width), HIGH),
                    pltpu.VMEM((slots, width), LOW),
                    pltpu.SemaphoreType.DMA((2, 6)),
                ],
            ),
            out_shape=[jax.ShapeDtypeStruct((slots, width), LOW)]
            + [jax.ShapeDtypeStruct((parts // 2, rows, c), LOW) for c in grad_columns for _ in range(2)]
            + [jax.ShapeDtypeStruct((slots, width), HIGH), jax.ShapeDtypeStruct((16, width), HIGH)]
            + [jax.ShapeDtypeStruct((own_cols, slots), LOW)] * parts,
            compiler_params=params(44),
            cost_estimate=cost(2 * slots * width * (6 * hidden + 3 * width), 30e6, slots * hidden),
            name="mlp",
        )(prefetch, side, live_own, tokens, cotangent, vectors, *mixed_own, *wide)
        block_out, keep_a, send_a, keep_b, send_b, grad_resid, mid_grads, *do_pieces = out

        do_own = deal(do_pieces, parts)
        got_a = swap(send_a, "shard", 1, parts)
        got_b = swap(send_b, "shard", 1, parts)
        own_a, other_a = [add_low(keep_a[n], got_a[n]) for n in range(2)]
        own_b, other_b = halve(add_low(keep_b, got_b), half, 1)
        *do_own, own_a, other_a, own_b, other_b = lax.optimization_barrier(
            (*do_own, own_a, other_a, own_b, other_b)
        )
        got_a = swap(other_a, "shard", parts // 2, parts)
        got_b = swap(other_b, "dp", 1, replicas)

        def attend_back(h, qkv):
            return pl.pallas_call(
                functools.partial(attend_back_kernel, scale),
                grid_spec=pltpu.PrefetchScalarGridSpec(
                    num_scalar_prefetch=1,
                    grid=(1,),
                    in_specs=head_specs(h)
                    + [whole(total, 1), whole(1, total), whole(1, total, 1)]
                    + [pl.BlockSpec((head_size, slots), lambda *_: (h, 0))] * parts,
                    out_specs=whole(3, head_size, total),
                    scratch_shapes=[
                        pltpu.VMEM((total, head_size), LOW),
                        pltpu.VMEM((parts, head_size, slots), LOW),
                        pltpu.VMEM((head_size, total), HIGH),
                        pltpu.VMEM((head_size, total), HIGH),
                    ],
                ),
                out_shape=jax.ShapeDtypeStruct((3, head_size, total), LOW),
                compiler_params=params(28),
                cost_estimate=cost(pair_flops // 4, 4e5),
                name="attend_back",
            )(prefetch, qkv, qkv, qkv, seg_col, seg_row, lse[h], *do_own)

        dqkv = [attend_back(h, qkv) for h in range(own_heads)]

        q_cols = 3 * own_cols
        extra = vec_w.shape[0]
        half_rows = rows // 2
        da1_keep, da1_send, own_q, other_q = pl.pallas_call(
            functools.partial(projection_back_kernel, own_heads, parts),
            grid_spec=pltpu.PrefetchScalarGridSpec(
                num_scalar_prefetch=2,
                grid=(parts,),
                in_specs=[
                    *[pl.BlockSpec(memory_space=pl.ANY)] * parts,
                    pl.BlockSpec((slots, width), lambda i, p, _: (p[0] ^ i, 0)),
                ]
                + [pl.BlockSpec((3, head_size, slots), lambda i, p, _: (0, 0, p[0] ^ i))] * own_heads
                + [whole(q_cols, width), whole(16, width), whole(16, width)],
                out_specs=[pl.BlockSpec((1, slots, width), lambda i, *_: (i // 2, 0, 0))] * 2
                + [whole(parts, half_rows, q_cols + extra)] * 2,
                scratch_shapes=[
                    pltpu.VMEM((q_cols, width), HIGH),
                    pltpu.VMEM((16, width), HIGH),
                    pltpu.VMEM((q_cols, 1), HIGH),
                    pltpu.VMEM((width, 16), HIGH),
                    pltpu.VMEM((width, q_cols + 64), HIGH),
                    pltpu.VMEM((parts, slots, width), LOW),
                    pltpu.SemaphoreType.DMA((parts,)),
                ],
            ),
            out_shape=[jax.ShapeDtypeStruct((parts // 2, slots, width), LOW)] * 2
            + [jax.ShapeDtypeStruct((parts, half_rows, q_cols + extra), LOW)] * 2,
            compiler_params=params(28),
            cost_estimate=cost(total * width * own_cols // 4, 1e6),
            name="projection_back",
        )(prefetch, side, *x_all, a1, *dqkv, w_t, vectors, mid_grads)

        share = rows // replicas
        z_bits = [bit for bit in (1 << n for n in range(1, 20)) if bit < replicas]
        last_event = [own_q]

        def seen(value):
            return lax.optimization_barrier((value, last_event[0]))[0]

        def event(value):
            last_event[0] = value
            return value

        def next_half(keep, got, bit, dim):
            array = event(add_low(keep, seen(got)))
            return scatter_half(array, dim, bit, replica, replicas)

        got_q = swap(other_q, "dp", 1, replicas)
        own_a, other_a = halve(event(add_low(own_a, seen(got_a))), half, 0)
        got_a = swap(other_a, "dp", 1, replicas)
        got_b = seen(got_b)
        own_b, other_b = [event(add_low(own_b[n], got_b[n])) for n in range(2)]
        got_b = swap(other_b, "shard", parts // 2, parts)
        da1_got = swap(da1_send, "shard", 1, parts)
        state_a = next_half(own_a, got_a, z_bits[0], 0)
        state_b = next_half(own_b, got_b, z_bits[0], 0)
        for bit in z_bits[1:]:
            state_a = next_half(*state_a, bit, 0)
        state_q = next_half(own_q, got_q, z_bits[0], 1)
        for bit in z_bits[1:]:
            state_b = next_half(*state_b, bit, 0)
        part_a = event(add_low(state_a[0], seen(state_a[1])))
        for bit in z_bits[1:]:
            state_q = next_half(*state_q, bit, 1)
        part_b = event(add_low(state_b[0], seen(state_b[1])))
        part_ab = event(jnp.concatenate([part_a, part_b], axis=1))
        all_ab = lax.all_gather(part_ab, "dp", axis=0)
        part_q = event(add_low(state_q[0], seen(state_q[1])))

        def as_pair(value):
            high = lax.reduce_precision(value, 8, 7)
            return jnp.stack([high, value - high]).astype(LOW)

        main = part_q[:, :, :q_cols]
        squares = sum(jnp.sum(jnp.square(p.astype(HIGH))) for p in (part_ab, main))
        vec_parts = part_q[:, :, q_cols:].transpose(1, 0, 2).reshape(1, share, parts * extra)
        shared = jnp.concatenate(
            [vec_parts, jnp.broadcast_to(as_pair(squares), (1, share, 2))], axis=2
        )
        pieces = jnp.concatenate([main, jnp.broadcast_to(shared, (parts,) + shared.shape[1:])], axis=2)
        dealt = in_order(deal([pick(pieces, place ^ j) for j in range(parts)], parts), place, parts)
        q_rows = (
            dealt[:, :, :q_cols]
            .reshape(parts, share, 3, own_cols)
            .transpose(1, 2, 0, 3)
            .reshape(share, 3 * width)
        )
        summed = jnp.sum(dealt[:, :, q_cols:].astype(HIGH), axis=0)
        vec_parts = summed[:, : parts * extra].reshape(share, parts, extra).astype(LOW)
        squares = jnp.sum(summed[0, parts * extra :]) + jnp.sum(jnp.square(vec_parts.astype(HIGH)))
        vec_own = lax.dynamic_index_in_dim(vec_parts, place, 1, keepdims=False)
        near_q = jnp.concatenate(
            [q_rows, vec_own, jnp.broadcast_to(as_pair(squares), (share, 2))], axis=1
        )[None]
        for bit in z_bits[::-1]:
            near_q = jnp.concatenate([near_q, swap(near_q, "dp", bit, replicas)], axis=0)
        far_q = swap(near_q, "dp", 1, replicas)

        def block_of(index):
            block = index % 2
            for bit in z_bits:
                block = block * 2 + index // bit % 2
            return block

        def index_of(block):
            index = 0
            for bit in z_bits[::-1]:
                index = index + block % 2 * bit
                block = block // 2
            return index + block

        turn = block_of(replica)
        small = jnp.concatenate([near_q[:, :, 3 * width :], far_q[:, :, 3 * width :]], axis=0)
        small = jnp.stack([pick(small, turn ^ r) for r in range(replicas)]).astype(HIGH)
        summed_vec = small[:, :, :extra].reshape(rows, extra).T
        squares = jnp.sum(small[:, 0, extra:])

        own_da1 = da1_keep[0].astype(HIGH) + da1_got[0].astype(HIGH)
        da1 = own_da1 + swap(add_low(da1_keep[1], da1_got[1]), "shard", 2, parts).astype(HIGH)
        unit, inverse = normalize(tokens.astype(HIGH))
        grad_input = grad_resid + normalize_back(unit, inverse, da1 * vectors[0:1])
        live_rows = jnp.arange(slots, dtype=jnp.int32) < live_own[0]
        grad_in = jnp.where(live_rows[:, None], grad_input, 0.0).astype(LOW)

        norm_total = jnp.sqrt(squares)
        factor = jnp.minimum(1.0, CLIP_LIMIT / (norm_total + 1e-06))
        near_count = replicas // 2
        q_block = (1,) + near_q.shape[1:]

        def gathered_spec(array):
            return pl.BlockSpec((1,) + array.shape[1:], lambda i, _, p: (index_of(i ^ p[0]), 0, 0))

        attn_shape = (replicas, share, 4 * width)
        mlp_shape = (2, replicas, share, hidden)
        attn_spec = pl.BlockSpec((1, share, 4 * width), lambda i, _, p: (i ^ p[0], 0, 0))
        mlp_spec = pl.BlockSpec((2, 1, share, hidden), lambda i, _, p: (0, i ^ p[0], 0, 0))
        updated = pl.pallas_call(
            functools.partial(adam_kernel, fc_rows),
            grid_spec=pltpu.PrefetchScalarGridSpec(
                num_scalar_prefetch=2,
                grid=(replicas,),
                in_specs=[gathered_spec(all_ab)]
                + [
                    pl.BlockSpec(q_block, lambda i, *_: (jnp.minimum(i, near_count - 1), 0, 0)),
                    pl.BlockSpec(q_block, lambda i, *_: (jnp.maximum(i - near_count, 0), 0, 0)),
                ]
                + [attn_spec] * 3
                + [mlp_spec] * 3,
                out_specs=[attn_spec] * 4 + [mlp_spec] * 4,
            ),
            out_shape=[jax.ShapeDtypeStruct(attn_shape, HIGH)] * 4
            + [jax.ShapeDtypeStruct(mlp_shape, HIGH)] * 4,
            compiler_params=params(50),
            cost_estimate=cost(30 * 9 * rows * width, 54e6),
            name="adam",
        )(
            factor.reshape(1),
            turn.reshape(1).astype(jnp.int32),
            all_ab,
            near_q,
            far_q,
            *[array.reshape(attn_shape) for array in (attn_w, attn_m, attn_v)],
            *[array.reshape(mlp_shape) for array in (mlp_w, mlp_m, mlp_v)],
        )
        attn_grad, attn_w_new, attn_m_new, attn_v_new = [u.reshape(attn_w.shape) for u in updated[:4]]
        mlp_grad, mlp_w_new, mlp_m_new, mlp_v_new = [u.reshape(mlp_w.shape) for u in updated[4:]]
        vec_grad, vec_w_new, vec_m_new, vec_v_new = adam_update(
            vec_w, vec_m, vec_v, summed_vec, factor, RATE_VECTOR, 0.0
        )
        return (
            block_out, grad_in, attn_grad, mlp_grad, vec_grad,
            attn_w_new, attn_m_new, attn_v_new, mlp_w_new, mlp_m_new, mlp_v_new,
            vec_w_new, vec_m_new, vec_v_new, norm_total.reshape(1),
        )

    return on_device


def solution(mesh):
    tokens = P(("dp", "shard"), None)
    groups = P("dp", None)
    attn = P("shard", None)
    mlp = P(None, "shard", None)
    vec = P(None, "shard")
    return jax.shard_map(
        make_on_device(mesh.shape["shard"], mesh.shape["dp"]),
        mesh=mesh,
        in_specs=(tokens, tokens, groups, groups) + (attn,) * 3 + (mlp,) * 3 + (vec,) * 3,
        out_specs=(tokens, tokens, attn, mlp, vec) + (attn,) * 3 + (mlp,) * 3 + (vec,) * 3 + (P(),),
        check_vma=False,
    )
```

```python
import functools

import jax
import jax.numpy as jnp
from jax import lax
from jax.experimental import pallas as pl
from jax.experimental.pallas import tpu as pltpu
from jax.sharding import PartitionSpec as P

HEADS = 12
STEP = 10
NORM_EPSILON = 1e-05
BETA_FIRST = 0.9
BETA_SECOND = 0.999
ADAM_EPSILON = 1e-08
RATE_MATRIX = 0.1
RATE_VECTOR = 0.2
DECAY_MATRIX = 0.1
CLIP_LIMIT = 1.0
MASKED_SCORE = -1e30
QUERY_BLOCK = 256
LOW = jnp.bfloat16
HIGH = jnp.float32


def dot_nn(a, b):
    return lax.dot_general(a, b, (((1,), (0,)), ((), ())), preferred_element_type=HIGH)


def dot_nt(a, b):
    return lax.dot_general(a, b, (((1,), (1,)), ((), ())), preferred_element_type=HIGH)


def low_t(a):
    return a.astype(HIGH).T.astype(LOW)


def normalize(features):
    centered = features - jnp.mean(features, axis=-1, keepdims=True)
    variance = jnp.mean(centered * centered, axis=-1, keepdims=True)
    inverse = lax.rsqrt(variance + NORM_EPSILON)
    return centered * inverse, inverse


def normalize_back(unit, inverse, grad_unit):
    first = jnp.mean(grad_unit, axis=-1, keepdims=True)
    second = jnp.mean(grad_unit * unit, axis=-1, keepdims=True)
    return inverse * (grad_unit - first - unit * second)


def cut_kernel(place, w_ref, vec_ref, *out_refs):
    parts = len(out_refs)
    rows, columns = w_ref.shape
    width = columns // 3
    cols = width // parts
    vec = vec_ref[...]
    tail = [
        jnp.concatenate([vec[3 * k + m : 3 * k + m + 1, :] for m in range(3)], axis=1)
        for k in range(vec.shape[0] // 3)
    ]
    tail.append(jnp.zeros((16 - len(tail), 3 * cols), HIGH))
    tail = jnp.concatenate(tail, axis=0).astype(LOW)
    for r in range(parts):
        starts = [k * width + r * cols for k in range(3)]
        piece = jnp.concatenate([w_ref[:, c : c + cols] for c in starts], axis=1).astype(LOW)
        for j in range(parts):

            @pl.when((place[0] ^ j) == r)
            def _():
                out_refs[j][:rows, :] = piece
                out_refs[j][rows:, :] = tail


def widen_kernel(half, out_ref, mlp_ref, wide_ref, *half_refs):
    rows, width = out_ref.shape
    start = pl.multiple_of(half[0] * (rows // 2), 16)
    near = pl.ds(start, rows // 2)
    sources = [(out_ref[...], out_ref[near, :])]
    for f in range(mlp_ref.shape[2] // width):
        span = slice(f * width, (f + 1) * width)
        sources += [(mlp_ref[n, :, span], mlp_ref[n, near, span]) for n in range(2)]
    split = half_refs[0].shape[1] // width
    for n, (block, part) in enumerate(sources):
        wide_ref[:, n * width : (n + 1) * width] = block.astype(LOW)
        k = int(n >= split)
        at = (n - k * split) * width
        half_refs[k][:, at : at + width] = part.astype(LOW)


def project_kernel(parts, place, *refs):
    x_refs, w_refs, refs = refs[:parts], refs[parts : 2 * parts], refs[2 * parts :]
    bias_ref, a1_ref, qkv_ref, wt_ref, vec_ref, w_scr, x_scr, sems = refs
    step = pl.program_id(0)
    rows = vec_ref.shape[1] // parts

    def copy(j):
        return pltpu.make_async_copy(x_refs[j], x_scr.at[j], sems.at[j])

    @pl.when(step == 0)
    def _():
        for j in range(parts):
            copy(j).start()
        vec_ref[...] = jnp.zeros_like(vec_ref)
        for j in range(parts):
            start = pl.multiple_of((place[0] ^ j) * rows, 16)
            w_scr[pl.ds(start, rows), :] = w_refs[j][:rows, :].astype(HIGH)
            tail = w_refs[j][rows:, :].astype(HIGH)
            for r in range(parts):

                @pl.when((place[0] ^ j) == r)
                def _():
                    for n in range(12):
                        piece = tail[n // 3 : n // 3 + 1, n % 3 * rows : (n % 3 + 1) * rows]
                        vec_ref[n : n + 1, r * rows : (r + 1) * rows] = piece

        wt_ref[...] = w_scr[...].T.astype(LOW)

    for j in range(parts):

        @pl.when(step == j)
        def _():
            copy(j).wait()

    unit, _ = normalize(x_scr[step].astype(HIGH))
    a1 = (unit * vec_ref[0:1, :] + vec_ref[1:2, :]).astype(LOW)
    a1_ref[...] = a1
    qkv_ref[...] = (dot_nt(wt_ref[...], a1) + bias_ref[...]).astype(LOW)


def masked_scores(q, kt, seg_q, seg_k, start):
    block = q.shape[0]
    out = []
    if start:
        s = dot_nn(q, kt[:, :start])
        out.append(jnp.where(seg_q == seg_k[:, :start], s, MASKED_SCORE))
    s = dot_nn(q, kt[:, start : start + block])
    row = lax.broadcasted_iota(jnp.int32, (block, block), 0)
    col = lax.broadcasted_iota(jnp.int32, (block, block), 1)
    allowed = (seg_q == seg_k[:, start : start + block]) & (col <= row)
    out.append(jnp.where(allowed, s, MASKED_SCORE))
    return out


def attend_kernel(scale, place, qt_ref, kt_ref, vt_ref, segc_ref, segr_ref, o_ref, lse_ref, v_scr):
    total = qt_ref.shape[1]
    per_part = o_ref.shape[2]
    block = min(QUERY_BLOCK, per_part)
    v_scr[...] = low_t(vt_ref[...])
    for start in range(0, total, block):
        span = slice(start, start + block)
        q = (qt_ref[:, span].astype(HIGH) * scale).T.astype(LOW)
        pieces = masked_scores(q, kt_ref, segc_ref[span, :], segr_ref, start)
        top = functools.reduce(jnp.maximum, [jnp.max(s, axis=1, keepdims=True) for s in pieces])
        weights = [jnp.exp(s - top) for s in pieces]
        mass = sum(jnp.sum(w, axis=1, keepdims=True) for w in weights)
        lse_ref[0, span, :] = top + jnp.log(mass)
        inverse = 1.0 / mass
        mixed = dot_nn((weights[-1] * inverse).astype(LOW), v_scr[span, :])
        if start:
            mixed += dot_nn((weights[0] * inverse).astype(LOW), v_scr[:start, :])
        inner = start % per_part
        o_ref[place[0] ^ (start // per_part), :, inner : inner + block] = mixed.T.astype(LOW)


def attend_back_kernel(
    scale, place, qt_ref, kt_ref, vt_ref, segc_ref, segr_ref, lse_ref, *refs
):
    *do_refs, out_ref, k_scr, do_scr, dk_scr, dv_scr = refs
    total = qt_ref.shape[1]
    parts, per_part = len(do_refs), do_refs[0].shape[1]
    block = min(QUERY_BLOCK, per_part)
    k_scr[...] = low_t(kt_ref[...])
    for j in range(parts):
        do_scr[place[0] ^ j] = do_refs[j][...]
    dk_scr[...] = jnp.zeros_like(dk_scr)
    dv_scr[...] = jnp.zeros_like(dv_scr)
    for start in range(0, total, block):
        span = slice(start, start + block)
        inner = start % per_part
        qt = qt_ref[:, span].astype(HIGH) * scale
        dot_ = do_scr[start // per_part, :, inner : inner + block]
        q = qt.T.astype(LOW)
        qt = qt.astype(LOW)
        do = low_t(dot_)
        pieces = masked_scores(q, kt_ref, segc_ref[span, :], segr_ref, start)
        spans = [slice(0, start), span] if start else [span]
        lse = lse_ref[0, span, :]
        weights = [jnp.exp(s - lse) for s in pieces]
        grads = [dot_nn(do, vt_ref[:, at]) for at in spans]
        delta = sum(jnp.sum(g * w, axis=1, keepdims=True) for g, w in zip(grads, weights))
        dq = None
        for at, w, g in zip(spans, weights, grads):
            ds = (w * (g - delta)).astype(LOW)
            term = dot_nn(ds, k_scr[at, :])
            dq = term if dq is None else dq + term
            dk_scr[:, at] += dot_nn(qt, ds)
            dv_scr[:, at] += dot_nn(dot_, w.astype(LOW))
        out_ref[0, :, span] = (dq * scale).T.astype(LOW)
    out_ref[1] = dk_scr[...].astype(LOW)
    out_ref[2] = dv_scr[...].astype(LOW)


def projection_back_kernel(heads, parts, place, half, *refs):
    x_refs, (a1_ref, *refs) = refs[:parts], refs[parts:]
    head_refs, refs = refs[:heads], refs[heads:]
    wt_ref, vec_ref, grads_ref, keep_ref, send_ref, qkeep_ref, qsend_ref, *scratch = refs
    g_scr, vec_scr, sums_scr, ext_scr, all_scr, x_scr, sems = scratch
    step = pl.program_id(0)
    cols = g_scr.shape[0] // 3
    extra = grads_ref.shape[0]
    count = qkeep_ref.shape[2] - 3 * cols

    def copy(j):
        return pltpu.make_async_copy(x_refs[j], x_scr.at[j], sems.at[j])

    @pl.when(step == 0)
    def _():
        for j in range(parts):
            copy(j).start()
        g_scr[...] = jnp.zeros_like(g_scr)
        vec_scr[...] = grads_ref[...]
        sums_scr[...] = jnp.zeros_like(sums_scr)

    for j in range(parts):

        @pl.when(step == j)
        def _():
            copy(j).wait()

    dqkv = jnp.concatenate([ref[k] for k in range(3) for ref in head_refs], axis=0)
    da1 = dot_nn(low_t(dqkv), wt_ref[...])

    @pl.when(step % 2 == 0)
    def _():
        keep_ref[0] = da1.astype(LOW)

    @pl.when(step % 2 == 1)
    def _():
        send_ref[0] = da1.astype(LOW)

    g_scr[...] += dot_nn(dqkv, a1_ref[...])
    unit, _ = normalize(x_scr[step].astype(HIGH))
    vec_scr[0:1, :] += jnp.sum(da1 * unit, axis=0, keepdims=True)
    vec_scr[1:2, :] += jnp.sum(da1, axis=0, keepdims=True)
    sums_scr[...] += jnp.sum(dqkv.astype(HIGH), axis=1, keepdims=True)

    @pl.when(step == pl.num_programs(0) - 1)
    def _():
        ext_scr[...] = vec_scr[...].T
        own = pl.ds(pl.multiple_of(place[0] * cols, 16), cols)
        ext_scr[own, 2:3] = sums_scr[:cols, :]
        ext_scr[own, 3:4] = sums_scr[2 * cols :, :]
        all_scr[:, : 3 * cols] = g_scr[...].T
        all_scr[:, 3 * cols : 3 * cols + extra] = ext_scr[...]
        rows = all_scr.shape[0] // parts
        for r in range(parts):
            for ref, side in ((qkeep_ref, half[0]), (qsend_ref, 1 - half[0])):
                start = pl.multiple_of(r * rows + side * (rows // 2), 16)
                ref[r] = all_scr[pl.ds(start, rows // 2), : 3 * cols + count].astype(LOW)


GELU_C = 0.7978845608028654
GELU_A = 0.044715


def mlp_kernel(
    parts, first_blocks, place, half, live_ref, x_ref, cot_ref, vec_ref, *refs
):
    o_refs, refs = refs[:parts], refs[parts:]
    own_ref, core_ref, *wide_refs = refs[:10]
    out_ref, *grad_refs = refs[10:15]
    dr1_ref, vecg_ref, *refs = refs[15:]
    do_refs, scratch = refs[:parts], refs[parts:]
    wide, ot_scr, r1_scr, a2_scr, a2t_scr, dy_scr, dyt_scr, y_scr, da2_scr, act_scr, sems = scratch
    step = pl.program_id(0)
    rows = o_refs[0].shape[0]
    slots, width = x_ref.shape
    bo, gain, shift, bp = (vec_ref[r : r + 1, :] for r in (4, 5, 6, 11))
    split = wide_refs[0].shape[1]
    live = lax.broadcasted_iota(jnp.int32, (slots, 1), 0) < live_ref[0]

    def copies(k):
        half_rows = rows // 2
        near, far = half[0] * half_rows, (1 - half[0]) * half_rows
        span = slice(0, split) if k == 0 else slice(split, wide.shape[1])
        sources = [(own_ref.at[:, span], 0, 0), (core_ref.at[:, span], 1, 0)]
        spots = [(2, near), (2, far), (3, near), (3, far)]
        sources += [(wide_refs[4 * k + n], *spot) for n, spot in enumerate(spots)]
        for n, (source, j, offset) in enumerate(sources):
            start = pl.multiple_of((place[0] ^ j) * rows + offset, 16)
            target = wide.at[pl.ds(start, source.shape[0]), span]
            yield pltpu.make_async_copy(source, target, sems.at[k, n])

    def block(n):
        return wide[:, pl.ds(pl.multiple_of(n * width, 128), width)]

    def permuted(scratch, value):
        for j in range(parts):
            scratch[j * rows : (j + 1) * rows, :] = value(pl.multiple_of((place[0] ^ j) * rows, 16))

    def put(value):
        value = value.astype(LOW)
        for k in range(2):

            @pl.when((step >= first_blocks) == bool(k))
            def _():
                keep, send = grad_refs[2 * k : 2 * k + 2]
                for j in range(parts):
                    (send if j % 2 else keep)[j // 2] = value[j * rows : (j + 1) * rows, :]

    @pl.when(step == 0)
    def _():
        for k in range(2):
            for copy in copies(k):
                copy.start()
        for j in range(parts):
            start = pl.multiple_of((place[0] ^ j) * rows, 16)
            ot_scr[pl.ds(start, rows), :] = o_refs[j][...]
        mixed = low_t(ot_scr[...])
        dy = jnp.where(live, cot_ref[...].astype(HIGH), 0.0)
        dy_scr[...] = dy.astype(LOW)
        ot_scr[...] = dy.T.astype(LOW)
        permuted(dyt_scr, lambda start: ot_scr[pl.ds(start, rows), :])
        for copy in copies(0):
            copy.wait()
        r1 = x_ref[...].astype(HIGH) + dot_nn(mixed, wide[:, :width]) + bo
        r1_scr[...] = r1
        unit, _ = normalize(r1)
        a2 = unit * gain + shift
        a2_scr[...] = a2.astype(LOW)
        ot_scr[...] = a2.T.astype(LOW)
        permuted(a2t_scr, lambda start: ot_scr[pl.ds(start, rows), :])
        vecg_ref[...] = jnp.zeros_like(vecg_ref)
        vecg_ref[11:12, :] = jnp.sum(dy, axis=0, keepdims=True)
        y_scr[...] = r1 + bp
        da2_scr[...] = jnp.zeros_like(da2_scr)

    @pl.when(step == split // width - 1)
    def _():
        for copy in copies(1):
            copy.wait()

    last = pl.num_programs(0) - 1

    @pl.when((step < last) & (step % 2 == 0))
    def _():
        w_fc, w_pt = block(1 + step), block(2 + step)
        u = dot_nn(a2_scr[...], w_fc) + vec_ref[pl.ds(7 + step // 2, 1), :]
        square = u * u
        t = jnp.tanh(GELU_C * (u + GELU_A * (square * u)))
        grown = 0.5 * (1.0 + t)
        act = (u * grown).astype(LOW)
        act_scr[...] = act
        y_scr[...] += dot_nt(act, w_pt)
        slope = grown + 0.5 * u * (1.0 - t * t) * (GELU_C + (3.0 * GELU_C * GELU_A) * square)
        du = (dot_nn(dy_scr[...], w_pt) * slope).astype(LOW)
        vecg_ref[pl.ds(7 + step // 2, 1), :] = jnp.sum(du.astype(HIGH), axis=0, keepdims=True)
        da2_scr[...] += dot_nt(du, w_fc)
        put(dot_nn(a2t_scr[...], du))

    @pl.when((step < last) & (step % 2 == 1))
    def _():
        put(dot_nn(dyt_scr[...], act_scr[...]))

    @pl.when(step == last)
    def _():
        out_ref[...] = jnp.where(live, y_scr[...], 0.0).astype(LOW)
        unit, inverse = normalize(r1_scr[...])
        da2 = da2_scr[...]
        vecg_ref[5:6, :] = jnp.sum(da2 * unit, axis=0, keepdims=True)
        vecg_ref[6:7, :] = jnp.sum(da2, axis=0, keepdims=True)
        dr1 = dy_scr[...].astype(HIGH) + normalize_back(unit, inverse, da2 * gain)
        dr1_ref[...] = dr1
        low = dr1.astype(LOW)
        vecg_ref[4:5, :] = jnp.sum(low.astype(HIGH), axis=0, keepdims=True)
        put(dot_nn(jnp.concatenate([ref[...] for ref in o_refs], axis=0), low))
        for j in range(parts):
            start = pl.multiple_of((place[0] ^ j) * rows, 16)
            do_refs[j][...] = dot_nt(wide[pl.ds(start, rows), :width], low).astype(LOW)


def group_layout(length_row, count_row, slots):
    starts = jnp.cumsum(count_row) - count_row
    within = jnp.arange(slots, dtype=jnp.int32)
    position = (starts[:, None] + within[None, :]).reshape(-1)
    live_rows = (within[None, :] < count_row[:, None]).reshape(-1)
    boundary = jnp.cumsum(length_row)
    segment = jnp.sum((position[:, None] >= boundary[None, :]).astype(jnp.int32), axis=1)
    buffer_slot = jnp.arange(position.shape[0], dtype=jnp.int32)
    return jnp.where(live_rows, segment, -1 - buffer_slot)


def adam_update(master, first, second, gradient, factor, rate, decay):
    clipped = gradient * factor
    first_new = BETA_FIRST * first + (1.0 - BETA_FIRST) * clipped
    second_new = BETA_SECOND * second + (1.0 - BETA_SECOND) * clipped * clipped
    first_hat = first_new / (1.0 - BETA_FIRST**STEP)
    second_hat = second_new / (1.0 - BETA_SECOND**STEP)
    master_new = master - rate * (
        first_hat / (jnp.sqrt(second_hat) + ADAM_EPSILON) + decay * master
    )
    return (clipped, master_new, first_new, second_new)


def adam_kernel(fc_rows, factor_ref, _, *refs):
    grads, states, outs = refs[:3], refs[3:9], refs[9:]
    near = pl.program_id(0) < pl.num_programs(0) // 2
    factor = factor_ref[0]
    width = outs[0].shape[-1] // fc_rows
    qkv = jnp.where(near, grads[1][0], grads[2][0])[:, : 3 * width]

    def update(gradient, at, base):
        results = adam_update(
            *[states[base + n][at] for n in range(3)],
            gradient.astype(HIGH), factor, RATE_MATRIX, DECAY_MATRIX,
        )
        for n, result in enumerate(results):
            outs[base // 3 * 4 + n][at] = result

    blocks = [grads[0][0, :, n : n + width] for n in range(0, grads[0].shape[2], width)]
    for f in range(fc_rows):
        span = slice(f * width, (f + 1) * width)
        for n in range(2):
            update(blocks[2 * f + n], (n, 0, slice(None), span), 3)
    update(qkv, (0, slice(None), slice(0, 3 * width)), 0)
    update(blocks[-1], (0, slice(None), slice(3 * width, 4 * width)), 0)


def swap(array, axis, bit, count):
    return lax.ppermute(array, axis, [(i, i ^ bit) for i in range(count)])


def pick(array, index):
    return lax.dynamic_index_in_dim(array, index, 0, keepdims=False)


def deal(pieces, parts):
    return list(pieces[:1]) + [swap(pieces[j], "shard", j, parts) for j in range(1, parts)]


def in_order(relative, place, parts):
    relative = jnp.stack(relative)
    return jnp.stack([pick(relative, place ^ r) for r in range(parts)])


def collect(own, parts):
    have = [own]
    bit = parts // 2
    slots = [0]
    while bit:
        have = have + [swap(piece, "shard", bit, parts) for piece in have]
        slots = slots + [s ^ bit for s in slots]
        bit //= 2
    return [have[slots.index(j)] for j in range(parts)]


def after(value, *others):
    return lax.optimization_barrier((value, *others))[0]


def add_low(a, b):
    return (a.astype(HIGH) + b.astype(HIGH)).astype(LOW)


def bits_of(count):
    return [1 << n for n in range(count.bit_length() - 1)]


def halve(array, upper, dim):
    length = array.shape[dim] // 2
    keep = lax.dynamic_slice_in_dim(array, upper * length, length, dim)
    return keep, lax.dynamic_slice_in_dim(array, (1 - upper) * length, length, dim)


def scatter_half(array, dim, bit, replica, replicas):
    keep, send = halve(array, (replica // bit) % 2, dim)
    return keep, swap(send, "dp", bit, replicas)


def params(mebibytes):
    return pltpu.CompilerParams(
        dimension_semantics=("arbitrary",), vmem_limit_bytes=mebibytes * 1024 * 1024
    )


def cost(flops, moved, special=0):
    return pl.CostEstimate(flops=int(flops), bytes_accessed=int(moved), transcendentals=int(special))


def whole(*shape):
    zeros = (0,) * len(shape)
    return pl.BlockSpec(shape, lambda *_: zeros)


def make_on_device(parts, replicas):
    def on_device(
        tokens, cotangent, lengths, counts,
        attn_w, attn_m, attn_v, mlp_w, mlp_m, mlp_v, vec_w, vec_m, vec_v,
    ):
        slots, width = tokens.shape
        rows = attn_w.shape[0]
        hidden = mlp_w.shape[2]
        fc_rows = hidden // width
        total = parts * slots
        head_size = width // HEADS
        own_heads = HEADS // parts
        own_cols = own_heads * head_size
        scale = head_size ** (-0.5)
        place = lax.axis_index("shard")
        replica = lax.axis_index("dp")
        prefetch = place.reshape(1).astype(jnp.int32)

        half = replica % 2
        side = half.reshape(1).astype(jnp.int32)

        x_all = collect(tokens, parts)
        w_pieces = pl.pallas_call(
            cut_kernel,
            grid_spec=pltpu.PrefetchScalarGridSpec(
                num_scalar_prefetch=1,
                grid=(1,),
                in_specs=[whole(rows, 3 * width), whole(vec_w.shape[0], rows)],
                out_specs=[whole(rows + 16, 3 * own_cols)] * parts,
            ),
            out_shape=[jax.ShapeDtypeStruct((rows + 16, 3 * own_cols), LOW)] * parts,
            compiler_params=params(12),
            cost_estimate=cost(0, 4e6),
            name="cut",
        )(prefetch, attn_w, vec_w)
        w_local = deal(w_pieces, parts)

        blocks = 2 * fc_rows + 1
        split = (fc_rows // 2 * 2 + 1) * width
        wide_own, *wide_half = pl.pallas_call(
            widen_kernel,
            grid_spec=pltpu.PrefetchScalarGridSpec(
                num_scalar_prefetch=1,
                grid=(1,),
                in_specs=[
                    pl.BlockSpec((rows, width), lambda *_: (0, 3)),
                    whole(2, rows, hidden),
                ],
                out_specs=[
                    whole(rows, blocks * width),
                    whole(rows // 2, split),
                    whole(rows // 2, blocks * width - split),
                ],
            ),
            out_shape=[
                jax.ShapeDtypeStruct((rows, blocks * width), LOW),
                jax.ShapeDtypeStruct((rows // 2, split), LOW),
                jax.ShapeDtypeStruct((rows // 2, blocks * width - split), LOW),
            ],
            compiler_params=params(28),
            cost_estimate=cost(0, 12e6),
            name="widen",
        )(side, attn_w, mlp_w)
        wide_own, *wide_half = lax.optimization_barrier((wide_own, *wide_half, *w_local, *x_all))[:3]
        near = [swap(mine, "shard", parts // 2, parts) for mine in wide_half]
        wide_core = swap(wide_own, "shard", 1, parts)

        segment = group_layout(lengths[0], counts[0], slots)
        seg_col = segment[:, None]
        seg_row = segment[None, :]
        own_vec = vec_w.astype(LOW).astype(HIGH)
        bias_local = jnp.concatenate(
            [own_vec[2], jnp.zeros((own_cols,), HIGH), own_vec[3]]
        )[:, None]

        a1, qkv, w_t, vectors = pl.pallas_call(
            functools.partial(project_kernel, parts),
            grid_spec=pltpu.PrefetchScalarGridSpec(
                num_scalar_prefetch=1,
                grid=(parts,),
                in_specs=[
                    *[pl.BlockSpec(memory_space=pl.ANY)] * parts,
                    *[whole(rows + 16, 3 * own_cols)] * parts,
                    whole(3 * own_cols, 1),
                ],
                out_specs=[
                    pl.BlockSpec((slots, width), lambda i, p: (p[0] ^ i, 0)),
                    pl.BlockSpec((3 * own_cols, slots), lambda i, p: (0, p[0] ^ i)),
                    whole(3 * own_cols, width),
                    whole(16, width),
                ],
                scratch_shapes=[
                    pltpu.VMEM((width, 3 * own_cols), HIGH),
                    pltpu.VMEM((parts, slots, width), LOW),
                    pltpu.SemaphoreType.DMA((parts,)),
                ],
            ),
            out_shape=[
                jax.ShapeDtypeStruct((total, width), LOW),
                jax.ShapeDtypeStruct((3 * own_cols, total), LOW),
                jax.ShapeDtypeStruct((3 * own_cols, width), LOW),
                jax.ShapeDtypeStruct((16, width), HIGH),
            ],
            compiler_params=params(24),
            cost_estimate=cost(2 * total * width * 3 * own_cols * 3, 12e6),
            name="project",
        )(prefetch, *x_all, *w_local, bias_local)

        pair_flops = 2 * total * total * head_size * 4 // 2

        def head_specs(h):
            return [
                pl.BlockSpec((head_size, total), functools.partial(lambda k, *_: (k * own_heads + h, 0), k))
                for k in range(3)
            ]

        def attend(h, qkv):
            return pl.pallas_call(
                functools.partial(attend_kernel, scale),
                grid_spec=pltpu.PrefetchScalarGridSpec(
                    num_scalar_prefetch=1,
                    grid=(1,),
                    in_specs=head_specs(h) + [whole(total, 1), whole(1, total)],
                    out_specs=[whole(parts, head_size, slots), whole(1, total, 1)],
                    scratch_shapes=[pltpu.VMEM((total, head_size), LOW)],
                ),
                out_shape=[
                    jax.ShapeDtypeStruct((parts, head_size, slots), LOW),
                    jax.ShapeDtypeStruct((1, total, 1), HIGH),
                ],
                compiler_params=params(24),
                cost_estimate=cost(2 * pair_flops, 4e6, total * total // 2),
                name="attend",
            )(prefetch, qkv, qkv, qkv, seg_col, seg_row)

        mixed, lse = [], []
        for h in range(own_heads):
            if h == 1:
                qkv, near[0] = lax.optimization_barrier((qkv, near[0]))
                far = [swap(near[0], "dp", 1, replicas)]
                turned = [swap(near[0], "shard", 1, parts)]
            head_mixed, head_lse = attend(h, qkv)
            mixed.append(head_mixed)
            lse.append(head_lse)
        near[1] = after(near[1], mixed[-1])
        far.append(swap(near[1], "dp", 1, replicas))
        mixed_own = deal(
            [jnp.concatenate([head[j] for head in mixed], axis=0) for j in range(parts)], parts
        )
        turned.append(swap(near[1], "shard", 1, parts))
        wide = [wide_own, wide_core]
        for k in range(2):
            wide += [near[k], far[k], turned[k], swap(far[k], "shard", 1, parts)]

        steps = blocks
        live_own = lax.dynamic_index_in_dim(counts[0], place, 0, keepdims=True)
        first_blocks = fc_rows // 2 * 2 + 1

        def grad_spec(k):
            first, last = ((0, first_blocks - 1), (first_blocks, steps - 1))[k]
            return pl.BlockSpec(
                (parts // 2, rows, width), lambda i, *_: (0, 0, jnp.clip(i, first, last) - first)
            )

        grad_columns = [first_blocks * width, (steps - first_blocks) * width]

        in_hbm = pl.BlockSpec(memory_space=pltpu.HBM)
        out = pl.pallas_call(
            functools.partial(mlp_kernel, parts, first_blocks),
            grid_spec=pltpu.PrefetchScalarGridSpec(
                num_scalar_prefetch=3,
                grid=(steps,),
                in_specs=[whole(slots, width), whole(slots, width), whole(16, width)]
                + [whole(own_cols, slots)] * parts
                + [in_hbm] * len(wide),
                out_specs=[whole(slots, width)]
                + [grad_spec(k) for k in range(2) for _ in range(2)]
                + [whole(slots, width), whole(16, width)]
                + [whole(own_cols, slots)] * parts,
                scratch_shapes=[
                    pltpu.VMEM((width, blocks * width), LOW),
                    pltpu.VMEM((width, slots), LOW),
                    pltpu.VMEM((slots, width), HIGH),
                    pltpu.VMEM((slots, width), LOW),
                    pltpu.VMEM((width, slots), LOW),
                    pltpu.VMEM((slots, width), LOW),
                    pltpu.VMEM((width, slots), LOW),
                    pltpu.VMEM((slots, width), HIGH),
                    pltpu.VMEM((slots, width), HIGH),
                    pltpu.VMEM((slots, width), LOW),
                    pltpu.SemaphoreType.DMA((2, 6)),
                ],
            ),
            out_shape=[jax.ShapeDtypeStruct((slots, width), LOW)]
            + [jax.ShapeDtypeStruct((parts // 2, rows, c), LOW) for c in grad_columns for _ in range(2)]
            + [jax.ShapeDtypeStruct((slots, width), HIGH), jax.ShapeDtypeStruct((16, width), HIGH)]
            + [jax.ShapeDtypeStruct((own_cols, slots), LOW)] * parts,
            compiler_params=params(50),
            cost_estimate=cost(2 * slots * width * (6 * hidden + 3 * width), 30e6, slots * hidden),
            name="mlp",
        )(prefetch, side, live_own, tokens, cotangent, vectors, *mixed_own, *wide)
        block_out, keep_a, send_a, keep_b, send_b, grad_resid, mid_grads, *do_pieces = out

        do_own = deal(do_pieces, parts)
        got_a = swap(send_a, "shard", 1, parts)
        got_b = swap(send_b, "shard", 1, parts)
        own_a, other_a = [add_low(keep_a[n], got_a[n]) for n in range(2)]
        got_a = swap(other_a, "shard", parts // 2, parts)
        got_b = after(got_b, own_a, other_a)
        own_b, other_b = halve(add_low(keep_b, got_b), half, 1)
        *do_own, own_b, other_b = lax.optimization_barrier((*do_own, own_b, other_b))
        got_b = swap(other_b, "dp", 1, replicas)

        def attend_back(h, qkv):
            return pl.pallas_call(
                functools.partial(attend_back_kernel, scale),
                grid_spec=pltpu.PrefetchScalarGridSpec(
                    num_scalar_prefetch=1,
                    grid=(1,),
                    in_specs=head_specs(h)
                    + [whole(total, 1), whole(1, total), whole(1, total, 1)]
                    + [pl.BlockSpec((head_size, slots), lambda *_: (h, 0))] * parts,
                    out_specs=whole(3, head_size, total),
                    scratch_shapes=[
                        pltpu.VMEM((total, head_size), LOW),
                        pltpu.VMEM((parts, head_size, slots), LOW),
                        pltpu.VMEM((head_size, total), HIGH),
                        pltpu.VMEM((head_size, total), HIGH),
                    ],
                ),
                out_shape=jax.ShapeDtypeStruct((3, head_size, total), LOW),
                compiler_params=params(28),
                cost_estimate=cost(
                    5 * pair_flops, 4e6, total * total // 2
                ),
                name="attend_back",
            )(prefetch, qkv, qkv, qkv, seg_col, seg_row, lse[h], *do_own)

        dqkv = [attend_back(h, qkv) for h in range(own_heads)]
        *dqkv, got_a, got_b = lax.optimization_barrier((*dqkv, got_a, got_b))
        own_a, other_a = halve(add_low(own_a, got_a), half, 0)
        got_a = swap(other_a, "dp", 1, replicas)
        own_b, other_b = [add_low(own_b[n], got_b[n]) for n in range(2)]
        got_b = swap(other_b, "shard", parts // 2, parts)
        dqkv[0] = after(dqkv[0], other_a, own_b, other_b)

        q_cols = 3 * own_cols
        extra = vec_w.shape[0]
        half_rows = rows // 2
        da1_keep, da1_send, own_q, other_q = pl.pallas_call(
            functools.partial(projection_back_kernel, own_heads, parts),
            grid_spec=pltpu.PrefetchScalarGridSpec(
                num_scalar_prefetch=2,
                grid=(parts,),
                in_specs=[
                    *[pl.BlockSpec(memory_space=pl.ANY)] * parts,
                    pl.BlockSpec((slots, width), lambda i, p, _: (p[0] ^ i, 0)),
                ]
                + [pl.BlockSpec((3, head_size, slots), lambda i, p, _: (0, 0, p[0] ^ i))] * own_heads
                + [whole(q_cols, width), whole(16, width), whole(16, width)],
                out_specs=[pl.BlockSpec((1, slots, width), lambda i, *_: (i // 2, 0, 0))] * 2
                + [whole(parts, half_rows, q_cols + extra)] * 2,
                scratch_shapes=[
                    pltpu.VMEM((q_cols, width), HIGH),
                    pltpu.VMEM((16, width), HIGH),
                    pltpu.VMEM((q_cols, 1), HIGH),
                    pltpu.VMEM((width, 16), HIGH),
                    pltpu.VMEM((width, q_cols + 64), HIGH),
                    pltpu.VMEM((parts, slots, width), LOW),
                    pltpu.SemaphoreType.DMA((parts,)),
                ],
            ),
            out_shape=[jax.ShapeDtypeStruct((parts // 2, slots, width), LOW)] * 2
            + [jax.ShapeDtypeStruct((parts, half_rows, q_cols + extra), LOW)] * 2,
            compiler_params=params(28),
            cost_estimate=cost(4 * total * width * 3 * own_cols * 2, 16e6),
            name="projection_back",
        )(prefetch, side, *x_all, a1, *dqkv, w_t, vectors, mid_grads)

        share = rows // replicas
        z_bits = [bit for bit in (1 << n for n in range(1, 20)) if bit < replicas]
        last_event = [own_q]

        def seen(value):
            return lax.optimization_barrier((value, last_event[0]))[0]

        def event(value):
            last_event[0] = value
            return value

        def next_half(keep, got, bit, dim):
            array = event(add_low(keep, seen(got)))
            return scatter_half(array, dim, bit, replica, replicas)

        got_q = swap(other_q, "dp", 1, replicas)
        da1_got = swap(da1_send, "shard", 1, parts)
        state_a = next_half(own_a, got_a, z_bits[0], 0)
        state_b = next_half(own_b, got_b, z_bits[0], 0)
        for bit in z_bits[1:]:
            state_a = next_half(*state_a, bit, 0)
        state_q = next_half(own_q, got_q, z_bits[0], 1)
        for bit in z_bits[1:]:
            state_b = next_half(*state_b, bit, 0)
        part_a = event(add_low(state_a[0], seen(state_a[1])))
        for bit in z_bits[1:]:
            state_q = next_half(*state_q, bit, 1)
        part_b = event(add_low(state_b[0], seen(state_b[1])))
        part_ab = event(jnp.concatenate([part_a, part_b], axis=1))
        all_ab = lax.all_gather(part_ab, "dp", axis=0)
        part_q = event(add_low(state_q[0], seen(state_q[1])))

        def as_pair(value):
            high = lax.reduce_precision(value, 8, 7)
            return jnp.stack([high, value - high]).astype(LOW)

        main = part_q[:, :, :q_cols]
        squares = sum(jnp.sum(jnp.square(p.astype(HIGH))) for p in (part_ab, main))
        vec_parts = part_q[:, :, q_cols:].transpose(1, 0, 2).reshape(1, share, parts * extra)
        shared = jnp.concatenate(
            [vec_parts, jnp.broadcast_to(as_pair(squares), (1, share, 2))], axis=2
        )
        pieces = jnp.concatenate([main, jnp.broadcast_to(shared, (parts,) + shared.shape[1:])], axis=2)
        dealt = in_order(deal([pick(pieces, place ^ j) for j in range(parts)], parts), place, parts)
        q_rows = (
            dealt[:, :, :q_cols]
            .reshape(parts, share, 3, own_cols)
            .transpose(1, 2, 0, 3)
            .reshape(share, 3 * width)
        )
        summed = jnp.sum(dealt[:, :, q_cols:].astype(HIGH), axis=0)
        vec_parts = summed[:, : parts * extra].reshape(share, parts, extra).astype(LOW)
        squares = jnp.sum(summed[0, parts * extra :]) + jnp.sum(jnp.square(vec_parts.astype(HIGH)))
        vec_own = lax.dynamic_index_in_dim(vec_parts, place, 1, keepdims=False)
        near_q = jnp.concatenate(
            [q_rows, vec_own, jnp.broadcast_to(as_pair(squares), (share, 2))], axis=1
        )[None]
        for bit in z_bits[::-1]:
            near_q = jnp.concatenate([near_q, swap(near_q, "dp", bit, replicas)], axis=0)
        far_q = swap(near_q, "dp", 1, replicas)

        def block_of(index):
            block = index % 2
            for bit in z_bits:
                block = block * 2 + index // bit % 2
            return block

        def index_of(block):
            index = 0
            for bit in z_bits[::-1]:
                index = index + block % 2 * bit
                block = block // 2
            return index + block

        turn = block_of(replica)
        small = jnp.concatenate([near_q[:, :, 3 * width :], far_q[:, :, 3 * width :]], axis=0)
        small = jnp.stack([pick(small, turn ^ r) for r in range(replicas)]).astype(HIGH)
        summed_vec = small[:, :, :extra].reshape(rows, extra).T
        squares = jnp.sum(small[:, 0, extra:])

        own_da1 = da1_keep[0].astype(HIGH) + da1_got[0].astype(HIGH)
        da1 = own_da1 + swap(add_low(da1_keep[1], da1_got[1]), "shard", 2, parts).astype(HIGH)
        unit, inverse = normalize(tokens.astype(HIGH))
        grad_input = grad_resid + normalize_back(unit, inverse, da1 * vectors[0:1])
        live_rows = jnp.arange(slots, dtype=jnp.int32) < live_own[0]
        grad_in = jnp.where(live_rows[:, None], grad_input, 0.0).astype(LOW)

        norm_total = jnp.sqrt(squares)
        factor = jnp.minimum(1.0, CLIP_LIMIT / (norm_total + 1e-06))
        near_count = replicas // 2
        q_block = (1,) + near_q.shape[1:]

        def gathered_spec(array):
            return pl.BlockSpec((1,) + array.shape[1:], lambda i, _, p: (index_of(i ^ p[0]), 0, 0))

        attn_shape = (replicas, share, 4 * width)
        mlp_shape = (2, replicas, share, hidden)
        attn_spec = pl.BlockSpec((1, share, 4 * width), lambda i, _, p: (i ^ p[0], 0, 0))
        mlp_spec = pl.BlockSpec((2, 1, share, hidden), lambda i, _, p: (0, i ^ p[0], 0, 0))
        updated = pl.pallas_call(
            functools.partial(adam_kernel, fc_rows),
            grid_spec=pltpu.PrefetchScalarGridSpec(
                num_scalar_prefetch=2,
                grid=(replicas,),
                in_specs=[gathered_spec(all_ab)]
                + [
                    pl.BlockSpec(q_block, lambda i, *_: (jnp.minimum(i, near_count - 1), 0, 0)),
                    pl.BlockSpec(q_block, lambda i, *_: (jnp.maximum(i - near_count, 0), 0, 0)),
                ]
                + [attn_spec] * 3
                + [mlp_spec] * 3,
                out_specs=[attn_spec] * 4 + [mlp_spec] * 4,
            ),
            out_shape=[jax.ShapeDtypeStruct(attn_shape, HIGH)] * 4
            + [jax.ShapeDtypeStruct(mlp_shape, HIGH)] * 4,
            compiler_params=params(50),
            cost_estimate=cost(30 * 9 * rows * width, 54e6),
            name="adam",
        )(
            factor.reshape(1),
            turn.reshape(1).astype(jnp.int32),
            all_ab,
            near_q,
            far_q,
            *[array.reshape(attn_shape) for array in (attn_w, attn_m, attn_v)],
            *[array.reshape(mlp_shape) for array in (mlp_w, mlp_m, mlp_v)],
        )
        attn_grad, attn_w_new, attn_m_new, attn_v_new = [u.reshape(attn_w.shape) for u in updated[:4]]
        mlp_grad, mlp_w_new, mlp_m_new, mlp_v_new = [u.reshape(mlp_w.shape) for u in updated[4:]]
        vec_grad, vec_w_new, vec_m_new, vec_v_new = adam_update(
            vec_w, vec_m, vec_v, summed_vec, factor, RATE_VECTOR, 0.0
        )
        return (
            block_out, grad_in, attn_grad, mlp_grad, vec_grad,
            attn_w_new, attn_m_new, attn_v_new, mlp_w_new, mlp_m_new, mlp_v_new,
            vec_w_new, vec_m_new, vec_v_new, norm_total.reshape(1),
        )

    return on_device


def solution(mesh):
    tokens = P(("dp", "shard"), None)
    groups = P("dp", None)
    attn = P("shard", None)
    mlp = P(None, "shard", None)
    vec = P(None, "shard")
    return jax.shard_map(
        make_on_device(mesh.shape["shard"], mesh.shape["dp"]),
        mesh=mesh,
        in_specs=(tokens, tokens, groups, groups) + (attn,) * 3 + (mlp,) * 3 + (vec,) * 3,
        out_specs=(tokens, tokens, attn, mlp, vec) + (attn,) * 3 + (mlp,) * 3 + (vec,) * 3 + (P(),),
        check_vma=False,
    )
```

```python
import functools

import jax
import jax.numpy as jnp
from jax import lax
from jax.experimental import pallas as pl
from jax.experimental.pallas import tpu as pltpu
from jax.sharding import PartitionSpec as P

HEADS = 12
STEP = 10
NORM_EPSILON = 1e-05
BETA_FIRST = 0.9
BETA_SECOND = 0.999
ADAM_EPSILON = 1e-08
RATE_MATRIX = 0.1
RATE_VECTOR = 0.2
DECAY_MATRIX = 0.1
CLIP_LIMIT = 1.0
MASKED_SCORE = -1e30
QUERY_BLOCK = 256
LOW = jnp.bfloat16
HIGH = jnp.float32


def dot_nn(a, b):
    return lax.dot_general(a, b, (((1,), (0,)), ((), ())), preferred_element_type=HIGH)


def dot_nt(a, b):
    return lax.dot_general(a, b, (((1,), (1,)), ((), ())), preferred_element_type=HIGH)


def low_t(a):
    return a.astype(HIGH).T.astype(LOW)


def normalize(features):
    centered = features - jnp.mean(features, axis=-1, keepdims=True)
    variance = jnp.mean(centered * centered, axis=-1, keepdims=True)
    inverse = lax.rsqrt(variance + NORM_EPSILON)
    return centered * inverse, inverse


def normalize_back(unit, inverse, grad_unit):
    first = jnp.mean(grad_unit, axis=-1, keepdims=True)
    second = jnp.mean(grad_unit * unit, axis=-1, keepdims=True)
    return inverse * (grad_unit - first - unit * second)


def cut_kernel(place, w_ref, vec_ref, *out_refs):
    parts = len(out_refs)
    rows, columns = w_ref.shape
    width = columns // 3
    cols = width // parts
    vec = vec_ref[...]
    tail = [
        jnp.concatenate([vec[3 * k + m : 3 * k + m + 1, :] for m in range(3)], axis=1)
        for k in range(vec.shape[0] // 3)
    ]
    tail.append(jnp.zeros((16 - len(tail), 3 * cols), HIGH))
    tail = jnp.concatenate(tail, axis=0).astype(LOW)
    for r in range(parts):
        starts = [k * width + r * cols for k in range(3)]
        piece = jnp.concatenate([w_ref[:, c : c + cols] for c in starts], axis=1).astype(LOW)
        for j in range(parts):

            @pl.when((place[0] ^ j) == r)
            def _():
                out_refs[j][:rows, :] = piece
                out_refs[j][rows:, :] = tail


def widen_kernel(half, out_ref, mlp_ref, wide_ref, *half_refs):
    rows, width = out_ref.shape
    start = pl.multiple_of(half[0] * (rows // 2), 16)
    near = pl.ds(start, rows // 2)
    sources = [(out_ref[...], out_ref[near, :])]
    for f in range(mlp_ref.shape[2] // width):
        span = slice(f * width, (f + 1) * width)
        sources += [(mlp_ref[n, :, span], mlp_ref[n, near, span]) for n in range(2)]
    split = half_refs[0].shape[1] // width
    for n, (block, part) in enumerate(sources):
        wide_ref[:, n * width : (n + 1) * width] = block.astype(LOW)
        k = int(n >= split)
        at = (n - k * split) * width
        half_refs[k][:, at : at + width] = part.astype(LOW)


def project_kernel(parts, place, *refs):
    x_refs, w_refs, refs = refs[:parts], refs[parts : 2 * parts], refs[2 * parts :]
    bias_ref, a1_ref, qkv_ref, wt_ref, vec_ref, w_scr, x_scr, sems = refs
    step = pl.program_id(0)
    rows = vec_ref.shape[1] // parts

    def copy(j):
        return pltpu.make_async_copy(x_refs[j], x_scr.at[j], sems.at[j])

    @pl.when(step == 0)
    def _():
        for j in range(parts):
            copy(j).start()
        vec_ref[...] = jnp.zeros_like(vec_ref)
        for j in range(parts):
            start = pl.multiple_of((place[0] ^ j) * rows, 16)
            w_scr[pl.ds(start, rows), :] = w_refs[j][:rows, :].astype(HIGH)
            tail = w_refs[j][rows:, :].astype(HIGH)
            for r in range(parts):

                @pl.when((place[0] ^ j) == r)
                def _():
                    for n in range(12):
                        piece = tail[n // 3 : n // 3 + 1, n % 3 * rows : (n % 3 + 1) * rows]
                        vec_ref[n : n + 1, r * rows : (r + 1) * rows] = piece

        wt_ref[...] = w_scr[...].T.astype(LOW)

    for j in range(parts):

        @pl.when(step == j)
        def _():
            copy(j).wait()

    unit, _ = normalize(x_scr[step].astype(HIGH))
    a1 = (unit * vec_ref[0:1, :] + vec_ref[1:2, :]).astype(LOW)
    a1_ref[...] = a1
    qkv_ref[...] = (dot_nt(wt_ref[...], a1) + bias_ref[...]).astype(LOW)


def masked_scores(q, kt, seg_q, seg_k, start):
    block = q.shape[0]
    out = []
    if start:
        s = dot_nn(q, kt[:, :start])
        out.append(jnp.where(seg_q == seg_k[:, :start], s, MASKED_SCORE))
    s = dot_nn(q, kt[:, start : start + block])
    row = lax.broadcasted_iota(jnp.int32, (block, block), 0)
    col = lax.broadcasted_iota(jnp.int32, (block, block), 1)
    allowed = (seg_q == seg_k[:, start : start + block]) & (col <= row)
    out.append(jnp.where(allowed, s, MASKED_SCORE))
    return out


def attend_kernel(scale, place, qt_ref, kt_ref, vt_ref, segc_ref, segr_ref, o_ref, lse_ref, v_scr):
    total = qt_ref.shape[1]
    per_part = o_ref.shape[2]
    block = min(QUERY_BLOCK, per_part)
    v_scr[...] = low_t(vt_ref[...])
    for start in range(0, total, block):
        span = slice(start, start + block)
        q = (qt_ref[:, span].astype(HIGH) * scale).T.astype(LOW)
        pieces = masked_scores(q, kt_ref, segc_ref[span, :], segr_ref, start)
        top = functools.reduce(jnp.maximum, [jnp.max(s, axis=1, keepdims=True) for s in pieces])
        weights = [jnp.exp(s - top) for s in pieces]
        mass = sum(jnp.sum(w, axis=1, keepdims=True) for w in weights)
        lse_ref[0, span, :] = top + jnp.log(mass)
        inverse = 1.0 / mass
        mixed = dot_nn((weights[-1] * inverse).astype(LOW), v_scr[span, :])
        if start:
            mixed += dot_nn((weights[0] * inverse).astype(LOW), v_scr[:start, :])
        inner = start % per_part
        o_ref[place[0] ^ (start // per_part), :, inner : inner + block] = mixed.T.astype(LOW)


def attend_back_kernel(
    scale, place, qt_ref, kt_ref, vt_ref, segc_ref, segr_ref, lse_ref, *refs
):
    *do_refs, out_ref, k_scr, do_scr, dk_scr, dv_scr = refs
    total = qt_ref.shape[1]
    parts, per_part = len(do_refs), do_refs[0].shape[1]
    block = min(QUERY_BLOCK, per_part)
    k_scr[...] = low_t(kt_ref[...])
    for j in range(parts):
        do_scr[place[0] ^ j] = do_refs[j][...]
    dk_scr[...] = jnp.zeros_like(dk_scr)
    dv_scr[...] = jnp.zeros_like(dv_scr)
    for start in range(0, total, block):
        span = slice(start, start + block)
        inner = start % per_part
        qt = qt_ref[:, span].astype(HIGH) * scale
        dot_ = do_scr[start // per_part, :, inner : inner + block]
        q = qt.T.astype(LOW)
        qt = qt.astype(LOW)
        do = low_t(dot_)
        pieces = masked_scores(q, kt_ref, segc_ref[span, :], segr_ref, start)
        spans = [slice(0, start), span] if start else [span]
        lse = lse_ref[0, span, :]
        weights = [jnp.exp(s - lse) for s in pieces]
        grads = [dot_nn(do, vt_ref[:, at]) for at in spans]
        delta = sum(jnp.sum(g * w, axis=1, keepdims=True) for g, w in zip(grads, weights))
        dq = None
        for at, w, g in zip(spans, weights, grads):
            ds = (w * (g - delta)).astype(LOW)
            term = dot_nn(ds, k_scr[at, :])
            dq = term if dq is None else dq + term
            dk_scr[:, at] += dot_nn(qt, ds)
            dv_scr[:, at] += dot_nn(dot_, w.astype(LOW))
        out_ref[0, :, span] = (dq * scale).T.astype(LOW)
    out_ref[1] = dk_scr[...].astype(LOW)
    out_ref[2] = dv_scr[...].astype(LOW)


def projection_back_kernel(heads, parts, place, half, *refs):
    x_refs, (a1_ref, *refs) = refs[:parts], refs[parts:]
    head_refs, refs = refs[:heads], refs[heads:]
    wt_ref, vec_ref, grads_ref, keep_ref, send_ref, qkeep_ref, qsend_ref, *scratch = refs
    g_scr, vec_scr, sums_scr, ext_scr, all_scr, x_scr, sems = scratch
    step = pl.program_id(0)
    cols = g_scr.shape[0] // 3
    extra = grads_ref.shape[0]
    count = qkeep_ref.shape[2] - 3 * cols

    def copy(j):
        return pltpu.make_async_copy(x_refs[j], x_scr.at[j], sems.at[j])

    @pl.when(step == 0)
    def _():
        for j in range(parts):
            copy(j).start()
        g_scr[...] = jnp.zeros_like(g_scr)
        vec_scr[...] = grads_ref[...]
        sums_scr[...] = jnp.zeros_like(sums_scr)

    for j in range(parts):

        @pl.when(step == j)
        def _():
            copy(j).wait()

    dqkv = jnp.concatenate([ref[k] for k in range(3) for ref in head_refs], axis=0)
    da1 = dot_nn(low_t(dqkv), wt_ref[...])

    @pl.when(step % 2 == 0)
    def _():
        keep_ref[0] = da1.astype(LOW)

    @pl.when(step % 2 == 1)
    def _():
        send_ref[0] = da1.astype(LOW)

    g_scr[...] += dot_nn(dqkv, a1_ref[...])
    unit, _ = normalize(x_scr[step].astype(HIGH))
    vec_scr[0:1, :] += jnp.sum(da1 * unit, axis=0, keepdims=True)
    vec_scr[1:2, :] += jnp.sum(da1, axis=0, keepdims=True)
    sums_scr[...] += jnp.sum(dqkv.astype(HIGH), axis=1, keepdims=True)

    @pl.when(step == pl.num_programs(0) - 1)
    def _():
        ext_scr[...] = vec_scr[...].T
        own = pl.ds(pl.multiple_of(place[0] * cols, 16), cols)
        ext_scr[own, 2:3] = sums_scr[:cols, :]
        ext_scr[own, 3:4] = sums_scr[2 * cols :, :]
        all_scr[:, : 3 * cols] = g_scr[...].T
        all_scr[:, 3 * cols : 3 * cols + extra] = ext_scr[...]
        rows = all_scr.shape[0] // parts
        for r in range(parts):
            for ref, side in ((qkeep_ref, half[0]), (qsend_ref, 1 - half[0])):
                start = pl.multiple_of(r * rows + side * (rows // 2), 16)
                ref[r] = all_scr[pl.ds(start, rows // 2), : 3 * cols + count].astype(LOW)


GELU_C = 0.7978845608028654
GELU_A = 0.044715


def mlp_kernel(
    parts, first_blocks, place, half, live_ref, x_ref, cot_ref, vec_ref, *refs
):
    o_refs, refs = refs[:parts], refs[parts:]
    own_ref, core_ref, *wide_refs = refs[:10]
    out_ref, *grad_refs = refs[10:15]
    dr1_ref, vecg_ref, *refs = refs[15:]
    do_refs, scratch = refs[:parts], refs[parts:]
    wide, ot_scr, r1_scr, a2_scr, a2t_scr, dy_scr, dyt_scr, y_scr, da2_scr, act_scr, sems = scratch
    step = pl.program_id(0)
    rows = o_refs[0].shape[0]
    slots, width = x_ref.shape
    bo, gain, shift, bp = (vec_ref[r : r + 1, :] for r in (4, 5, 6, 11))
    split = wide_refs[0].shape[1]
    live = lax.broadcasted_iota(jnp.int32, (slots, 1), 0) < live_ref[0]

    def copies(k):
        half_rows = rows // 2
        near, far = half[0] * half_rows, (1 - half[0]) * half_rows
        span = slice(0, split) if k == 0 else slice(split, wide.shape[1])
        sources = [(own_ref.at[:, span], 0, 0), (core_ref.at[:, span], 1, 0)]
        spots = [(2, near), (2, far), (3, near), (3, far)]
        sources += [(wide_refs[4 * k + n], *spot) for n, spot in enumerate(spots)]
        for n, (source, j, offset) in enumerate(sources):
            start = pl.multiple_of((place[0] ^ j) * rows + offset, 16)
            target = wide.at[pl.ds(start, source.shape[0]), span]
            yield pltpu.make_async_copy(source, target, sems.at[k, n])

    def block(n):
        return wide[:, pl.ds(pl.multiple_of(n * width, 128), width)]

    def permuted(scratch, value):
        for j in range(parts):
            scratch[j * rows : (j + 1) * rows, :] = value(pl.multiple_of((place[0] ^ j) * rows, 16))

    def put(value):
        value = value.astype(LOW)
        for k in range(2):

            @pl.when((step >= first_blocks) == bool(k))
            def _():
                keep, send = grad_refs[2 * k : 2 * k + 2]
                for j in range(parts):
                    (send if j % 2 else keep)[j // 2] = value[j * rows : (j + 1) * rows, :]

    @pl.when(step == 0)
    def _():
        for k in range(2):
            for copy in copies(k):
                copy.start()
        for j in range(parts):
            start = pl.multiple_of((place[0] ^ j) * rows, 16)
            ot_scr[pl.ds(start, rows), :] = o_refs[j][...]
        mixed = low_t(ot_scr[...])
        dy = jnp.where(live, cot_ref[...].astype(HIGH), 0.0)
        dy_scr[...] = dy.astype(LOW)
        ot_scr[...] = dy.T.astype(LOW)
        permuted(dyt_scr, lambda start: ot_scr[pl.ds(start, rows), :])
        for copy in copies(0):
            copy.wait()
        r1 = x_ref[...].astype(HIGH) + dot_nn(mixed, wide[:, :width]) + bo
        r1_scr[...] = r1
        unit, _ = normalize(r1)
        a2 = unit * gain + shift
        a2_scr[...] = a2.astype(LOW)
        ot_scr[...] = a2.T.astype(LOW)
        permuted(a2t_scr, lambda start: ot_scr[pl.ds(start, rows), :])
        vecg_ref[...] = jnp.zeros_like(vecg_ref)
        vecg_ref[11:12, :] = jnp.sum(dy, axis=0, keepdims=True)
        y_scr[...] = r1 + bp
        da2_scr[...] = jnp.zeros_like(da2_scr)

    @pl.when(step == split // width - 1)
    def _():
        for copy in copies(1):
            copy.wait()

    last = pl.num_programs(0) - 1

    @pl.when((step < last) & (step % 2 == 0))
    def _():
        w_fc, w_pt = block(1 + step), block(2 + step)
        u = dot_nn(a2_scr[...], w_fc) + vec_ref[pl.ds(7 + step // 2, 1), :]
        square = u * u
        t = jnp.tanh(GELU_C * (u + GELU_A * (square * u)))
        grown = 0.5 * (1.0 + t)
        act = (u * grown).astype(LOW)
        act_scr[...] = act
        y_scr[...] += dot_nt(act, w_pt)
        slope = grown + 0.5 * u * (1.0 - t * t) * (GELU_C + (3.0 * GELU_C * GELU_A) * square)
        du = (dot_nn(dy_scr[...], w_pt) * slope).astype(LOW)
        vecg_ref[pl.ds(7 + step // 2, 1), :] = jnp.sum(du.astype(HIGH), axis=0, keepdims=True)
        da2_scr[...] += dot_nt(du, w_fc)
        put(dot_nn(a2t_scr[...], du))

    @pl.when((step < last) & (step % 2 == 1))
    def _():
        put(dot_nn(dyt_scr[...], act_scr[...]))

    @pl.when(step == last)
    def _():
        out_ref[...] = jnp.where(live, y_scr[...], 0.0).astype(LOW)
        unit, inverse = normalize(r1_scr[...])
        da2 = da2_scr[...]
        vecg_ref[5:6, :] = jnp.sum(da2 * unit, axis=0, keepdims=True)
        vecg_ref[6:7, :] = jnp.sum(da2, axis=0, keepdims=True)
        dr1 = dy_scr[...].astype(HIGH) + normalize_back(unit, inverse, da2 * gain)
        dr1_ref[...] = dr1
        low = dr1.astype(LOW)
        vecg_ref[4:5, :] = jnp.sum(low.astype(HIGH), axis=0, keepdims=True)
        put(dot_nn(jnp.concatenate([ref[...] for ref in o_refs], axis=0), low))
        for j in range(parts):
            start = pl.multiple_of((place[0] ^ j) * rows, 16)
            do_refs[j][...] = dot_nt(wide[pl.ds(start, rows), :width], low).astype(LOW)


def group_layout(length_row, count_row, slots):
    starts = jnp.cumsum(count_row) - count_row
    within = jnp.arange(slots, dtype=jnp.int32)
    position = (starts[:, None] + within[None, :]).reshape(-1)
    live_rows = (within[None, :] < count_row[:, None]).reshape(-1)
    boundary = jnp.cumsum(length_row)
    segment = jnp.sum((position[:, None] >= boundary[None, :]).astype(jnp.int32), axis=1)
    buffer_slot = jnp.arange(position.shape[0], dtype=jnp.int32)
    return jnp.where(live_rows, segment, -1 - buffer_slot)


def adam_update(master, first, second, gradient, factor, rate, decay):
    clipped = gradient * factor
    first_new = BETA_FIRST * first + (1.0 - BETA_FIRST) * clipped
    second_new = BETA_SECOND * second + (1.0 - BETA_SECOND) * clipped * clipped
    first_hat = first_new / (1.0 - BETA_FIRST**STEP)
    second_hat = second_new / (1.0 - BETA_SECOND**STEP)
    master_new = master - rate * (
        first_hat / (jnp.sqrt(second_hat) + ADAM_EPSILON) + decay * master
    )
    return (clipped, master_new, first_new, second_new)


def adam_kernel(fc_rows, factor_ref, _, *refs):
    grads, states, outs = refs[:3], refs[3:9], refs[9:]
    near = pl.program_id(0) < pl.num_programs(0) // 2
    factor = factor_ref[0]
    width = outs[0].shape[-1] // fc_rows
    qkv = jnp.where(near, grads[1][0], grads[2][0])[:, : 3 * width]

    def update(gradient, at, base):
        results = adam_update(
            *[states[base + n][at] for n in range(3)],
            gradient.astype(HIGH), factor, RATE_MATRIX, DECAY_MATRIX,
        )
        for n, result in enumerate(results):
            outs[base // 3 * 4 + n][at] = result

    blocks = [grads[0][0, :, n : n + width] for n in range(0, grads[0].shape[2], width)]
    for f in range(fc_rows):
        span = slice(f * width, (f + 1) * width)
        for n in range(2):
            update(blocks[2 * f + n], (n, 0, slice(None), span), 3)
    update(qkv, (0, slice(None), slice(0, 3 * width)), 0)
    update(blocks[-1], (0, slice(None), slice(3 * width, 4 * width)), 0)


def swap(array, axis, bit, count):
    return lax.ppermute(array, axis, [(i, i ^ bit) for i in range(count)])


def pick(array, index):
    return lax.dynamic_index_in_dim(array, index, 0, keepdims=False)


def deal(pieces, parts):
    return list(pieces[:1]) + [swap(pieces[j], "shard", j, parts) for j in range(1, parts)]


def in_order(relative, place, parts):
    relative = jnp.stack(relative)
    return jnp.stack([pick(relative, place ^ r) for r in range(parts)])


def collect(own, parts):
    have = [own]
    bit = parts // 2
    slots = [0]
    while bit:
        have = have + [swap(piece, "shard", bit, parts) for piece in have]
        slots = slots + [s ^ bit for s in slots]
        bit //= 2
    return [have[slots.index(j)] for j in range(parts)]


def after(value, *others):
    return lax.optimization_barrier((value, *others))[0]


def add_low(a, b):
    return (a.astype(HIGH) + b.astype(HIGH)).astype(LOW)


def bits_of(count):
    return [1 << n for n in range(count.bit_length() - 1)]


def halve(array, upper, dim):
    length = array.shape[dim] // 2
    keep = lax.dynamic_slice_in_dim(array, upper * length, length, dim)
    return keep, lax.dynamic_slice_in_dim(array, (1 - upper) * length, length, dim)


def scatter_half(array, dim, bit, replica, replicas):
    keep, send = halve(array, (replica // bit) % 2, dim)
    return keep, swap(send, "dp", bit, replicas)


def params(mebibytes):
    return pltpu.CompilerParams(
        dimension_semantics=("arbitrary",), vmem_limit_bytes=mebibytes * 1024 * 1024
    )


def cost(flops, moved, special=0):
    return pl.CostEstimate(flops=int(flops), bytes_accessed=int(moved), transcendentals=int(special))


def whole(*shape):
    zeros = (0,) * len(shape)
    return pl.BlockSpec(shape, lambda *_: zeros)


def make_on_device(parts, replicas):
    def on_device(
        tokens, cotangent, lengths, counts,
        attn_w, attn_m, attn_v, mlp_w, mlp_m, mlp_v, vec_w, vec_m, vec_v,
    ):
        slots, width = tokens.shape
        rows = attn_w.shape[0]
        hidden = mlp_w.shape[2]
        fc_rows = hidden // width
        total = parts * slots
        head_size = width // HEADS
        own_heads = HEADS // parts
        own_cols = own_heads * head_size
        scale = head_size ** (-0.5)
        place = lax.axis_index("shard")
        replica = lax.axis_index("dp")
        prefetch = place.reshape(1).astype(jnp.int32)

        half = replica % 2
        side = half.reshape(1).astype(jnp.int32)

        x_all = collect(tokens, parts)
        w_pieces = pl.pallas_call(
            cut_kernel,
            grid_spec=pltpu.PrefetchScalarGridSpec(
                num_scalar_prefetch=1,
                grid=(1,),
                in_specs=[whole(rows, 3 * width), whole(vec_w.shape[0], rows)],
                out_specs=[whole(rows + 16, 3 * own_cols)] * parts,
            ),
            out_shape=[jax.ShapeDtypeStruct((rows + 16, 3 * own_cols), LOW)] * parts,
            compiler_params=params(12),
            cost_estimate=cost(0, 4e6),
            name="cut",
        )(prefetch, attn_w, vec_w)
        w_local = deal(w_pieces, parts)

        blocks = 2 * fc_rows + 1
        split = (fc_rows // 2 * 2 + 1) * width
        wide_own, *wide_half = pl.pallas_call(
            widen_kernel,
            grid_spec=pltpu.PrefetchScalarGridSpec(
                num_scalar_prefetch=1,
                grid=(1,),
                in_specs=[
                    pl.BlockSpec((rows, width), lambda *_: (0, 3)),
                    whole(2, rows, hidden),
                ],
                out_specs=[
                    whole(rows, blocks * width),
                    whole(rows // 2, split),
                    whole(rows // 2, blocks * width - split),
                ],
            ),
            out_shape=[
                jax.ShapeDtypeStruct((rows, blocks * width), LOW),
                jax.ShapeDtypeStruct((rows // 2, split), LOW),
                jax.ShapeDtypeStruct((rows // 2, blocks * width - split), LOW),
            ],
            compiler_params=params(28),
            cost_estimate=cost(0, 12e6),
            name="widen",
        )(side, attn_w, mlp_w)
        wide_own, *wide_half = lax.optimization_barrier((wide_own, *wide_half, *w_local, *x_all))[:3]
        near = [swap(mine, "shard", parts // 2, parts) for mine in wide_half]
        wide_core = swap(wide_own, "shard", 1, parts)

        segment = group_layout(lengths[0], counts[0], slots)
        seg_col = segment[:, None]
        seg_row = segment[None, :]
        own_vec = vec_w.astype(LOW).astype(HIGH)
        bias_local = jnp.concatenate(
            [own_vec[2], jnp.zeros((own_cols,), HIGH), own_vec[3]]
        )[:, None]

        a1, qkv, w_t, vectors = pl.pallas_call(
            functools.partial(project_kernel, parts),
            grid_spec=pltpu.PrefetchScalarGridSpec(
                num_scalar_prefetch=1,
                grid=(parts,),
                in_specs=[
                    *[pl.BlockSpec(memory_space=pl.ANY)] * parts,
                    *[whole(rows + 16, 3 * own_cols)] * parts,
                    whole(3 * own_cols, 1),
                ],
                out_specs=[
                    pl.BlockSpec((slots, width), lambda i, p: (p[0] ^ i, 0)),
                    pl.BlockSpec((3 * own_cols, slots), lambda i, p: (0, p[0] ^ i)),
                    whole(3 * own_cols, width),
                    whole(16, width),
                ],
                scratch_shapes=[
                    pltpu.VMEM((width, 3 * own_cols), HIGH),
                    pltpu.VMEM((parts, slots, width), LOW),
                    pltpu.SemaphoreType.DMA((parts,)),
                ],
            ),
            out_shape=[
                jax.ShapeDtypeStruct((total, width), LOW),
                jax.ShapeDtypeStruct((3 * own_cols, total), LOW),
                jax.ShapeDtypeStruct((3 * own_cols, width), LOW),
                jax.ShapeDtypeStruct((16, width), HIGH),
            ],
            compiler_params=params(24),
            cost_estimate=cost(2 * total * width * 3 * own_cols * 3, 12e6),
            name="project",
        )(prefetch, *x_all, *w_local, bias_local)

        pair_flops = 2 * total * total * head_size * 4 // 2

        def head_specs(h):
            return [
                pl.BlockSpec((head_size, total), functools.partial(lambda k, *_: (k * own_heads + h, 0), k))
                for k in range(3)
            ]

        def attend(h, qkv):
            return pl.pallas_call(
                functools.partial(attend_kernel, scale),
                grid_spec=pltpu.PrefetchScalarGridSpec(
                    num_scalar_prefetch=1,
                    grid=(1,),
                    in_specs=head_specs(h) + [whole(total, 1), whole(1, total)],
                    out_specs=[whole(parts, head_size, slots), whole(1, total, 1)],
                    scratch_shapes=[pltpu.VMEM((total, head_size), LOW)],
                ),
                out_shape=[
                    jax.ShapeDtypeStruct((parts, head_size, slots), LOW),
                    jax.ShapeDtypeStruct((1, total, 1), HIGH),
                ],
                compiler_params=params(24),
                cost_estimate=cost(2 * pair_flops, 4e6, total * total // 2),
                name="attend",
            )(prefetch, qkv, qkv, qkv, seg_col, seg_row)

        mixed, lse = [], []
        for h in range(own_heads):
            if h == 1:
                qkv, near[0] = lax.optimization_barrier((qkv, near[0]))
                far = [swap(near[0], "dp", 1, replicas)]
                turned = [swap(near[0], "shard", 1, parts)]
            head_mixed, head_lse = attend(h, qkv)
            mixed.append(head_mixed)
            lse.append(head_lse)
        near[1] = after(near[1], mixed[-1])
        far.append(swap(near[1], "dp", 1, replicas))
        mixed_own = deal(
            [jnp.concatenate([head[j] for head in mixed], axis=0) for j in range(parts)], parts
        )
        turned.append(swap(near[1], "shard", 1, parts))
        wide = [wide_own, wide_core]
        for k in range(2):
            wide += [near[k], far[k], turned[k], swap(far[k], "shard", 1, parts)]

        steps = blocks
        live_own = lax.dynamic_index_in_dim(counts[0], place, 0, keepdims=True)
        first_blocks = fc_rows // 2 * 2 + 1

        def grad_spec(k):
            first, last = ((0, first_blocks - 1), (first_blocks, steps - 1))[k]
            return pl.BlockSpec(
                (parts // 2, rows, width), lambda i, *_: (0, 0, jnp.clip(i, first, last) - first)
            )

        grad_columns = [first_blocks * width, (steps - first_blocks) * width]

        in_hbm = pl.BlockSpec(memory_space=pltpu.HBM)
        out = pl.pallas_call(
            functools.partial(mlp_kernel, parts, first_blocks),
            grid_spec=pltpu.PrefetchScalarGridSpec(
                num_scalar_prefetch=3,
                grid=(steps,),
                in_specs=[whole(slots, width), whole(slots, width), whole(16, width)]
                + [whole(own_cols, slots)] * parts
                + [in_hbm] * len(wide),
                out_specs=[whole(slots, width)]
                + [grad_spec(k) for k in range(2) for _ in range(2)]
                + [whole(slots, width), whole(16, width)]
                + [whole(own_cols, slots)] * parts,
                scratch_shapes=[
                    pltpu.VMEM((width, blocks * width), LOW),
                    pltpu.VMEM((width, slots), LOW),
                    pltpu.VMEM((slots, width), HIGH),
                    pltpu.VMEM((slots, width), LOW),
                    pltpu.VMEM((width, slots), LOW),
                    pltpu.VMEM((slots, width), LOW),
                    pltpu.VMEM((width, slots), LOW),
                    pltpu.VMEM((slots, width), HIGH),
                    pltpu.VMEM((slots, width), HIGH),
                    pltpu.VMEM((slots, width), LOW),
                    pltpu.SemaphoreType.DMA((2, 6)),
                ],
            ),
            out_shape=[jax.ShapeDtypeStruct((slots, width), LOW)]
            + [jax.ShapeDtypeStruct((parts // 2, rows, c), LOW) for c in grad_columns for _ in range(2)]
            + [jax.ShapeDtypeStruct((slots, width), HIGH), jax.ShapeDtypeStruct((16, width), HIGH)]
            + [jax.ShapeDtypeStruct((own_cols, slots), LOW)] * parts,
            compiler_params=params(50),
            cost_estimate=cost(2 * slots * width * (6 * hidden + 3 * width), 30e6, slots * hidden),
            name="mlp",
        )(prefetch, side, live_own, tokens, cotangent, vectors, *mixed_own, *wide)
        block_out, keep_a, send_a, keep_b, send_b, grad_resid, mid_grads, *do_pieces = out

        do_own = deal(do_pieces, parts)
        got_a = swap(send_a, "shard", 1, parts)
        got_b = swap(send_b, "shard", 1, parts)
        own_a, other_a = [add_low(keep_a[n], got_a[n]) for n in range(2)]
        got_a = swap(other_a, "shard", parts // 2, parts)
        got_b = after(got_b, own_a, other_a)
        own_b, other_b = halve(add_low(keep_b, got_b), half, 1)
        *do_own, own_b, other_b = lax.optimization_barrier((*do_own, own_b, other_b))
        got_b = swap(other_b, "dp", 1, replicas)

        def attend_back(h, qkv):
            return pl.pallas_call(
                functools.partial(attend_back_kernel, scale),
                grid_spec=pltpu.PrefetchScalarGridSpec(
                    num_scalar_prefetch=1,
                    grid=(1,),
                    in_specs=head_specs(h)
                    + [whole(total, 1), whole(1, total), whole(1, total, 1)]
                    + [pl.BlockSpec((head_size, slots), lambda *_: (h, 0))] * parts,
                    out_specs=whole(3, head_size, total),
                    scratch_shapes=[
                        pltpu.VMEM((total, head_size), LOW),
                        pltpu.VMEM((parts, head_size, slots), LOW),
                        pltpu.VMEM((head_size, total), HIGH),
                        pltpu.VMEM((head_size, total), HIGH),
                    ],
                ),
                out_shape=jax.ShapeDtypeStruct((3, head_size, total), LOW),
                compiler_params=params(28),
                cost_estimate=cost(
                    5 * pair_flops, 4e6, total * total // 2
                ),
                name="attend_back",
            )(prefetch, qkv, qkv, qkv, seg_col, seg_row, lse[h], *do_own)

        dqkv = [attend_back(h, qkv) for h in range(own_heads)]
        *dqkv, got_a, got_b = lax.optimization_barrier((*dqkv, got_a, got_b))
        own_a, other_a = halve(add_low(own_a, got_a), half, 0)
        got_a = swap(other_a, "dp", 1, replicas)
        own_b, other_b = [add_low(own_b[n], got_b[n]) for n in range(2)]
        got_b = swap(other_b, "shard", parts // 2, parts)
        dqkv[0] = after(dqkv[0], other_a, own_b, other_b)

        q_cols = 3 * own_cols
        extra = vec_w.shape[0]
        half_rows = rows // 2
        da1_keep, da1_send, own_q, other_q = pl.pallas_call(
            functools.partial(projection_back_kernel, own_heads, parts),
            grid_spec=pltpu.PrefetchScalarGridSpec(
                num_scalar_prefetch=2,
                grid=(parts,),
                in_specs=[
                    *[pl.BlockSpec(memory_space=pl.ANY)] * parts,
                    pl.BlockSpec((slots, width), lambda i, p, _: (p[0] ^ i, 0)),
                ]
                + [pl.BlockSpec((3, head_size, slots), lambda i, p, _: (0, 0, p[0] ^ i))] * own_heads
                + [whole(q_cols, width), whole(16, width), whole(16, width)],
                out_specs=[pl.BlockSpec((1, slots, width), lambda i, *_: (i // 2, 0, 0))] * 2
                + [whole(parts, half_rows, q_cols + extra)] * 2,
                scratch_shapes=[
                    pltpu.VMEM((q_cols, width), HIGH),
                    pltpu.VMEM((16, width), HIGH),
                    pltpu.VMEM((q_cols, 1), HIGH),
                    pltpu.VMEM((width, 16), HIGH),
                    pltpu.VMEM((width, q_cols + 64), HIGH),
                    pltpu.VMEM((parts, slots, width), LOW),
                    pltpu.SemaphoreType.DMA((parts,)),
                ],
            ),
            out_shape=[jax.ShapeDtypeStruct((parts // 2, slots, width), LOW)] * 2
            + [jax.ShapeDtypeStruct((parts, half_rows, q_cols + extra), LOW)] * 2,
            compiler_params=params(28),
            cost_estimate=cost(4 * total * width * 3 * own_cols * 2, 16e6),
            name="projection_back",
        )(prefetch, side, *x_all, a1, *dqkv, w_t, vectors, mid_grads)

        share = rows // replicas
        z_bits = [bit for bit in (1 << n for n in range(1, 20)) if bit < replicas]
        last_event = [own_q]

        def seen(value):
            return lax.optimization_barrier((value, last_event[0]))[0]

        def event(value):
            last_event[0] = value
            return value

        def next_half(keep, got, bit, dim):
            array = event(add_low(keep, seen(got)))
            return scatter_half(array, dim, bit, replica, replicas)

        got_q = swap(other_q, "dp", 1, replicas)
        da1_got = swap(da1_send, "shard", 1, parts)
        state_a = next_half(own_a, got_a, z_bits[0], 0)
        state_b = next_half(own_b, got_b, z_bits[0], 0)
        da1_got = seen(da1_got)
        own_da1 = da1_keep[0].astype(HIGH) + da1_got[0].astype(HIGH)
        other_da1 = event(add_low(da1_keep[1], da1_got[1]))
        got_da1 = swap(other_da1, "shard", 2, parts)
        for bit in z_bits[1:]:
            state_a = next_half(*state_a, bit, 0)
        state_q = next_half(own_q, got_q, z_bits[0], 1)
        for bit in z_bits[1:]:
            state_b = next_half(*state_b, bit, 0)
        da1 = own_da1 + seen(got_da1).astype(HIGH)
        unit, inverse = normalize(seen(tokens).astype(HIGH))
        grad_input = grad_resid + normalize_back(unit, inverse, da1 * vectors[0:1])
        live_rows = jnp.arange(slots, dtype=jnp.int32) < live_own[0]
        grad_in = event(jnp.where(live_rows[:, None], grad_input, 0.0).astype(LOW))
        part_a = event(add_low(state_a[0], seen(state_a[1])))
        for bit in z_bits[1:]:
            state_q = next_half(*state_q, bit, 1)
        part_b = event(add_low(state_b[0], seen(state_b[1])))
        part_ab = event(jnp.concatenate([part_a, part_b], axis=1))
        all_ab = lax.all_gather(part_ab, "dp", axis=0)
        part_q = event(add_low(state_q[0], seen(state_q[1])))

        def as_pair(value):
            high = lax.reduce_precision(value, 8, 7)
            return jnp.stack([high, value - high]).astype(LOW)

        main = part_q[:, :, :q_cols]
        squares = sum(jnp.sum(jnp.square(p.astype(HIGH))) for p in (part_ab, main))
        vec_parts = part_q[:, :, q_cols:].transpose(1, 0, 2).reshape(1, share, parts * extra)
        shared = jnp.concatenate(
            [vec_parts, jnp.broadcast_to(as_pair(squares), (1, share, 2))], axis=2
        )
        pieces = jnp.concatenate([main, jnp.broadcast_to(shared, (parts,) + shared.shape[1:])], axis=2)
        dealt = in_order(deal([pick(pieces, place ^ j) for j in range(parts)], parts), place, parts)
        q_rows = (
            dealt[:, :, :q_cols]
            .reshape(parts, share, 3, own_cols)
            .transpose(1, 2, 0, 3)
            .reshape(share, 3 * width)
        )
        summed = jnp.sum(dealt[:, :, q_cols:].astype(HIGH), axis=0)
        vec_parts = summed[:, : parts * extra].reshape(share, parts, extra).astype(LOW)
        squares = jnp.sum(summed[0, parts * extra :]) + jnp.sum(jnp.square(vec_parts.astype(HIGH)))
        vec_own = lax.dynamic_index_in_dim(vec_parts, place, 1, keepdims=False)
        near_q = jnp.concatenate(
            [q_rows, vec_own, jnp.broadcast_to(as_pair(squares), (share, 2))], axis=1
        )[None]
        for bit in z_bits[::-1]:
            near_q = jnp.concatenate([near_q, swap(near_q, "dp", bit, replicas)], axis=0)
        far_q = swap(near_q, "dp", 1, replicas)

        def block_of(index):
            block = index % 2
            for bit in z_bits:
                block = block * 2 + index // bit % 2
            return block

        def index_of(block):
            index = 0
            for bit in z_bits[::-1]:
                index = index + block % 2 * bit
                block = block // 2
            return index + block

        turn = block_of(replica)
        small = jnp.concatenate([near_q[:, :, 3 * width :], far_q[:, :, 3 * width :]], axis=0)
        small = jnp.stack([pick(small, turn ^ r) for r in range(replicas)]).astype(HIGH)
        summed_vec = small[:, :, :extra].reshape(rows, extra).T
        squares = jnp.sum(small[:, 0, extra:])

        norm_total = jnp.sqrt(squares)
        factor = jnp.minimum(1.0, CLIP_LIMIT / (norm_total + 1e-06))
        near_count = replicas // 2
        q_block = (1,) + near_q.shape[1:]

        def gathered_spec(array):
            return pl.BlockSpec((1,) + array.shape[1:], lambda i, _, p: (index_of(i ^ p[0]), 0, 0))

        attn_shape = (replicas, share, 4 * width)
        mlp_shape = (2, replicas, share, hidden)
        attn_spec = pl.BlockSpec((1, share, 4 * width), lambda i, _, p: (i ^ p[0], 0, 0))
        mlp_spec = pl.BlockSpec((2, 1, share, hidden), lambda i, _, p: (0, i ^ p[0], 0, 0))
        updated = pl.pallas_call(
            functools.partial(adam_kernel, fc_rows),
            grid_spec=pltpu.PrefetchScalarGridSpec(
                num_scalar_prefetch=2,
                grid=(replicas,),
                in_specs=[gathered_spec(all_ab)]
                + [
                    pl.BlockSpec(q_block, lambda i, *_: (jnp.minimum(i, near_count - 1), 0, 0)),
                    pl.BlockSpec(q_block, lambda i, *_: (jnp.maximum(i - near_count, 0), 0, 0)),
                ]
                + [attn_spec] * 3
                + [mlp_spec] * 3,
                out_specs=[attn_spec] * 4 + [mlp_spec] * 4,
            ),
            out_shape=[jax.ShapeDtypeStruct(attn_shape, HIGH)] * 4
            + [jax.ShapeDtypeStruct(mlp_shape, HIGH)] * 4,
            compiler_params=params(50),
            cost_estimate=cost(30 * 9 * rows * width, 54e6),
            name="adam",
        )(
            factor.reshape(1),
            turn.reshape(1).astype(jnp.int32),
            all_ab,
            near_q,
            far_q,
            *[array.reshape(attn_shape) for array in (attn_w, attn_m, attn_v)],
            *[array.reshape(mlp_shape) for array in (mlp_w, mlp_m, mlp_v)],
        )
        attn_grad, attn_w_new, attn_m_new, attn_v_new = [u.reshape(attn_w.shape) for u in updated[:4]]
        mlp_grad, mlp_w_new, mlp_m_new, mlp_v_new = [u.reshape(mlp_w.shape) for u in updated[4:]]
        vec_grad, vec_w_new, vec_m_new, vec_v_new = adam_update(
            vec_w, vec_m, vec_v, summed_vec, factor, RATE_VECTOR, 0.0
        )
        return (
            block_out, grad_in, attn_grad, mlp_grad, vec_grad,
            attn_w_new, attn_m_new, attn_v_new, mlp_w_new, mlp_m_new, mlp_v_new,
            vec_w_new, vec_m_new, vec_v_new, norm_total.reshape(1),
        )

    return on_device


def solution(mesh):
    tokens = P(("dp", "shard"), None)
    groups = P("dp", None)
    attn = P("shard", None)
    mlp = P(None, "shard", None)
    vec = P(None, "shard")
    return jax.shard_map(
        make_on_device(mesh.shape["shard"], mesh.shape["dp"]),
        mesh=mesh,
        in_specs=(tokens, tokens, groups, groups) + (attn,) * 3 + (mlp,) * 3 + (vec,) * 3,
        out_specs=(tokens, tokens, attn, mlp, vec) + (attn,) * 3 + (mlp,) * 3 + (vec,) * 3 + (P(),),
        check_vma=False,
    )
```
